128 devices in a mesh: gx: 4 (over x), gy: 32 (over y, z, core).
Axes of the slice: x: 4, y: 4, z: 4, core: 2. Of those that a mesh axis runs over, the one named last changes fastest.
Arguments:
- bricks: bfloat16 [4, 32, 56, 64, 96], P('gx', 'gy'), may hold values from -6 to 6
- brick_owner: int32 [4, 32, 56], P('gx', 'gy'), may hold values from 0 to 31, as said below
- brick_slot: int32 [4, 32, 56], P('gx', 'gy'), may hold values from 0 to 63, as said below
- down_weight: bfloat16 [27, 96, 192], replicated, may hold values from -0.25 to 0.25
- up_weight: bfloat16 [27, 192, 96], replicated, may hold values from -0.25 to 0.25
- cotangent: bfloat16 [64, 512, 16, 96], P('gx', 'gy'), may hold values from -6 to 6
Outputs:
- result: bfloat16 [64, 512, 16, 96], P('gx', 'gy')
- brick_grads: bfloat16 [4, 32, 56, 64, 96], P('gx', 'gy')
- down_grad: float32 [27, 96, 192], replicated
- up_grad: float32 [27, 192, 96], replicated
The draws below stay inside these ranges and needn't reach their ends.
Inputs may be any that keep to these rules, and one draw needn't show every extreme that they name: `brick_owner`: at most 2 of one device's bricks name the same owner, and in every draw some device hands exactly 2 bricks to one owner. `brick_slot`: no two bricks of one tile row with the same owner share a slot.
All inputs are finite; a program needn't handle non-finite values.
Results may differ from the reference program's by a relative error of at most 0.0042.
Values may be sent and summed in bfloat16 or wider, within the bound.
A program may use at most 128 MiB of HBM per device.

```python
import jax
import jax.numpy as jnp
from jax import lax

C = 96
C2 = 192
BE = 4
TBD = 4
NB_DEV = 56
TB = 64
VOX = 64
NX = 64
NY = 512
NZ = 16
N_GX = 4
N_GY = 32


def brick_routes(key):
    capacity = TB // N_GY
    send_keys = jax.random.split(jax.random.fold_in(key, 11), N_GX * N_GY)
    send_rank = jax.vmap(lambda sub_key: jax.random.permutation(sub_key, TB))(send_keys).reshape(N_GX, N_GY, TB)
    favour = jax.random.randint(jax.random.fold_in(key, 12), (N_GX, N_GY), 0, N_GY)
    send_ids = jnp.arange(TB, dtype=jnp.int32)
    forced = (send_ids // capacity)[None, None, :] == favour[..., None]
    scores = jnp.where(forced, send_ids % capacity - capacity, send_rank)
    send_order = jnp.argsort(scores, axis=-1, stable=True)[..., :NB_DEV].astype(jnp.int32)
    owners = send_order // capacity
    rank_ids = send_order % capacity
    tile_keys = jax.random.split(jax.random.fold_in(key, 13), N_GX * N_GY)
    tile_perm = jax.vmap(lambda sub_key: jax.random.permutation(sub_key, TB))(tile_keys).reshape(N_GX, N_GY, TB)
    sources = jnp.arange(N_GY, dtype=jnp.int32)[None, :, None]
    row_ids = jnp.broadcast_to(jnp.arange(N_GX, dtype=jnp.int32)[:, None, None], owners.shape)
    incoming_ids = sources * capacity + rank_ids
    slot_ids = tile_perm[row_ids, owners, incoming_ids]
    return (owners.astype(jnp.int32), slot_ids.astype(jnp.int32))


def draw_brick_owner(key, part):
    routes = brick_routes(key)
    return routes[0]


def draw_brick_slot(key, part):
    routes = brick_routes(key)
    return routes[1]


def level_of(own_key, extent, pieces, least, top_value):
    def one(dim, shards_of):
        steps = jax.random.uniform(jax.random.fold_in(jax.random.fold_in(own_key, 6), dim), (shards_of,), jnp.float32, least / len(pieces), top_value / len(pieces))
        return jnp.repeat(jnp.exp(steps), extent[dim] // shards_of).reshape((-1,) + (1,) * (len(extent) - dim - 1))

    factor_of = one(*pieces[0])
    for cut in pieces[1:]:
        factor_of = factor_of * one(*cut)
    return factor_of


def gaussian(key, dims, spread, reach, cuts=(), kind=jnp.bfloat16):
    entries = jax.random.normal(key, dims, jnp.float32) * spread
    if len(cuts) > 0:
        entries = level_of(key, dims, cuts, -0.22, 0.18) * entries
    return jnp.clip(entries, min=-reach, max=reach).astype(kind)


def setup_inputs(seed: int = 0) -> dict:
    key_of = jax.random.split(jax.random.key(seed), 7)
    return {
        "bricks": gaussian(key_of[0], (N_GX, N_GY, NB_DEV, VOX, C), 1.0, 6.0, ((0, 4), (1, 32))),
        "brick_owner": draw_brick_owner(jax.random.fold_in(key_of[6], 71), 0),
        "brick_slot": draw_brick_slot(jax.random.fold_in(key_of[6], 71), 0),
        "down_weight": gaussian(key_of[3], (27, C, C2), (27 * C // 4) ** -0.5, 0.25),
        "up_weight": gaussian(key_of[4], (27, C2, C), (27 * C2 // 8) ** -0.5, 0.25),
        "cotangent": gaussian(key_of[5], (NX, NY, NZ, C), 1.0, 6.0, ((0, 4), (1, 32))),
    }


LAYOUT = ("NDHWC", "DHWIO", "NDHWC")


def down_conv(values, weights):
    kernel = weights.astype(jnp.float32).reshape(3, 3, 3, weights.shape[1], weights.shape[2])
    convolved = lax.conv_general_dilated(values.astype(jnp.float32)[None], kernel, (2, 2, 2), ((1, 0), (1, 0), (1, 0)), dimension_numbers=LAYOUT, precision=lax.Precision.HIGHEST)
    return convolved[0]


def up_conv(values, weights):
    kernel = weights.astype(jnp.float32).reshape(3, 3, 3, weights.shape[1], weights.shape[2])[::-1, ::-1, ::-1]
    convolved = lax.conv_general_dilated(values.astype(jnp.float32)[None], kernel, (1, 1, 1), ((1, 2), (1, 2), (1, 2)), lhs_dilation=(2, 2, 2), dimension_numbers=LAYOUT, precision=lax.Precision.HIGHEST)
    return convolved[0]


def table_grads(values, coarse_vals):
    padded = jnp.pad(values, ((1, 0), (1, 0), (1, 0), (0, 0)))
    half_x, half_y, half_z = coarse_vals.shape[0], coarse_vals.shape[1], coarse_vals.shape[2]
    flat_rows = coarse_vals.reshape(-1, coarse_vals.shape[3])
    summands = []
    for offset_id in range(27):
        shift_x, shift_y, shift_z = offset_id // 9, (offset_id // 3) % 3, offset_id % 3
        window = lax.slice(padded, (shift_x, shift_y, shift_z, 0), (shift_x + 2 * half_x - 1, shift_y + 2 * half_y - 1, shift_z + 2 * half_z - 1, padded.shape[3]), (2, 2, 2, 1))
        summands.append(jnp.dot(window.reshape(-1, padded.shape[3]).T, flat_rows, preferred_element_type=jnp.float32))
    return jnp.stack(summands)


def expand_mask(occupied, edge):
    grown = jnp.repeat(jnp.repeat(jnp.repeat(occupied, edge, 0), edge, 1), edge, 2)
    return grown[..., None]


def reference(bricks, brick_owner, brick_slot, down_weight, up_weight, cotangent):
    tile_rows = jnp.arange(N_GX, dtype=jnp.int32)[:, None, None]
    brick_x = tile_rows * TBD + brick_slot // (TBD * TBD)
    brick_y = brick_owner * TBD + (brick_slot // TBD) % TBD
    brick_z = brick_slot % TBD
    grid_shape = (N_GX * TBD, N_GY * TBD, TBD)
    placed = jnp.zeros(grid_shape + (VOX, C), jnp.bfloat16).at[brick_x, brick_y, brick_z].set(bricks)
    occupied = jnp.zeros(grid_shape, jnp.float32).at[brick_x, brick_y, brick_z].set(1.0)
    fine_grid = placed.reshape(grid_shape + (BE, BE, BE, C)).transpose(0, 3, 1, 4, 2, 5, 6).reshape(NX, NY, NZ, C)
    fine_mask = expand_mask(occupied, BE)
    coarse_mask = expand_mask(occupied, BE // 2)
    before = down_conv(fine_grid, down_weight)
    gate_sig = jax.nn.sigmoid(before)
    coarse = (before * gate_sig * coarse_mask).astype(jnp.bfloat16)
    lifted = up_conv(coarse, up_weight)
    result = ((fine_grid.astype(jnp.float32) + lifted) * fine_mask).astype(jnp.bfloat16)
    grad_seed = cotangent * fine_mask.astype(jnp.bfloat16)
    up_grad = jnp.swapaxes(table_grads(grad_seed, coarse), 1, 2)
    back_grad = down_conv(grad_seed, jnp.swapaxes(up_weight, 1, 2))
    slope_term = gate_sig * (1.0 + before * (1.0 - gate_sig))
    coarse_grad = (back_grad * slope_term * coarse_mask).astype(jnp.bfloat16)
    down_grad = table_grads(fine_grid, coarse_grad)
    lowered = up_conv(coarse_grad, jnp.swapaxes(down_weight, 1, 2))
    fine_grad = (grad_seed.astype(jnp.float32) + lowered).astype(jnp.bfloat16)
    bricked = fine_grad.reshape(N_GX * TBD, BE, N_GY * TBD, BE, TBD, BE, C).transpose(0, 2, 4, 1, 3, 5, 6).reshape(grid_shape + (VOX, C))
    brick_grads = bricked[brick_x, brick_y, brick_z]
    return result, brick_grads, down_grad, up_grad
```

```python
import functools

import jax
import jax.numpy as jnp
from jax import lax
from jax.experimental import pallas as pl
from jax.experimental.pallas import tpu as pltpu
from jax.sharding import PartitionSpec as P

C = 96
C2 = 192
L = 128
TB = 64
VOX = 64
ENTRIES = 56
NY_DEV = 32
NX_DEV = 4
NL = 28 * L
PART = 7 * L

BF = jnp.bfloat16
F32 = jnp.float32
I32 = jnp.int32
MESH = pl.DeviceIdType.MESH
ORDERS = (("x", "y", "z"), ("y", "z", "x"), ("z", "x", "y"))
NT = (((1,), (1,)), ((), ()))


def dot(a, b):
    return jnp.dot(a, b, preferred_element_type=F32)


def dot_nt(a, b):
    return lax.dot_general(a, b, NT, preferred_element_type=F32)


def routes_kernel(me_ref, owner_ref, slot_ref, entry_ref, place_ref, target_ref):
    def clear(i, carry):
        entry_ref[i] = 0
        place_ref[i] = -1
        return carry

    lax.fori_loop(0, TB, clear, 0)

    def step(j, carry):
        first = 2 * lax.rem(owner_ref[j] - me_ref[0] + NY_DEV, NY_DEV)
        t = jnp.where(place_ref[first] < 0, first, first + 1)
        entry_ref[t] = j
        place_ref[t] = slot_ref[j]
        target_ref[j] = t
        return carry

    lax.fori_loop(0, ENTRIES, step, 0)


def routes(me, owner, slot):
    smem = pl.BlockSpec(memory_space=pltpu.SMEM)
    return pl.pallas_call(
        routes_kernel,
        out_shape=(
            jax.ShapeDtypeStruct((TB,), I32),
            jax.ShapeDtypeStruct((TB,), I32),
            jax.ShapeDtypeStruct((ENTRIES,), I32),
        ),
        in_specs=[smem] * 3,
        out_specs=[smem] * 3,
    )(me, owner, slot)


def iotas(rows, cols):
    return (
        lax.broadcasted_iota(I32, (rows, cols), 0),
        lax.broadcasted_iota(I32, (rows, cols), 1),
    )


def one_hot(hit):
    return jnp.where(hit, 1.0, 0.0).astype(BF)


def col(block, width=L, count=1):
    return pl.ds(block * width, count * width)


SCRATCH = dict(
    bricks_v=((ENTRIES, VOX, C), BF),
    cot_v=((256, 16, C), BF),
    wd_v=((27, C, C2), BF),
    wu_v=((27, C2, C), BF),
    out_b=((NY_DEV, 2 * VOX, L), BF),
    recv_b=((NY_DEV, 2 * VOX, L), BF),
    scr=((TB * VOX, L), F32),
    scr2=((TB * VOX, L), F32),
    packed=((TB, VOX * L), BF),
    eg=((2, TB, VOX * L), BF),
    ex=((2, TB, 16 * L), BF),
    ey=((2, TB, 20 * L), BF),
    ez=((2, TB, 25 * L), BF),
    hx=((2, 16, 16 * L), BF),
    hy=((2, 16, 16 * L), BF),
    hc=((2, 16, 4 * L), BF),
    hy_send=((2, 16, 16 * L), BF),
    pm=((2, 8 * TB, NL), BF),
    wdp=((NL, C2), BF),
    wup=((C2, NL), BF),
    before=((8 * TB, C2), F32),
    back=((8 * TB, C2), F32),
    cc=((2, 8, TB, C2), BF),
    ce=((2, 27, TB, C2), BF),
    chx=((2, 4, 16, C2), BF),
    chy=((2, 4, 16, C2), BF),
    chc=((2, 2, 16, C2), BF),
    chy_send=((2, 4, 16, C2), BF),
    part=((2, C2, NL), F32),
    sb=((C2, NL), BF),
    r0=((C2, NL), BF),
    ab=((C2, NL), BF),
    ar=((3, 3, 16, NL), BF),
    bb=((3, 16, NL), BF),
    br=((3, 3, 16, PART), BF),
    cr=((3, 4, 16, PART), BF),
    total=((2, C2, NL), BF),
    fb=((TB, VOX * L), BF),
    rep=((NY_DEV, 2 * VOX, L), BF),
    ret=((NY_DEV, 2 * VOX, L), BF),
    res_v=((256, 16, C), BF),
)
SEMS = dict(
    load=(4,),
    store=(3,),
    a2a_send=(1,),
    a2a_recv=(1,),
    halo_send=(6,),
    halo_recv=(6,),
    back_send=(1,),
    back_recv=(1,),
    core_send=(6,),
    core_recv=(6,),
    ax_send=(5, 3, 3),
    ax_recv=(5, 3, 3),
)


def main_kernel(entry, place, bricks, cot, wd, wu, result, ret_out, grads, *scratch):
    r = dict(zip(list(SCRATCH) + list(SEMS), scratch))

    class R:
        pass

    m = R()
    m.__dict__.update(r)

    a = lax.axis_index("gx")
    s = lax.axis_index("gy")
    core = lax.rem(s, 2)
    zpos = lax.rem(s // 2, 4)
    ypos = s // 8
    pos = dict(x=a, y=ypos, z=zpos)

    def along(axis, i):
        if axis == "x":
            return (i, s)
        if axis == "y":
            return (a, (i * 4 + zpos) * 2 + core)
        return (a, (ypos * 4 + i) * 2 + core)

    def near(dx, dy):
        return (lax.rem(a + dx + NX_DEV, NX_DEV), lax.rem(s + dy + NY_DEV, NY_DEV))

    sibling = (a, s + 1 - 2 * core)

    def send(src, dst, send_sem, recv_sem, device):
        copy = pltpu.make_async_remote_copy(
            src_ref=src,
            dst_ref=dst,
            send_sem=send_sem,
            recv_sem=recv_sem,
            device_id=device,
            device_id_type=MESH,
        )
        copy.start()
        return copy

    def await_bytes(ref, sem):
        pltpu.make_async_copy(ref, ref, sem).wait()

    loads = [
        pltpu.make_async_copy(src, dst, m.load.at[i])
        for i, (src, dst) in enumerate(
            ((bricks, m.bricks_v), (cot, m.cot_v), (wd, m.wd_v), (wu, m.wu_v))
        )
    ]
    for load in loads:
        load.start()

    barrier = pltpu.get_barrier_semaphore()

    def greet(d, carry):
        pl.semaphore_signal(barrier, inc=1, device_id=near(0, d), device_id_type=MESH)
        return carry

    lax.fori_loop(1, NY_DEV, greet, 0)
    for d in range(1, NX_DEV):
        pl.semaphore_signal(barrier, inc=1, device_id=near(d, 0), device_id_type=MESH)
    pl.semaphore_signal(barrier, inc=1, device_id=near(1, 1), device_id_type=MESH)
    pl.semaphore_signal(barrier, inc=1, device_id=near(-1, -1), device_id_type=MESH)

    lane = lax.broadcasted_iota(I32, (VOX, L - C), 1)
    loads[0].wait()

    def pack(d, carry):
        for rank in range(2):
            t = 2 * d + rank
            rows = pl.ds(rank * VOX, VOX)
            slot = place[t]
            m.out_b[d, rows, pl.ds(0, C)] = m.bricks_v[entry[t]]
            tag = jnp.where(lane == 0, jnp.where(slot >= 0, 1, 0), jnp.where(lane == 1, slot, 0))
            m.out_b[d, rows, pl.ds(C, L - C)] = tag.astype(F32).astype(BF)
        return carry

    lax.fori_loop(0, NY_DEV, pack, 0)
    pl.semaphore_wait(barrier, NY_DEV - 1 + NX_DEV - 1 + 2)

    def scatter(d, carry):
        send(m.out_b.at[d], m.recv_b.at[d], m.a2a_send.at[0], m.a2a_recv.at[0], near(0, d))
        return carry

    lax.fori_loop(1, NY_DEV, scatter, 0)
    m.recv_b[0] = m.out_b[0]

    m.scr[...] = jnp.zeros((TB * VOX, L), F32)
    loads[1].wait()

    def cot_in(g, carry):
        vx, vy = g // 4, lax.rem(g, 4)
        for b in range(16):
            x, y = 4 * (b // 4) + vx, 4 * (b % 4) + vy
            rows = pl.ds(pl.multiple_of(g * 256 + b * 16, 16), 16)
            m.scr[rows, pl.ds(0, C)] = m.cot_v[x * 16 + y].astype(F32)
        return carry

    lax.fori_loop(0, 16, cot_in, 0)

    def cot_out(g, carry):
        for vz in range(4):
            rows = pl.ds(g * 256 + vz, TB, stride=4)
            cols = pl.ds(pl.multiple_of((g * 4 + vz) * L, L), L)
            m.eg[1, :, cols] = m.scr[rows, :].astype(BF)
        return carry

    lax.fori_loop(0, 16, cot_out, 0)

    loads[2].wait()
    loads[3].wait()
    m.wup[...] = jnp.zeros((C2, NL), BF)
    for k in range(27):
        m.wdp[pl.ds(k * L, C), :] = m.wd_v[k]
        m.wdp[pl.ds(k * L + C, L - C), :] = jnp.zeros((L - C, C2), BF)
        m.wup[:, pl.ds(k * L, C)] = m.wu_v[k]
    m.wdp[pl.ds(27 * L, L), :] = jnp.zeros((L, C2), BF)
    for i in range(2):
        m.pm[i, :, pl.ds(27 * L, L)] = jnp.zeros((8 * TB, L), BF)

    await_bytes(m.recv_b.at[pl.ds(1, NY_DEV - 1)], m.a2a_recv.at[0])

    def brick_in(d, carry):
        rows = pl.ds(pl.multiple_of(d * 2 * VOX, 2 * VOX), 2 * VOX)
        m.scr[rows, :] = m.recv_b[d].astype(F32)
        return carry

    lax.fori_loop(0, NY_DEV, brick_in, 0)

    def brick_out(v, carry):
        cols = pl.ds(pl.multiple_of(v * L, L), L)
        m.packed[:, cols] = m.scr[pl.ds(v, TB, stride=VOX), :].astype(BF)
        return carry

    lax.fori_loop(0, VOX, brick_out, 0, unroll=4)

    rows_i, cols_i = iotas(TB, TB)
    slot_col = m.packed[:, pl.ds(0, L)].astype(F32)[:, C + 1 : C + 2]
    from_slot = one_hot(slot_col == cols_i.astype(F32))
    to_slot = dot_nt(one_hot(rows_i == cols_i), from_slot).astype(BF)

    def place_bricks(n, carry):
        cols = pl.ds(pl.multiple_of(n * 1024, 1024), 1024)
        m.eg[0, :, cols] = dot(to_slot, m.packed[:, cols]).astype(BF)
        return carry

    lax.fori_loop(0, 8, place_bricks, 0)
    occ = m.eg[0, :, pl.ds(0, L)].astype(F32)[:, C : C + 1]

    def mask_seed(n, carry):
        cols = pl.ds(pl.multiple_of(n * 1024, 1024), 1024)
        m.eg[1, :, cols] = (m.eg[1, :, cols].astype(F32) * occ).astype(BF)
        return carry

    lax.fori_loop(0, 8, mask_seed, 0)

    q, c = iotas(16, TB)
    pick_top = one_hot(c == (q >> 2) * 16 + 12 + (q & 3))
    pick_low = one_hot(c == (q >> 2) * 16 + (q & 3))
    for i in range(2):
        for vx in range(4):
            m.hy_send[i, :, col(vx, 512)] = dot(
                pick_top, m.eg[i, :, pl.ds((vx * 16 + 12) * L, 512)]
            ).astype(BF)
    halo = [
        send(
            m.eg.at[:, pl.ds(48, 16), pl.ds(48 * L, 16 * L)],
            m.hx,
            m.halo_send.at[0],
            m.halo_recv.at[0],
            near(1, 0),
        ),
        send(m.hy_send, m.hy, m.halo_send.at[1], m.halo_recv.at[1], near(0, 1)),
        send(
            m.eg.at[:, pl.ds(48, 16), pl.ds(60 * L, 4 * L)],
            m.hc,
            m.halo_send.at[2],
            m.halo_recv.at[2],
            near(1, 1),
        ),
    ]

    rw, cw = iotas(TB, 80)
    by = (rw >> 2) & 3
    shift_y = one_hot(
        ((cw < TB) & (by > 0) & (cw == rw - 4))
        | ((by == 0) & (s > 0) & (cw == TB + (rw >> 4) * 4 + (rw & 3)))
    )
    rw, cw = iotas(TB, 96)
    by = (rw >> 2) & 3
    bx = rw >> 4
    shift_xy = one_hot(
        ((cw < TB) & (by > 0) & (cw == rw - 4))
        | ((by == 0) & (s > 0) & (bx > 0) & (cw == TB + (bx - 1) * 4 + (rw & 3)))
        | ((by == 0) & (s > 0) & (bx == 0) & (a > 0) & (cw == 80 + 12 + (rw & 3)))
    )
    shift_z = one_hot(((rows_i & 3) > 0) & (cols_i == rows_i - 1))

    for copy in halo:
        copy.wait()

    for i in range(2):
        hx = m.hx[i]
        m.ex[i, pl.ds(0, 16), :] = jnp.where(a > 0, hx, jnp.zeros_like(hx))
        m.ex[i, pl.ds(16, 48), :] = m.eg[i, pl.ds(0, 48), pl.ds(48 * L, 16 * L)]
        rows = jnp.concatenate(
            [m.ex[i, :, pl.ds(12 * L, 512)], m.hy[i, :, pl.ds(3 * 512, 512)], m.hc[i]], axis=0
        )
        m.ey[i, :, pl.ds(0, 512)] = dot(shift_xy, rows).astype(BF)
        for vx in range(4):
            rows = jnp.concatenate(
                [m.eg[i, :, pl.ds((vx * 16 + 12) * L, 512)], m.hy[i, :, pl.ds(vx * 512, 512)]],
                axis=0,
            )
            m.ey[i, :, pl.ds((vx + 1) * 512, 512)] = dot(shift_y, rows).astype(BF)

        def block(vx, vy, vz):
            if vz < 0:
                return m.ez[i, :, col((vx + 1) * 5 + vy + 1)]
            if vy < 0:
                return m.ey[i, :, col((vx + 1) * 4 + vz)]
            if vx < 0:
                return m.ex[i, :, col(vy * 4 + vz)]
            return m.eg[i, :, col(vx * 16 + vy * 4 + vz)]

        for vx in range(-1, 4):
            cols = jnp.concatenate([block(vx, vy, 3) for vy in range(-1, 4)], axis=1)
            m.ez[i, :, pl.ds((vx + 1) * 5 * L, 5 * L)] = dot(shift_z, cols).astype(BF)
        for u in range(8):
            ux, uy, uz = u // 4, u // 2 % 2, u % 2
            for k in range(27):
                kx, ky, kz = k // 9, k // 3 % 3, k % 3
                m.pm[i, pl.ds(u * TB, TB), col(k)] = block(
                    2 * ux + kx - 1, 2 * uy + ky - 1, 2 * uz + kz - 1
                )

    m.before[...] = jnp.zeros((8 * TB, C2), F32)
    m.back[...] = jnp.zeros((8 * TB, C2), F32)

    def strided(n, carry):
        ks = pl.ds(pl.multiple_of(n * 512, 512), 512)
        m.before[...] += dot(m.pm[0, :, ks], m.wdp[ks, :])
        m.back[...] += dot_nt(m.pm[1, :, ks], m.wup[:, ks])
        return carry

    lax.fori_loop(0, 7, strided, 0)

    def gate(u, carry):
        rows = pl.ds(pl.multiple_of(u * TB, TB), TB)
        v = m.before[rows, :]
        g = jax.nn.sigmoid(v)
        m.cc[0, u] = (v * g * occ).astype(BF)
        m.cc[1, u] = (m.back[rows, :] * (g * (1.0 + v * (1.0 - g))) * occ).astype(BF)
        return carry

    lax.fori_loop(0, 8, gate, 0)

    for i in range(2):
        for u in range(4):
            m.chy_send[i, u] = dot(pick_low, m.cc[i, (u // 2) * 4 + u % 2]).astype(BF)
    coarse_halo = [
        send(
            m.cc.at[:, pl.ds(0, 4), pl.ds(0, 16)],
            m.chx,
            m.halo_send.at[3],
            m.halo_recv.at[3],
            near(-1, 0),
        ),
        send(m.chy_send, m.chy, m.halo_send.at[4], m.halo_recv.at[4], near(0, -1)),
        send(
            m.cc.at[:, pl.ds(0, 2), pl.ds(0, 16)],
            m.chc,
            m.halo_send.at[5],
            m.halo_recv.at[5],
            near(-1, -1),
        ),
    ]

    ident = one_hot(jnp.equal(*iotas(C2, C2)))
    for i in range(2):
        turned = dot_nt(ident, m.cc[i].reshape(8 * TB, C2)).astype(BF)

        def grad(n, carry):
            cols = pl.ds(pl.multiple_of(n * 512, 512), 512)
            m.part[i, :, cols] = dot(turned, m.pm[1 - i, :, cols])
            return carry

        lax.fori_loop(0, 7, grad, 0)

    core_copies = []
    for t in range(3):
        rows = pl.ds(t * 64, 64)
        m.sb[rows, :] = m.part[1 - core, rows, :].astype(BF)
        core_copies.append(
            send(m.sb.at[rows], m.r0.at[rows], m.core_send.at[t], m.core_recv.at[t], sibling)
        )

    axis_copies = []

    def to_axis(stage, t, axis, src, dst):
        copies = []
        for d in range(1, 4):
            i = lax.rem(pos[axis] + d, 4)
            copies.append(
                send(
                    src(i),
                    dst(d),
                    m.ax_send.at[stage, t, d - 1],
                    m.ax_recv.at[stage, t, d - 1],
                    along(axis, i),
                )
            )
        axis_copies.extend(copies)
        return copies

    def rows_of(t, i):
        return pl.ds(pl.multiple_of(t * 64 + i * 16, 16), 16)

    def cols_of(j):
        return pl.ds(pl.multiple_of(j * PART, L), PART)

    stage_a, stage_b, stage_c, stage_d, stage_e = [], [], [], [], []

    def run_a():
        for t in range(3):
            rows = pl.ds(t * 64, 64)
            core_copies[t].wait_recv()
            m.part[core, rows, :] = m.part[core, rows, :] + m.r0[rows, :].astype(F32)
            m.ab[rows, :] = m.part[core, rows, :].astype(BF)
            stage_a.append(
                to_axis(
                    0,
                    t,
                    ORDERS[t][0],
                    lambda i: m.ab.at[rows_of(t, i)],
                    lambda d: m.ar.at[t, d - 1],
                )
            )

    def run_b():
        for t in range(3):
            for copy in stage_a[t]:
                copy.wait_recv()
            mine = m.part[core, rows_of(t, pos[ORDERS[t][0]]), :]
            for d in range(3):
                mine = mine + m.ar[t, d].astype(F32)
            m.part[core, rows_of(t, pos[ORDERS[t][0]]), :] = mine
            m.bb[t] = mine.astype(BF)
            stage_b.append(
                to_axis(
                    1,
                    t,
                    ORDERS[t][1],
                    lambda j: m.bb.at[t, :, cols_of(j)],
                    lambda d: m.br.at[t, d - 1],
                )
            )

    def run_c():
        for t in range(3):
            first, second, third = ORDERS[t]
            for copy in stage_b[t]:
                copy.wait_recv()
            mine = m.part[core, rows_of(t, pos[first]), cols_of(pos[second])]
            for d in range(3):
                mine = mine + m.br[t, d].astype(F32)
            m.cr[t, pos[third]] = mine.astype(BF)
            stage_c.append(
                to_axis(
                    2,
                    t,
                    third,
                    lambda i: m.cr.at[t, pos[third]],
                    lambda d: m.cr.at[t, pos[third]],
                )
            )

    def run_d():
        for t in range(3):
            first, second, third = ORDERS[t]
            for d in range(1, 4):
                await_bytes(
                    m.cr.at[t, lax.rem(pos[third] + 4 - d, 4)], m.ax_recv.at[2, t, d - 1]
                )
            whole = m.cr[t, 0].astype(F32)
            for d in range(1, 4):
                whole = whole + m.cr[t, d].astype(F32)
            here = m.total.at[core, rows_of(t, pos[first]), cols_of(pos[second])]
            here[...] = whole.astype(BF)
            stage_d.append(to_axis(3, t, second, lambda j: here, lambda d: here))

    def run_e():
        for t in range(3):
            first, second, third = ORDERS[t]
            for d in range(1, 4):
                j = lax.rem(pos[second] + 4 - d, 4)
                await_bytes(
                    m.total.at[core, rows_of(t, pos[first]), cols_of(j)],
                    m.ax_recv.at[3, t, d - 1],
                )
            here = m.total.at[core, rows_of(t, pos[first])]
            stage_e.append(to_axis(4, t, first, lambda j: here, lambda d: here))

    def run_f():
        for t in range(3):
            first = ORDERS[t][0]
            for d in range(1, 4):
                i = lax.rem(pos[first] + 4 - d, 4)
                await_bytes(m.total.at[core, rows_of(t, i)], m.ax_recv.at[4, t, d - 1])
            here = m.total.at[core, pl.ds(t * 64, 64)]
            core_copies.append(
                send(here, here, m.core_send.at[3 + t], m.core_recv.at[3 + t], sibling)
            )

    rw, cw = iotas(TB, 80)
    by = (rw >> 2) & 3
    lift_y = one_hot(
        ((cw < TB) & (by < 3) & (cw == rw + 4))
        | ((by == 3) & (s < NY_DEV - 1) & (cw == TB + (rw >> 4) * 4 + (rw & 3)))
    )
    rw, cw = iotas(TB, 96)
    by = (rw >> 2) & 3
    bx = rw >> 4
    lift_xy = one_hot(
        ((cw < TB) & (by < 3) & (cw == rw + 4))
        | ((by == 3) & (s < NY_DEV - 1) & (bx < 3) & (cw == TB + (bx + 1) * 4 + (rw & 3)))
        | (
            (by == 3)
            & (s < NY_DEV - 1)
            & (bx == 3)
            & (a < NX_DEV - 1)
            & (cw == 80 + (rw & 3))
        )
    )
    lift_z = one_hot(((rows_i & 3) < 3) & (cols_i == rows_i + 1))

    def at(ux, uy, uz):
        return ux * 9 + uy * 3 + uz

    def extend(i):
        for u in range(8):
            m.ce[i, at(u // 4, u // 2 % 2, u % 2)] = m.cc[i, u]
        for uy in range(2):
            for uz in range(2):
                h = m.chx[i, uy * 2 + uz]
                m.ce[i, at(2, uy, uz), pl.ds(0, 48), :] = m.cc[i, uy * 2 + uz, pl.ds(16, 48), :]
                m.ce[i, at(2, uy, uz), pl.ds(48, 16), :] = jnp.where(
                    a < NX_DEV - 1, h, jnp.zeros_like(h)
                )
        for uz in range(2):
            for ux in range(2):
                rows = jnp.concatenate([m.ce[i, at(ux, 0, uz)], m.chy[i, ux * 2 + uz]], axis=0)
                m.ce[i, at(ux, 2, uz)] = dot(lift_y, rows).astype(BF)
            rows = jnp.concatenate(
                [m.ce[i, at(2, 0, uz)], m.chy[i, uz], m.chc[i, uz]], axis=0
            )
            m.ce[i, at(2, 2, uz)] = dot(lift_xy, rows).astype(BF)
        for ux in range(3):
            for uy in range(3):
                m.ce[i, at(ux, uy, 2)] = dot(lift_z, m.ce[i, at(ux, uy, 0)]).astype(BF)

    terms = (((1, 0),), ((2, 0), (0, 1)))

    def transposed(i, emit):
        for p in range(8):
            px, py, pz = p // 4, p // 2 % 2, p % 2
            total = None
            for kx, sx in terms[px]:
                for ky, sy in terms[py]:
                    for kz, sz in terms[pz]:
                        rows = jnp.concatenate(
                            [
                                m.ce[i, at(u // 4 + sx, u // 2 % 2 + sy, u % 2 + sz)]
                                for u in range(8)
                            ],
                            axis=0,
                        )
                        k = kx * 9 + ky * 3 + kz
                        if i == 0:
                            term = dot(rows, m.wup[:, col(k)])
                        else:
                            term = dot_nt(rows, m.wdp[col(k), :])
                        total = term if total is None else total + term
            for u in range(8):
                vx, vy, vz = 2 * (u // 4) + px, 2 * (u // 2 % 2) + py, 2 * (u % 2) + pz
                emit(vx, vy, vz, total[u * TB : (u + 1) * TB])

    def emit_result(vx, vy, vz, value):
        value = (m.eg[0, :, col(vx * 16 + vy * 4 + vz)].astype(F32) + value) * occ
        m.scr[pl.ds((vx * 4 + vy) * 256 + vz, TB, stride=4), :] = value

    def emit_grad(vx, vy, vz, value):
        cols = col(vx * 16 + vy * 4 + vz)
        m.fb[:, cols] = (m.eg[1, :, cols].astype(F32) + value).astype(BF)

    for copy in coarse_halo:
        copy.wait()
    extend(1)
    run_a()
    transposed(1, emit_grad)

    def gather(n, carry):
        cols = pl.ds(pl.multiple_of(n * 512, 512), 512)
        values = dot(from_slot, m.fb[:, cols])
        for b in range(4):
            m.scr2[pl.ds(n * 4 + b, TB, stride=VOX), :] = values[:, b * L : (b + 1) * L]
        return carry

    lax.fori_loop(0, 16, gather, 0)

    def reply(d, carry):
        rows = pl.ds(pl.multiple_of(d * 2 * VOX, 2 * VOX), 2 * VOX)
        m.rep[d] = m.scr2[rows, :].astype(BF)
        return carry

    lax.fori_loop(0, NY_DEV, reply, 0)

    def send_back(d, carry):
        send(m.rep.at[d], m.ret.at[d], m.back_send.at[0], m.back_recv.at[0], near(0, -d))
        return carry

    run_b()
    lax.fori_loop(1, NY_DEV, send_back, 0)
    m.ret[0] = m.rep[0]
    extend(0)
    run_c()
    transposed(0, emit_result)
    run_d()

    def result_out(g, carry):
        vx, vy = g // 4, lax.rem(g, 4)
        for b in range(16):
            x, y = 4 * (b // 4) + vx, 4 * (b % 4) + vy
            rows = pl.ds(pl.multiple_of(g * 256 + b * 16, 16), 16)
            m.res_v[x * 16 + y] = m.scr[rows, :][:, :C].astype(BF)
        return carry

    lax.fori_loop(0, 16, result_out, 0)
    stores = [pltpu.make_async_copy(m.res_v, result, m.store.at[0])]
    stores[0].start()
    run_e()
    await_bytes(m.ret.at[pl.ds(1, NY_DEV - 1)], m.back_recv.at[0])
    stores.append(pltpu.make_async_copy(m.ret, ret_out, m.store.at[1]))
    stores[1].start()
    run_f()
    for t in range(3):
        core_copies[t].wait_send()
        core_copies[3 + t].wait_send()
        await_bytes(m.total.at[1 - core, pl.ds(t * 64, 64)], m.core_recv.at[3 + t])
    stores.append(pltpu.make_async_copy(m.total, grads, m.store.at[2]))
    stores[2].start()
    await_bytes(m.out_b.at[pl.ds(1, NY_DEV - 1)], m.a2a_send.at[0])
    await_bytes(m.rep.at[pl.ds(1, NY_DEV - 1)], m.back_send.at[0])
    for copy in axis_copies:
        copy.wait_send()
    for store in stores:
        store.wait()


def main_call(entry, place, bricks, cot, wd, wu):
    smem = pl.BlockSpec(memory_space=pltpu.SMEM)
    hbm = pl.BlockSpec(memory_space=pl.ANY)
    scratch = [pltpu.VMEM(shape, dtype) for shape, dtype in SCRATCH.values()]
    scratch += [pltpu.SemaphoreType.DMA(shape) for shape in SEMS.values()]
    return pl.pallas_call(
        main_kernel,
        out_shape=(
            jax.ShapeDtypeStruct((256, 16, C), BF),
            jax.ShapeDtypeStruct((NY_DEV, 2 * VOX, L), BF),
            jax.ShapeDtypeStruct((2, C2, NL), BF),
        ),
        in_specs=[smem, smem, hbm, hbm, hbm, hbm],
        out_specs=[hbm] * 3,
        scratch_shapes=scratch,
        compiler_params=pltpu.CompilerParams(
            collective_id=0, has_side_effects=True, vmem_limit_bytes=60 * 2**20
        ),
    )(entry, place, bricks, cot, wd, wu)


def final_kernel(target, ret, grads, early, brick_grads, down, up, result, ret_v, grads_v, bg_v, down_v, up_v, sems):
    pass_on = pltpu.make_async_copy(early, result, sems.at[0])
    pass_on.start()
    get_ret = pltpu.make_async_copy(ret, ret_v, sems.at[1])
    get_ret.start()
    get_grads = pltpu.make_async_copy(grads, grads_v, sems.at[2])
    get_grads.start()
    get_ret.wait()

    def take(j, carry):
        t = target[j]
        bg_v[j] = ret_v[t][:, :C]
        return carry

    lax.fori_loop(0, ENTRIES, take, 0, unroll=2)
    put_bricks = pltpu.make_async_copy(bg_v, brick_grads, sems.at[3])
    put_bricks.start()
    get_grads.wait()
    ident = one_hot(jnp.equal(*iotas(C, L)))
    for k in range(27):
        up_v[k] = grads_v[0, :, pl.ds(k * L, L)][:, :C].astype(F32)
    put_up = pltpu.make_async_copy(up_v, up, sems.at[4])
    put_up.start()
    for k in range(27):
        down_v[k] = dot_nt(ident, grads_v[1, :, pl.ds(k * L, L)])
    put_down = pltpu.make_async_copy(down_v, down, sems.at[5])
    put_down.start()
    pass_on.wait()
    put_bricks.wait()
    put_up.wait()
    put_down.wait()


def final_call(target, ret, grads, early):
    smem = pl.BlockSpec(memory_space=pltpu.SMEM)
    hbm = pl.BlockSpec(memory_space=pl.ANY)
    return pl.pallas_call(
        final_kernel,
        out_shape=(
            jax.ShapeDtypeStruct((ENTRIES, VOX, C), BF),
            jax.ShapeDtypeStruct((27, C, C2), F32),
            jax.ShapeDtypeStruct((27, C2, C), F32),
            jax.ShapeDtypeStruct((256, 16, C), BF),
        ),
        in_specs=[smem, hbm, hbm, hbm],
        out_specs=[hbm] * 4,
        scratch_shapes=[
            pltpu.VMEM((TB, VOX, L), BF),
            pltpu.VMEM((2, C2, NL), BF),
            pltpu.VMEM((ENTRIES, VOX, C), BF),
            pltpu.VMEM((27, C, C2), F32),
            pltpu.VMEM((27, C2, C), F32),
            pltpu.SemaphoreType.DMA((6,)),
        ],
        compiler_params=pltpu.CompilerParams(vmem_limit_bytes=40 * 2**20),
    )(target, ret, grads, early)


def on_device(bricks, brick_owner, brick_slot, down_weight, up_weight, cotangent):
    me = lax.axis_index("gy").reshape(1)
    entry, place, target = routes(me, brick_owner.reshape(ENTRIES), brick_slot.reshape(ENTRIES))
    early, ret, grads = main_call(
        entry,
        place,
        bricks.reshape(ENTRIES, VOX, C),
        cotangent.reshape(256, 16, C),
        down_weight,
        up_weight,
    )
    brick_grads, down, up, result = final_call(target, ret.reshape(TB, VOX, L), grads, early)
    return (
        result.reshape(16, 16, 16, C),
        brick_grads.reshape(1, 1, ENTRIES, VOX, C),
        down,
        up,
    )


def solution(mesh):
    placed = (
        P("gx", "gy", None, None, None),
        P("gx", "gy", None),
        P("gx", "gy", None),
        P(),
        P(),
        P("gx", "gy", None, None),
    )
    return jax.shard_map(
        on_device,
        mesh=mesh,
        in_specs=placed,
        out_specs=(P("gx", "gy", None, None), P("gx", "gy", None, None, None), P(), P()),
        check_vma=False,
    )
```

```python
import jax
import jax.numpy as jnp
from jax import lax
from jax.experimental import pallas as pl
from jax.experimental.pallas import tpu as pltpu
from jax.sharding import PartitionSpec as P

C = 96
C2 = 192
L = 128
TB = 64
VOX = 64
ENTRIES = 56
NY_DEV = 32
NX_DEV = 4
NL = 28 * L
PART = 7 * L
ROWS = VOX * C // L
PAIR = 2 * ROWS

BF = jnp.bfloat16
F32 = jnp.float32
I32 = jnp.int32
MESH = pl.DeviceIdType.MESH
ORDERS = (("x", "y", "z"), ("y", "z", "x"), ("z", "x", "y"))
NT = (((1,), (1,)), ((), ()))


def dot(a, b):
    return jnp.dot(a, b, preferred_element_type=F32)


def dot_nt(a, b):
    return lax.dot_general(a, b, NT, preferred_element_type=F32)


def iotas(rows, cols):
    return (
        lax.broadcasted_iota(I32, (rows, cols), 0),
        lax.broadcasted_iota(I32, (rows, cols), 1),
    )


def one_hot(hit):
    return jnp.where(hit, 1.0, 0.0).astype(BF)


def col(block, width=L, count=1):
    return pl.ds(block * width, count * width)


SCRATCH = dict(
    bricks_v=((ENTRIES, VOX, C), BF),
    cot_v=((256, 16, C), BF),
    wd_v=((27, C, C2), BF),
    wu_v=((27, C2, C), BF),
    out_b=((NY_DEV, PAIR, L), BF),
    recv_b=((NY_DEV, PAIR, L), BF),
    entry_v=((1, L), I32),
    tag_v=((1, L), I32),
    tag_r=((NY_DEV, 1, L), I32),
    target_v=((1, L), I32),
    scr=((TB * VOX, L), F32),
    scr2=((TB * VOX, L), F32),
    eg=((2, TB, VOX * L), BF),
    ex=((2, TB, 16 * L), BF),
    ey=((2, TB, 20 * L), BF),
    ez=((2, TB, 25 * L), BF),
    hx=((2, 16, 16 * L), BF),
    hy=((2, 16, 16 * L), BF),
    hc=((2, 16, 4 * L), BF),
    hy_send=((2, 16, 16 * L), BF),
    pm=((2, 8 * TB, NL), BF),
    wdp=((NL, C2), BF),
    wup=((C2, NL), BF),
    before=((8 * TB, C2), F32),
    back=((8 * TB, C2), F32),
    cc=((2, 8, TB, C2), BF),
    ce=((2, 27, TB, C2), BF),
    chx=((2, 4, 16, C2), BF),
    chy=((2, 4, 16, C2), BF),
    chc=((2, 2, 16, C2), BF),
    chy_send=((2, 4, 16, C2), BF),
    part=((C2, NL), F32),
    sb=((C2, NL), BF),
    r0=((C2, NL), BF),
    ab=((C2, NL), BF),
    ar=((3, 3, 16, NL), BF),
    bb=((3, 16, NL), BF),
    br=((3, 3, 16, PART), BF),
    cr=((3, 4, 16, PART), BF),
    total=((2, C2, NL), BF),
    fb=((TB, VOX * L), BF),
    rep=((NY_DEV, PAIR, L), BF),
    ret=((NY_DEV, PAIR, L), BF),
    res_v=((256, 16, C), BF),
)
SEMS = dict(
    load=(4,),
    route=(1,),
    store=(6,),
    tag_send=(1,),
    tag_recv=(1,),
    a2a_send=(1,),
    a2a_recv=(1,),
    halo_send=(9,),
    halo_recv=(9,),
    back_send=(1,),
    back_recv=(1,),
    core_send=(3, 5),
    core_recv=(3, 5),
    ax_send=(5, 3, 3),
    ax_recv=(5, 3, 3),
)


def main_kernel(owner, slot, bricks, cot, wd, wu, result, ret_out, grads, target, *scratch):
    r = dict(zip(list(SCRATCH) + list(SEMS) + ["entry_s"], scratch))

    class R:
        pass

    m = R()
    m.__dict__.update(r)

    a = lax.axis_index("gx")
    s = lax.axis_index("gy")
    core = lax.rem(s, 2)
    zpos = lax.rem(s // 2, 4)
    ypos = s // 8
    pos = dict(x=a, y=ypos, z=zpos)

    def along(axis, i):
        if axis == "x":
            return (i, s)
        if axis == "y":
            return (a, (i * 4 + zpos) * 2 + core)
        return (a, (ypos * 4 + i) * 2 + core)

    def near(dx, dy):
        return (lax.rem(a + dx + NX_DEV, NX_DEV), lax.rem(s + dy + NY_DEV, NY_DEV))

    sibling = (a, s + 1 - 2 * core)

    def send(src, dst, send_sem, recv_sem, device):
        copy = pltpu.make_async_remote_copy(
            src_ref=src,
            dst_ref=dst,
            send_sem=send_sem,
            recv_sem=recv_sem,
            device_id=device,
            device_id_type=MESH,
        )
        copy.start()
        return copy

    def await_bytes(ref, sem):
        pltpu.make_async_copy(ref, ref, sem).wait()

    loads = [
        pltpu.make_async_copy(src, dst, m.load.at[i])
        for i, (src, dst) in enumerate(
            ((bricks, m.bricks_v), (cot, m.cot_v), (wd, m.wd_v), (wu, m.wu_v))
        )
    ]
    for load in loads:
        load.start()

    barrier = pltpu.get_barrier_semaphore()

    def greet(d, carry):
        pl.semaphore_signal(barrier, inc=1, device_id=near(0, d), device_id_type=MESH)
        return carry

    lax.fori_loop(1, NY_DEV, greet, 0)
    for d in range(1, NX_DEV):
        pl.semaphore_signal(barrier, inc=1, device_id=near(d, 0), device_id_type=MESH)
    pl.semaphore_signal(barrier, inc=1, device_id=near(1, 1), device_id_type=MESH)
    pl.semaphore_signal(barrier, inc=1, device_id=near(-1, -1), device_id_type=MESH)

    rj, cj = iotas(ENTRIES, ENTRIES)
    far = jnp.broadcast_to((owner[...] - s) & (NY_DEV - 1), (ENTRIES, ENTRIES))

    def turn(rows):
        return jnp.sum(jnp.where(rj == cj, rows, 0), axis=1, keepdims=True)

    far_col = turn(far)
    rank = jnp.sum(jnp.where((far_col == far) & (rj < cj), 1, 0), axis=0, keepdims=True)
    goes = jnp.broadcast_to(2 * far[:1] + rank, (ENTRIES, ENTRIES))
    goes_col = turn(goes)
    slot_of = turn(jnp.broadcast_to(slot[...], (ENTRIES, ENTRIES)))
    rt, ct = iotas(ENTRIES, L)
    hit = goes_col == ct
    m.entry_v[...] = jnp.sum(jnp.where(hit, rt, 0), axis=0, keepdims=True)
    m.tag_v[...] = jnp.sum(jnp.where(hit, slot_of + 1, 0), axis=0, keepdims=True) - 1
    m.target_v[...] = jnp.zeros((1, L), I32)
    m.target_v[:, pl.ds(0, ENTRIES)] = goes[:1]
    route = pltpu.make_async_copy(m.entry_v, m.entry_s, m.route.at[0])
    route.start()
    route.wait()
    stores = [pltpu.make_async_copy(m.target_v, target, m.store.at[2])]
    stores[0].start()

    lane = lax.broadcasted_iota(I32, (16, L), 1)
    loads[0].wait()

    def pack(d, carry):
        for rank in range(2):
            brick = m.bricks_v[m.entry_s[0, 2 * d + rank]]
            m.out_b[d, pl.ds(rank * ROWS, ROWS), pl.ds(0, C)] = brick[:ROWS]
            for p in range(3):
                m.out_b[d, pl.ds(rank * ROWS + p * 16, 16), pl.ds(C, L - C)] = brick[
                    ROWS:, p * 32 : (p + 1) * 32
                ]
        return carry

    lax.fori_loop(0, NY_DEV, pack, 0)
    pl.semaphore_wait(barrier, NY_DEV - 1 + NX_DEV - 1 + 2)

    def scatter_tags(d, carry):
        send(m.tag_v, m.tag_r.at[d], m.tag_send.at[0], m.tag_recv.at[0], near(0, d))
        return carry

    lax.fori_loop(1, NY_DEV, scatter_tags, 0)
    m.tag_r[0] = m.tag_v[...]

    def scatter(d, carry):
        send(m.out_b.at[d], m.recv_b.at[d], m.a2a_send.at[0], m.a2a_recv.at[0], near(0, d))
        return carry

    lax.fori_loop(1, NY_DEV, scatter, 0)
    m.recv_b[0] = m.out_b[0]

    m.scr[...] = jnp.zeros((TB * VOX, L), F32)
    loads[1].wait()

    def cot_in(g, carry):
        vx, vy = g // 4, lax.rem(g, 4)
        for b in range(16):
            x, y = 4 * (b // 4) + vx, 4 * (b % 4) + vy
            rows = pl.ds(pl.multiple_of(g * 256 + b * 16, 16), 16)
            m.scr[rows, pl.ds(0, C)] = m.cot_v[x * 16 + y].astype(F32)
        return carry

    lax.fori_loop(0, 16, cot_in, 0)

    def cot_out(g, carry):
        for vz in range(4):
            rows = pl.ds(g * 256 + vz, TB, stride=4)
            cols = pl.ds(pl.multiple_of((g * 4 + vz) * L, L), L)
            m.eg[1, :, cols] = m.scr[rows, :].astype(BF)
        return carry

    lax.fori_loop(0, 16, cot_out, 0)

    rows_i, cols_i = iotas(TB, TB)
    await_bytes(m.tag_r.at[pl.ds(1, NY_DEV - 1)], m.tag_recv.at[0])
    rg, cg = iotas(NY_DEV, L)
    tags = m.tag_r[...].reshape(NY_DEV, L).astype(F32)
    slot_col = jnp.concatenate(
        [
            jnp.sum(jnp.where(cg == 2 * rg + rank, tags, 0.0), axis=1, keepdims=True)
            for rank in range(2)
        ],
        axis=0,
    )
    from_slot = one_hot(slot_col == cols_i.astype(F32))
    to_slot = dot_nt(one_hot(rows_i == cols_i), from_slot)
    occ = jnp.sum(to_slot, axis=1, keepdims=True)
    to_slot = to_slot.astype(BF)

    def mask_seed(n, carry):
        cols = pl.ds(pl.multiple_of(n * 1024, 1024), 1024)
        m.eg[1, :, cols] = (m.eg[1, :, cols].astype(F32) * occ).astype(BF)
        return carry

    lax.fori_loop(0, 8, mask_seed, 0)

    q, c = iotas(16, TB)
    pick_top = one_hot(c == (q >> 2) * 16 + 12 + (q & 3))
    pick_low = one_hot(c == (q >> 2) * 16 + (q & 3))

    def send_halo(i):
        for vx in range(4):
            m.hy_send[i, :, col(vx, 512)] = dot(
                pick_top, m.eg[i, :, pl.ds((vx * 16 + 12) * L, 512)]
            ).astype(BF)
        moves = (
            (m.eg.at[i, pl.ds(48, 16), pl.ds(48 * L, 16 * L)], m.hx.at[i], near(1, 0)),
            (m.hy_send.at[i], m.hy.at[i], near(0, 1)),
            (m.eg.at[i, pl.ds(48, 16), pl.ds(60 * L, 4 * L)], m.hc.at[i], near(1, 1)),
        )
        return [
            send(src, dst, m.halo_send.at[3 * i + n], m.halo_recv.at[3 * i + n], device)
            for n, (src, dst, device) in enumerate(moves)
        ]

    seed_halo = send_halo(1)

    loads[2].wait()
    loads[3].wait()
    m.wup[...] = jnp.zeros((C2, NL), BF)
    for k in range(27):
        m.wdp[pl.ds(k * L, C), :] = m.wd_v[k]
        m.wdp[pl.ds(k * L + C, L - C), :] = jnp.zeros((L - C, C2), BF)
        m.wup[:, pl.ds(k * L, C)] = m.wu_v[k]
    m.wdp[pl.ds(27 * L, L), :] = jnp.zeros((L, C2), BF)
    for i in range(2):
        m.pm[i, :, pl.ds(27 * L, L)] = jnp.zeros((8 * TB, L), BF)

    await_bytes(m.recv_b.at[pl.ds(1, NY_DEV - 1)], m.a2a_recv.at[0])

    def brick_in(d, carry):
        for rank in range(2):
            body = m.recv_b[d, pl.ds(rank * ROWS, ROWS), :].astype(F32)
            base = pl.multiple_of((2 * d + rank) * VOX, VOX)
            m.scr[pl.ds(base, ROWS), :] = body
            tail = [pltpu.roll(body[p * 16 : (p + 1) * 16], 32 * (p + 1), 1) for p in range(3)]
            m.scr[pl.ds(base + ROWS, 16), :] = jnp.where(
                lane < 32,
                tail[0],
                jnp.where(lane < 64, tail[1], jnp.where(lane < 96, tail[2], 0.0)),
            )
        return carry

    lax.fori_loop(0, NY_DEV, brick_in, 0)

    def place_bricks(g):
        blocks = []
        for vz in range(4):
            v = g * 4 + vz
            ranks = [m.scr[pl.ds(rank * VOX + v, NY_DEV, stride=2 * VOX), :] for rank in range(2)]
            blocks.append(jnp.concatenate(ranks, axis=0).astype(BF))
        m.eg[0, :, col(g, 512)] = dot(to_slot, jnp.concatenate(blocks, axis=1)).astype(BF)

    rim = [g for g in range(16) if g // 4 == 3 or g % 4 == 3]
    for g in rim:
        place_bricks(g)
    brick_halo = send_halo(0)
    for g in range(16):
        if g not in rim:
            place_bricks(g)

    rw, cw = iotas(TB, 80)
    by = (rw >> 2) & 3
    shift_y = one_hot(
        ((cw < TB) & (by > 0) & (cw == rw - 4))
        | ((by == 0) & (s > 0) & (cw == TB + (rw >> 4) * 4 + (rw & 3)))
    )
    rw, cw = iotas(TB, 96)
    by = (rw >> 2) & 3
    bx = rw >> 4
    shift_xy = one_hot(
        ((cw < TB) & (by > 0) & (cw == rw - 4))
        | ((by == 0) & (s > 0) & (bx > 0) & (cw == TB + (bx - 1) * 4 + (rw & 3)))
        | ((by == 0) & (s > 0) & (bx == 0) & (a > 0) & (cw == 80 + 12 + (rw & 3)))
    )
    shift_z = one_hot(((rows_i & 3) > 0) & (cols_i == rows_i - 1))

    def patches(i):
        hx = m.hx[i]
        m.ex[i, pl.ds(0, 16), :] = jnp.where(a > 0, hx, jnp.zeros_like(hx))
        m.ex[i, pl.ds(16, 48), :] = m.eg[i, pl.ds(0, 48), pl.ds(48 * L, 16 * L)]
        rows = jnp.concatenate(
            [m.ex[i, :, pl.ds(12 * L, 512)], m.hy[i, :, pl.ds(3 * 512, 512)], m.hc[i]], axis=0
        )
        m.ey[i, :, pl.ds(0, 512)] = dot(shift_xy, rows).astype(BF)
        for vx in range(4):
            rows = jnp.concatenate(
                [m.eg[i, :, pl.ds((vx * 16 + 12) * L, 512)], m.hy[i, :, pl.ds(vx * 512, 512)]],
                axis=0,
            )
            m.ey[i, :, pl.ds((vx + 1) * 512, 512)] = dot(shift_y, rows).astype(BF)

        def block(vx, vy, vz):
            if vz < 0:
                return m.ez[i, :, col((vx + 1) * 5 + vy + 1)]
            if vy < 0:
                return m.ey[i, :, col((vx + 1) * 4 + vz)]
            if vx < 0:
                return m.ex[i, :, col(vy * 4 + vz)]
            return m.eg[i, :, col(vx * 16 + vy * 4 + vz)]

        for vx in range(-1, 4):
            cols = jnp.concatenate([block(vx, vy, 3) for vy in range(-1, 4)], axis=1)
            m.ez[i, :, pl.ds((vx + 1) * 5 * L, 5 * L)] = dot(shift_z, cols).astype(BF)
        for u in range(8):
            ux, uy, uz = u // 4, u // 2 % 2, u % 2
            for k in range(27):
                kx, ky, kz = k // 9, k // 3 % 3, k % 3
                m.pm[i, pl.ds(u * TB, TB), col(k)] = block(
                    2 * ux + kx - 1, 2 * uy + ky - 1, 2 * uz + kz - 1
                )

    m.before[...] = jnp.zeros((8 * TB, C2), F32)
    m.back[...] = jnp.zeros((8 * TB, C2), F32)

    def strided_back(n, carry):
        ks = pl.ds(pl.multiple_of(n * 512, 512), 512)
        m.back[...] += dot_nt(m.pm[1, :, ks], m.wup[:, ks])
        return carry

    def strided(n, carry):
        ks = pl.ds(pl.multiple_of(n * 512, 512), 512)
        m.before[...] += dot(m.pm[0, :, ks], m.wdp[ks, :])
        return carry

    for copy in seed_halo:
        copy.wait()
    patches(1)
    lax.fori_loop(0, 7, strided_back, 0)
    for copy in brick_halo:
        copy.wait()
    patches(0)
    lax.fori_loop(0, 7, strided, 0)

    def gate(u, carry):
        rows = pl.ds(pl.multiple_of(u * TB, TB), TB)
        v = m.before[rows, :]
        g = jax.nn.sigmoid(v)
        m.cc[0, u] = (v * g * occ).astype(BF)
        m.cc[1, u] = (m.back[rows, :] * (g * (1.0 + v * (1.0 - g))) * occ).astype(BF)
        return carry

    lax.fori_loop(0, 8, gate, 0)

    for i in range(2):
        for u in range(4):
            m.chy_send[i, u] = dot(pick_low, m.cc[i, (u // 2) * 4 + u % 2]).astype(BF)
    coarse_halo = [
        send(
            m.cc.at[:, pl.ds(0, 4), pl.ds(0, 16)],
            m.chx,
            m.halo_send.at[6],
            m.halo_recv.at[6],
            near(-1, 0),
        ),
        send(m.chy_send, m.chy, m.halo_send.at[7], m.halo_recv.at[7], near(0, -1)),
        send(
            m.cc.at[:, pl.ds(0, 2), pl.ds(0, 16)],
            m.chc,
            m.halo_send.at[8],
            m.halo_recv.at[8],
            near(-1, -1),
        ),
    ]

    ident = one_hot(jnp.equal(*iotas(C2, C2)))

    def tile_grad(i, out):
        turned = dot_nt(ident, m.cc[i].reshape(8 * TB, C2)).astype(BF)

        def grad(n, carry):
            cols = pl.ds(pl.multiple_of(n * 512, 512), 512)
            out[:, cols] = dot(turned, m.pm[1 - i, :, cols]).astype(out.dtype)
            return carry

        lax.fori_loop(0, 7, grad, 0)

    tile_grad(1 - core, m.sb)
    core_copies = []
    for t in range(3):
        rows = pl.ds(t * 64, 64)
        core_copies.append(
            send(m.sb.at[rows], m.r0.at[rows], m.core_send.at[t, 0], m.core_recv.at[t, 0], sibling)
        )
    tile_grad(core, m.part)

    axis_copies = []

    def to_axis(stage, t, axis, src, dst):
        copies = []
        for d in range(1, 4):
            i = lax.rem(pos[axis] + d, 4)
            copies.append(
                send(
                    src(i),
                    dst(d),
                    m.ax_send.at[stage, t, d - 1],
                    m.ax_recv.at[stage, t, d - 1],
                    along(axis, i),
                )
            )
        axis_copies.extend(copies)
        return copies

    def rows_of(t, i):
        return pl.ds(pl.multiple_of(t * 64 + i * 16, 16), 16)

    def cols_of(j):
        return pl.ds(pl.multiple_of(j * PART, L), PART)

    stage_a, stage_b, stage_c, stage_d, stage_e = [], [], [], [], []

    def run_a():
        for t in range(3):
            rows = pl.ds(t * 64, 64)
            core_copies[t].wait_recv()
            m.part[rows, :] = m.part[rows, :] + m.r0[rows, :].astype(F32)
            m.ab[rows, :] = m.part[rows, :].astype(BF)
            stage_a.append(
                to_axis(
                    0,
                    t,
                    ORDERS[t][0],
                    lambda i: m.ab.at[rows_of(t, i)],
                    lambda d: m.ar.at[t, d - 1],
                )
            )

    def run_b():
        for t in range(3):
            for copy in stage_a[t]:
                copy.wait_recv()
            mine = m.part[rows_of(t, pos[ORDERS[t][0]]), :]
            for d in range(3):
                mine = mine + m.ar[t, d].astype(F32)
            m.part[rows_of(t, pos[ORDERS[t][0]]), :] = mine
            m.bb[t] = mine.astype(BF)
            stage_b.append(
                to_axis(
                    1,
                    t,
                    ORDERS[t][1],
                    lambda j: m.bb.at[t, :, cols_of(j)],
                    lambda d: m.br.at[t, d - 1],
                )
            )

    def run_c():
        for t in range(3):
            first, second, third = ORDERS[t]
            for copy in stage_b[t]:
                copy.wait_recv()
            mine = m.part[rows_of(t, pos[first]), cols_of(pos[second])]
            for d in range(3):
                mine = mine + m.br[t, d].astype(F32)
            m.cr[t, pos[third]] = mine.astype(BF)
            stage_c.append(
                to_axis(
                    2,
                    t,
                    third,
                    lambda i: m.cr.at[t, pos[third]],
                    lambda d: m.cr.at[t, pos[third]],
                )
            )

    def run_d():
        for t in range(3):
            first, second, third = ORDERS[t]
            for d in range(1, 4):
                await_bytes(
                    m.cr.at[t, lax.rem(pos[third] + 4 - d, 4)], m.ax_recv.at[2, t, d - 1]
                )
            whole = m.cr[t, 0].astype(F32)
            for d in range(1, 4):
                whole = whole + m.cr[t, d].astype(F32)
            here = m.total.at[core, rows_of(t, pos[first]), cols_of(pos[second])]
            here[...] = whole.astype(BF)
            stage_d.append(to_axis(3, t, second, lambda j: here, lambda d: here))

    def hand_over(t, n, i):
        here = m.total.at[core, rows_of(t, i)]
        core_copies.append(
            send(here, here, m.core_send.at[t, 1 + n], m.core_recv.at[t, 1 + n], sibling)
        )

    def run_e():
        for t in range(3):
            first, second, third = ORDERS[t]
            for d in range(1, 4):
                j = lax.rem(pos[second] + 4 - d, 4)
                await_bytes(
                    m.total.at[core, rows_of(t, pos[first]), cols_of(j)],
                    m.ax_recv.at[3, t, d - 1],
                )
            here = m.total.at[core, rows_of(t, pos[first])]
            stage_e.append(to_axis(4, t, first, lambda j: here, lambda d: here))
            hand_over(t, 0, pos[first])

    def run_f():
        for d in (1, 3, 2):
            for t in range(3):
                i = lax.rem(pos[ORDERS[t][0]] + 4 - d, 4)
                await_bytes(m.total.at[core, rows_of(t, i)], m.ax_recv.at[4, t, d - 1])
                hand_over(t, d, i)

    rw, cw = iotas(TB, 80)
    by = (rw >> 2) & 3
    lift_y = one_hot(
        ((cw < TB) & (by < 3) & (cw == rw + 4))
        | ((by == 3) & (s < NY_DEV - 1) & (cw == TB + (rw >> 4) * 4 + (rw & 3)))
    )
    rw, cw = iotas(TB, 96)
    by = (rw >> 2) & 3
    bx = rw >> 4
    lift_xy = one_hot(
        ((cw < TB) & (by < 3) & (cw == rw + 4))
        | ((by == 3) & (s < NY_DEV - 1) & (bx < 3) & (cw == TB + (bx + 1) * 4 + (rw & 3)))
        | (
            (by == 3)
            & (s < NY_DEV - 1)
            & (bx == 3)
            & (a < NX_DEV - 1)
            & (cw == 80 + (rw & 3))
        )
    )
    lift_z = one_hot(((rows_i & 3) < 3) & (cols_i == rows_i + 1))

    def at(ux, uy, uz):
        return ux * 9 + uy * 3 + uz

    def extend(i):
        for u in range(8):
            m.ce[i, at(u // 4, u // 2 % 2, u % 2)] = m.cc[i, u]
        for uy in range(2):
            for uz in range(2):
                h = m.chx[i, uy * 2 + uz]
                m.ce[i, at(2, uy, uz), pl.ds(0, 48), :] = m.cc[i, uy * 2 + uz, pl.ds(16, 48), :]
                m.ce[i, at(2, uy, uz), pl.ds(48, 16), :] = jnp.where(
                    a < NX_DEV - 1, h, jnp.zeros_like(h)
                )
        for uz in range(2):
            for ux in range(2):
                rows = jnp.concatenate([m.ce[i, at(ux, 0, uz)], m.chy[i, ux * 2 + uz]], axis=0)
                m.ce[i, at(ux, 2, uz)] = dot(lift_y, rows).astype(BF)
            rows = jnp.concatenate(
                [m.ce[i, at(2, 0, uz)], m.chy[i, uz], m.chc[i, uz]], axis=0
            )
            m.ce[i, at(2, 2, uz)] = dot(lift_xy, rows).astype(BF)
        for ux in range(3):
            for uy in range(3):
                m.ce[i, at(ux, uy, 2)] = dot(lift_z, m.ce[i, at(ux, uy, 0)]).astype(BF)

    terms = (((1, 0),), ((2, 0), (0, 1)))

    def transposed(i, emit, parities=range(8)):
        for p in parities:
            px, py, pz = p // 4, p // 2 % 2, p % 2
            total = None
            for kx, sx in terms[px]:
                for ky, sy in terms[py]:
                    for kz, sz in terms[pz]:
                        rows = jnp.concatenate(
                            [
                                m.ce[i, at(u // 4 + sx, u // 2 % 2 + sy, u % 2 + sz)]
                                for u in range(8)
                            ],
                            axis=0,
                        )
                        k = kx * 9 + ky * 3 + kz
                        if i == 0:
                            term = dot(rows, m.wup[:, col(k)])
                        else:
                            term = dot_nt(rows, m.wdp[col(k), :])
                        total = term if total is None else total + term
            for u in range(8):
                vx, vy, vz = 2 * (u // 4) + px, 2 * (u // 2 % 2) + py, 2 * (u % 2) + pz
                emit(vx, vy, vz, total[u * TB : (u + 1) * TB])

    def emit_result(vx, vy, vz, value):
        value = (m.eg[0, :, col(vx * 16 + vy * 4 + vz)].astype(F32) + value) * occ
        m.scr[pl.ds((vx * 4 + vy) * 256 + vz, TB, stride=4), :] = value

    def emit_grad(vx, vy, vz, value):
        cols = col(vx * 16 + vy * 4 + vz)
        m.fb[:, cols] = (m.eg[1, :, cols].astype(F32) + value).astype(BF)

    for copy in coarse_halo:
        copy.wait()
    extend(1)
    run_a()
    transposed(1, emit_grad)

    def gather(n, carry):
        cols = pl.ds(pl.multiple_of(n * 512, 512), 512)
        values = dot(from_slot, m.fb[:, cols])
        for b in range(4):
            for rank in range(2):
                rows = pl.ds(rank * VOX + n * 4 + b, NY_DEV, stride=2 * VOX)
                m.scr2[rows, :] = values[
                    rank * NY_DEV : (rank + 1) * NY_DEV, b * L : (b + 1) * L
                ]
        return carry

    def reply(d, carry):
        for rank in range(2):
            base = pl.multiple_of((2 * d + rank) * VOX, VOX)
            tail = m.scr2[pl.ds(base + ROWS, 16), :]
            for p in range(3):
                body = m.scr2[pl.ds(base + p * 16, 16), :]
                m.rep[d, pl.ds(rank * ROWS + p * 16, 16), :] = jnp.where(
                    lane < C, body, pltpu.roll(tail, C - 32 * p, 1)
                ).astype(BF)
        return carry

    def send_back(d, carry):
        send(m.rep.at[d], m.ret.at[d], m.back_send.at[0], m.back_recv.at[0], near(0, -d))
        return carry

    lax.fori_loop(0, 16, gather, 0)
    run_b()
    lax.fori_loop(0, NY_DEV, reply, 0)
    lax.fori_loop(1, 9, send_back, 0)
    m.ret[0] = m.rep[0]
    extend(0)
    run_c()
    lax.fori_loop(9, 17, send_back, 0)
    transposed(0, emit_result, range(0, 6))
    run_d()
    lax.fori_loop(17, 25, send_back, 0)
    transposed(0, emit_result, range(6, 8))
    run_e()
    lax.fori_loop(25, NY_DEV, send_back, 0)

    def result_out(g, carry):
        vx, vy = g // 4, lax.rem(g, 4)
        for b in range(16):
            x, y = 4 * (b // 4) + vx, 4 * (b % 4) + vy
            rows = pl.ds(pl.multiple_of(g * 256 + b * 16, 16), 16)
            m.res_v[x * 16 + y] = m.scr[rows, :][:, :C].astype(BF)
        return carry

    lax.fori_loop(0, 16, result_out, 0)
    stores.append(pltpu.make_async_copy(m.res_v, result, m.store.at[0]))
    stores[1].start()
    run_f()
    await_bytes(m.ret.at[pl.ds(1, NY_DEV - 1)], m.back_recv.at[0])
    stores.append(pltpu.make_async_copy(m.ret, ret_out, m.store.at[1]))
    stores[2].start()
    for t in range(3):
        for d in range(4):
            i = lax.rem(pos[ORDERS[t][0]] + 4 - d, 4)
            await_bytes(m.total.at[1 - core, rows_of(t, i)], m.core_recv.at[t, 1 + d])
        rows = pl.ds(t * 64, 64)
        stores.append(
            pltpu.make_async_copy(m.total.at[:, rows], grads.at[:, rows], m.store.at[3 + t])
        )
        stores[3 + t].start()
    await_bytes(m.tag_r.at[pl.ds(1, NY_DEV - 1)], m.tag_send.at[0])
    await_bytes(m.out_b.at[pl.ds(1, NY_DEV - 1)], m.a2a_send.at[0])
    await_bytes(m.rep.at[pl.ds(1, NY_DEV - 1)], m.back_send.at[0])
    for copy in core_copies + axis_copies:
        copy.wait_send()
    for store in stores:
        store.wait()


def main_call(owner, slot, bricks, cot, wd, wu):
    vmem = pl.BlockSpec(memory_space=pltpu.VMEM)
    hbm = pl.BlockSpec(memory_space=pl.ANY)
    scratch = [pltpu.VMEM(shape, dtype) for shape, dtype in SCRATCH.values()]
    scratch += [pltpu.SemaphoreType.DMA(shape) for shape in SEMS.values()]
    scratch += [pltpu.SMEM((1, L), I32)]
    return pl.pallas_call(
        main_kernel,
        out_shape=(
            jax.ShapeDtypeStruct((256, 16, C), BF),
            jax.ShapeDtypeStruct((NY_DEV, PAIR, L), BF),
            jax.ShapeDtypeStruct((2, C2, NL), BF),
            jax.ShapeDtypeStruct((1, L), I32),
        ),
        in_specs=[vmem, vmem, hbm, hbm, hbm, hbm],
        out_specs=[hbm] * 4,
        scratch_shapes=scratch,
        compiler_params=pltpu.CompilerParams(
            collective_id=0, has_side_effects=True, vmem_limit_bytes=60 * 2**20
        ),
    )(owner, slot, bricks, cot, wd, wu)


def final_kernel(
    target, ret, grads, early, brick_grads, down, up, result, ret_v, grads_v, early_v, bg_v, down_v, up_v, sems
):
    gets = [pltpu.make_async_copy(grads.at[i], grads_v.at[i], sems.at[i]) for i in range(2)]
    get_ret = pltpu.make_async_copy(ret, ret_v, sems.at[2])
    get_early = pltpu.make_async_copy(early, early_v, sems.at[3])
    pass_on = pltpu.make_async_copy(early_v, result, sems.at[7])
    gets[0].start()
    gets[1].start()
    get_ret.start()
    get_early.start()
    lane = lax.broadcasted_iota(I32, (16, L), 1)
    gets[0].wait()
    for k in range(27):
        up_v[k] = grads_v[0, :, pl.ds(k * L, L)][:, :C].astype(F32)
    put_up = pltpu.make_async_copy(up_v, up, sems.at[4])
    put_up.start()
    gets[1].wait()
    ident = one_hot(jnp.equal(*iotas(C, L)))
    for k in range(27):
        down_v[k] = dot_nt(ident, grads_v[1, :, pl.ds(k * L, L)])
    put_down = pltpu.make_async_copy(down_v, down, sems.at[5])
    put_down.start()
    get_early.wait()
    pass_on.start()
    get_ret.wait()

    def take(j, carry):
        body = ret_v[target[0, j]]
        bg_v[j, pl.ds(0, ROWS), :] = body[:, :C]
        tail = [
            pltpu.roll(body[p * 16 : (p + 1) * 16].astype(F32), 32 * (p + 1), 1) for p in range(3)
        ]
        tail = jnp.where(lane < 32, tail[0], jnp.where(lane < 64, tail[1], tail[2]))
        bg_v[j, pl.ds(ROWS, 16), :] = tail[:, :C].astype(BF)
        return carry

    lax.fori_loop(0, ENTRIES, take, 0, unroll=2)
    put_bricks = pltpu.make_async_copy(bg_v, brick_grads, sems.at[6])
    put_bricks.start()
    pass_on.wait()
    put_up.wait()
    put_down.wait()
    put_bricks.wait()


def final_call(target, ret, grads, early):
    smem = pl.BlockSpec(memory_space=pltpu.SMEM)
    hbm = pl.BlockSpec(memory_space=pl.ANY)
    return pl.pallas_call(
        final_kernel,
        out_shape=(
            jax.ShapeDtypeStruct((ENTRIES, VOX, C), BF),
            jax.ShapeDtypeStruct((27, C, C2), F32),
            jax.ShapeDtypeStruct((27, C2, C), F32),
            jax.ShapeDtypeStruct((256, 16, C), BF),
        ),
        in_specs=[smem, hbm, hbm, hbm],
        out_specs=[hbm] * 4,
        scratch_shapes=[
            pltpu.VMEM((TB, ROWS, L), BF),
            pltpu.VMEM((2, C2, NL), BF),
            pltpu.VMEM((256, 16, C), BF),
            pltpu.VMEM((ENTRIES, VOX, C), BF),
            pltpu.VMEM((27, C, C2), F32),
            pltpu.VMEM((27, C2, C), F32),
            pltpu.SemaphoreType.DMA((8,)),
        ],
        compiler_params=pltpu.CompilerParams(vmem_limit_bytes=60 * 2**20),
    )(target, ret, grads, early)


def on_device(bricks, brick_owner, brick_slot, down_weight, up_weight, cotangent):
    early, ret, grads, target = main_call(
        brick_owner.reshape(1, ENTRIES),
        brick_slot.reshape(1, ENTRIES),
        bricks.reshape(ENTRIES, VOX, C),
        cotangent.reshape(256, 16, C),
        down_weight,
        up_weight,
    )
    brick_grads, down, up, result = final_call(target, ret.reshape(TB, ROWS, L), grads, early)
    return (
        result.reshape(16, 16, 16, C),
        brick_grads.reshape(1, 1, ENTRIES, VOX, C),
        down,
        up,
    )


def solution(mesh):
    placed = (
        P("gx", "gy", None, None, None),
        P("gx", "gy", None),
        P("gx", "gy", None),
        P(),
        P(),
        P("gx", "gy", None, None),
    )
    return jax.shard_map(
        on_device,
        mesh=mesh,
        in_specs=placed,
        out_specs=(P("gx", "gy", None, None), P("gx", "gy", None, None, None), P(), P()),
        check_vma=False,
    )
```

```python
import jax
import jax.numpy as jnp
from jax import lax
from jax.experimental import pallas as pl
from jax.experimental.pallas import tpu as pltpu
from jax.sharding import PartitionSpec as P

C = 96
C2 = 192
L = 128
TB = 64
VOX = 64
ENTRIES = 56
NY_DEV = 32
NX_DEV = 4
NL = 28 * L
PART = 7 * L
ROWS = VOX * C // L
PAIR = 2 * ROWS

BF = jnp.bfloat16
F32 = jnp.float32
I32 = jnp.int32
MESH = pl.DeviceIdType.MESH
ORDERS = (("x", "y", "z"), ("y", "z", "x"), ("z", "x", "y"))
FAR_FIRST = sorted(
    range(1, NY_DEV), key=lambda e: -(min(e // 8, 4 - e // 8) + min(e // 2 % 4, 4 - e // 2 % 4))
)
NT = (((1,), (1,)), ((), ()))


def dot(a, b):
    return jnp.dot(a, b, preferred_element_type=F32)


def dot_nt(a, b):
    return lax.dot_general(a, b, NT, preferred_element_type=F32)


def iotas(rows, cols):
    return (
        lax.broadcasted_iota(I32, (rows, cols), 0),
        lax.broadcasted_iota(I32, (rows, cols), 1),
    )


def one_hot(hit):
    return jnp.where(hit, 1.0, 0.0).astype(BF)


def col(block, width=L, count=1):
    return pl.ds(block * width, count * width)


SCRATCH = dict(
    bricks_v=((ENTRIES, VOX, C), BF),
    cot_v=((256, 16, C), BF),
    wd_v=((27, C, C2), BF),
    wu_v=((27, C2, C), BF),
    out_b=((NY_DEV, PAIR, L), BF),
    recv_b=((NY_DEV, PAIR, L), BF),
    entry_v=((1, L), I32),
    tag_v=((1, L), I32),
    tag_r=((NY_DEV, 1, L), I32),
    scr=((TB * VOX, L), F32),
    scr2=((TB * VOX, L), F32),
    eg=((2, TB, VOX * L), BF),
    ex=((2, TB, 16 * L), BF),
    ey=((2, TB, 20 * L), BF),
    ez=((2, TB, 25 * L), BF),
    hx=((2, 16, 16 * L), BF),
    hy=((2, 16, 16 * L), BF),
    hc=((2, 16, 4 * L), BF),
    hy_send=((2, 16, 16 * L), BF),
    pm=((2, 8 * TB, NL), BF),
    wdp=((NL, C2), BF),
    wup=((C2, NL), BF),
    before=((8 * TB, C2), F32),
    back=((8 * TB, C2), F32),
    cc=((2, 8, TB, C2), BF),
    ce=((2, 27, TB, C2), BF),
    chx=((2, 4, 16, C2), BF),
    chy=((2, 4, 16, C2), BF),
    chc=((2, 2, 16, C2), BF),
    chy_send=((2, 4, 16, C2), BF),
    part=((C2, NL), F32),
    sb=((C2, NL), BF),
    r0=((C2, NL), BF),
    ab=((C2, NL), BF),
    ar=((3, 3, 16, NL), BF),
    bb=((3, 16, NL), BF),
    br=((3, 3, 16, PART), BF),
    cr=((3, 4, 16, PART), BF),
    fb=((TB, VOX * L), BF),
    rep=((NY_DEV, PAIR, L), BF),
)
SEMS = dict(
    load=(4,),
    route=(1,),
    tag_send=(1,),
    tag_recv=(1,),
    a2a_send=(1,),
    a2a_recv=(NY_DEV,),
    halo_send=(9,),
    halo_recv=(9,),
    back_send=(1,),
    back_recv=(1,),
    core_send=(3, 5),
    core_recv=(3, 5),
    ax_send=(5, 3, 3),
    ax_recv=(5, 3, 3),
)


def main_kernel(owner, slot, bricks, cot, wd, wu, result, ret_out, grads, target, *scratch):
    r = dict(zip(list(SCRATCH) + list(SEMS) + ["entry_s"], scratch))

    class R:
        pass

    m = R()
    m.__dict__.update(r)
    m.res_v, m.ret, m.total = result, ret_out, grads

    a = lax.axis_index("gx")
    s = lax.axis_index("gy")
    core = lax.rem(s, 2)
    zpos = lax.rem(s // 2, 4)
    ypos = s // 8
    pos = dict(x=a, y=ypos, z=zpos)

    def along(axis, i):
        if axis == "x":
            return (i, s)
        if axis == "y":
            return (a, (i * 4 + zpos) * 2 + core)
        return (a, (ypos * 4 + i) * 2 + core)

    def near(dx, dy):
        return (lax.rem(a + dx + NX_DEV, NX_DEV), lax.rem(s + dy + NY_DEV, NY_DEV))

    def offset(e, sign):
        y = lax.rem(ypos + sign * (e // 8) + 4, 4)
        z = lax.rem(zpos + sign * (e // 2 % 4) + 4, 4)
        return (a, (y * 4 + z) * 2 + lax.rem(core + e % 2, 2))

    sibling = (a, s + 1 - 2 * core)

    def send(src, dst, send_sem, recv_sem, device):
        copy = pltpu.make_async_remote_copy(
            src_ref=src,
            dst_ref=dst,
            send_sem=send_sem,
            recv_sem=recv_sem,
            device_id=device,
            device_id_type=MESH,
        )
        copy.start()
        return copy

    def await_bytes(ref, sem):
        pltpu.make_async_copy(ref, ref, sem).wait()

    loads = [
        pltpu.make_async_copy(src, dst, m.load.at[i])
        for i, (src, dst) in enumerate(
            ((bricks, m.bricks_v), (cot, m.cot_v), (wd, m.wd_v), (wu, m.wu_v))
        )
    ]
    for load in loads:
        load.start()

    barrier = pltpu.get_barrier_semaphore()

    def greet(d, carry):
        pl.semaphore_signal(barrier, inc=1, device_id=near(0, d), device_id_type=MESH)
        return carry

    lax.fori_loop(1, NY_DEV, greet, 0)
    for d in range(1, NX_DEV):
        pl.semaphore_signal(barrier, inc=1, device_id=near(d, 0), device_id_type=MESH)
    pl.semaphore_signal(barrier, inc=1, device_id=near(1, 1), device_id_type=MESH)
    pl.semaphore_signal(barrier, inc=1, device_id=near(-1, -1), device_id_type=MESH)

    rj, cj = iotas(ENTRIES, ENTRIES)
    own = owner[...]
    far = (
        (((own >> 3) - ypos) & 3) * 8 + ((((own >> 1) & 3) - zpos) & 3) * 2 + ((own - core) & 1)
    )
    far = jnp.broadcast_to(far, (ENTRIES, ENTRIES))

    def turn(rows):
        return jnp.sum(jnp.where(rj == cj, rows, 0), axis=1, keepdims=True)

    far_col = turn(far)
    rank = jnp.sum(jnp.where((far_col == far) & (rj < cj), 1, 0), axis=0, keepdims=True)
    goes = jnp.broadcast_to(2 * far[:1] + rank, (ENTRIES, ENTRIES))
    goes_col = turn(goes)
    slot_of = turn(jnp.broadcast_to(slot[...], (ENTRIES, ENTRIES)))
    rt, ct = iotas(ENTRIES, L)
    hit = goes_col == ct
    m.entry_v[...] = jnp.sum(jnp.where(hit, rt, 0), axis=0, keepdims=True)
    m.tag_v[...] = jnp.sum(jnp.where(hit, slot_of + 1, 0), axis=0, keepdims=True) - 1
    target[...] = jnp.zeros((1, L), I32)
    target[:, pl.ds(0, ENTRIES)] = goes[:1]
    route = pltpu.make_async_copy(m.entry_v, m.entry_s, m.route.at[0])
    route.start()
    route.wait()

    lane = lax.broadcasted_iota(I32, (16, L), 1)
    loads[0].wait()

    def pack(d, carry):
        for rank in range(2):
            brick = m.bricks_v[m.entry_s[0, 2 * d + rank]]
            m.out_b[d, pl.ds(rank * ROWS, ROWS), pl.ds(0, C)] = brick[:ROWS]
            for p in range(3):
                m.out_b[d, pl.ds(rank * ROWS + p * 16, 16), pl.ds(C, L - C)] = brick[
                    ROWS:, p * 32 : (p + 1) * 32
                ]
        return carry

    lax.fori_loop(0, NY_DEV, pack, 0, unroll=8)
    pl.semaphore_wait(barrier, NY_DEV - 1 + NX_DEV - 1 + 2)

    for e in FAR_FIRST:
        send(m.tag_v, m.tag_r.at[e], m.tag_send.at[0], m.tag_recv.at[0], offset(e, 1))
    m.tag_r[0] = m.tag_v[...]
    for e in FAR_FIRST:
        send(m.out_b.at[e], m.recv_b.at[e], m.a2a_send.at[0], m.a2a_recv.at[e], offset(e, 1))
    m.recv_b[0] = m.out_b[0]

    m.scr[...] = jnp.zeros((TB * VOX, L), F32)
    loads[1].wait()

    def cot_in(g, carry):
        vx, vy = g // 4, lax.rem(g, 4)
        for b in range(16):
            x, y = 4 * (b // 4) + vx, 4 * (b % 4) + vy
            rows = pl.ds(pl.multiple_of(g * 256 + b * 16, 16), 16)
            m.scr[rows, pl.ds(0, C)] = m.cot_v[x * 16 + y].astype(F32)
        return carry

    lax.fori_loop(0, 16, cot_in, 0)

    def cot_out(g, carry):
        for vz in range(4):
            rows = pl.ds(g * 256 + vz, TB, stride=4)
            cols = pl.ds(pl.multiple_of((g * 4 + vz) * L, L), L)
            m.eg[1, :, cols] = m.scr[rows, :].astype(BF)
        return carry

    lax.fori_loop(0, 16, cot_out, 0)

    rows_i, cols_i = iotas(TB, TB)
    await_bytes(m.tag_r.at[pl.ds(1, NY_DEV - 1)], m.tag_recv.at[0])
    rg, cg = iotas(NY_DEV, L)
    tags = m.tag_r[...].reshape(NY_DEV, L).astype(F32)
    slot_col = jnp.concatenate(
        [
            jnp.sum(jnp.where(cg == 2 * rg + rank, tags, 0.0), axis=1, keepdims=True)
            for rank in range(2)
        ],
        axis=0,
    )
    from_slot = one_hot(slot_col == cols_i.astype(F32))
    to_slot = dot_nt(one_hot(rows_i == cols_i), from_slot)
    occ = jnp.sum(to_slot, axis=1, keepdims=True)
    to_slot = to_slot.astype(BF)

    def mask_seed(n, carry):
        cols = pl.ds(pl.multiple_of(n * 1024, 1024), 1024)
        m.eg[1, :, cols] = (m.eg[1, :, cols].astype(F32) * occ).astype(BF)
        return carry

    lax.fori_loop(0, 8, mask_seed, 0)

    q, c = iotas(16, TB)
    pick_top = one_hot(c == (q >> 2) * 16 + 12 + (q & 3))
    pick_low = one_hot(c == (q >> 2) * 16 + (q & 3))

    def send_halo(i):
        for vx in range(4):
            m.hy_send[i, :, col(vx, 512)] = dot(
                pick_top, m.eg[i, :, pl.ds((vx * 16 + 12) * L, 512)]
            ).astype(BF)
        moves = (
            (m.eg.at[i, pl.ds(48, 16), pl.ds(48 * L, 16 * L)], m.hx.at[i], near(1, 0)),
            (m.hy_send.at[i], m.hy.at[i], near(0, 1)),
            (m.eg.at[i, pl.ds(48, 16), pl.ds(60 * L, 4 * L)], m.hc.at[i], near(1, 1)),
        )
        return [
            send(src, dst, m.halo_send.at[3 * i + n], m.halo_recv.at[3 * i + n], device)
            for n, (src, dst, device) in enumerate(moves)
        ]

    seed_halo = send_halo(1)

    loads[2].wait()
    loads[3].wait()
    m.wup[...] = jnp.zeros((C2, NL), BF)
    for k in range(27):
        m.wdp[pl.ds(k * L, C), :] = m.wd_v[k]
        m.wdp[pl.ds(k * L + C, L - C), :] = jnp.zeros((L - C, C2), BF)
        m.wup[:, pl.ds(k * L, C)] = m.wu_v[k]
    m.wdp[pl.ds(27 * L, L), :] = jnp.zeros((L, C2), BF)
    for i in range(2):
        m.pm[i, :, pl.ds(27 * L, L)] = jnp.zeros((8 * TB, L), BF)

    def brick_in(d):
        for rank in range(2):
            body = m.recv_b[d, pl.ds(rank * ROWS, ROWS), :].astype(F32)
            base = (2 * d + rank) * VOX
            m.scr[pl.ds(base, ROWS), :] = body
            tail = [pltpu.roll(body[p * 16 : (p + 1) * 16], 32 * (p + 1), 1) for p in range(3)]
            m.scr[pl.ds(base + ROWS, 16), :] = jnp.where(
                lane < 32,
                tail[0],
                jnp.where(lane < 64, tail[1], jnp.where(lane < 96, tail[2], 0.0)),
            )

    brick_in(0)
    for e in FAR_FIRST:
        await_bytes(m.recv_b.at[e], m.a2a_recv.at[e])
        brick_in(e)

    def place_bricks(g):
        blocks = []
        for vz in range(4):
            v = g * 4 + vz
            ranks = [m.scr[pl.ds(rank * VOX + v, NY_DEV, stride=2 * VOX), :] for rank in range(2)]
            blocks.append(jnp.concatenate(ranks, axis=0).astype(BF))
        m.eg[0, :, col(g, 512)] = dot(to_slot, jnp.concatenate(blocks, axis=1)).astype(BF)

    rim = [g for g in range(16) if g // 4 == 3 or g % 4 == 3]
    for g in rim:
        place_bricks(g)
    brick_halo = send_halo(0)
    for g in range(16):
        if g not in rim:
            place_bricks(g)

    rw, cw = iotas(TB, 80)
    by = (rw >> 2) & 3
    shift_y = one_hot(
        ((cw < TB) & (by > 0) & (cw == rw - 4))
        | ((by == 0) & (s > 0) & (cw == TB + (rw >> 4) * 4 + (rw & 3)))
    )
    rw, cw = iotas(TB, 96)
    by = (rw >> 2) & 3
    bx = rw >> 4
    shift_xy = one_hot(
        ((cw < TB) & (by > 0) & (cw == rw - 4))
        | ((by == 0) & (s > 0) & (bx > 0) & (cw == TB + (bx - 1) * 4 + (rw & 3)))
        | ((by == 0) & (s > 0) & (bx == 0) & (a > 0) & (cw == 80 + 12 + (rw & 3)))
    )
    shift_z = one_hot(((rows_i & 3) > 0) & (cols_i == rows_i - 1))

    def patches(i):
        hx = m.hx[i]
        m.ex[i, pl.ds(0, 16), :] = jnp.where(a > 0, hx, jnp.zeros_like(hx))
        m.ex[i, pl.ds(16, 48), :] = m.eg[i, pl.ds(0, 48), pl.ds(48 * L, 16 * L)]
        rows = jnp.concatenate(
            [m.ex[i, :, pl.ds(12 * L, 512)], m.hy[i, :, pl.ds(3 * 512, 512)], m.hc[i]], axis=0
        )
        m.ey[i, :, pl.ds(0, 512)] = dot(shift_xy, rows).astype(BF)
        for vx in range(4):
            rows = jnp.concatenate(
                [m.eg[i, :, pl.ds((vx * 16 + 12) * L, 512)], m.hy[i, :, pl.ds(vx * 512, 512)]],
                axis=0,
            )
            m.ey[i, :, pl.ds((vx + 1) * 512, 512)] = dot(shift_y, rows).astype(BF)

        def block(vx, vy, vz):
            if vz < 0:
                return m.ez[i, :, col((vx + 1) * 5 + vy + 1)]
            if vy < 0:
                return m.ey[i, :, col((vx + 1) * 4 + vz)]
            if vx < 0:
                return m.ex[i, :, col(vy * 4 + vz)]
            return m.eg[i, :, col(vx * 16 + vy * 4 + vz)]

        for vx in range(-1, 4):
            cols = jnp.concatenate([block(vx, vy, 3) for vy in range(-1, 4)], axis=1)
            m.ez[i, :, pl.ds((vx + 1) * 5 * L, 5 * L)] = dot(shift_z, cols).astype(BF)
        for u in range(8):
            ux, uy, uz = u // 4, u // 2 % 2, u % 2
            for k in range(27):
                kx, ky, kz = k // 9, k // 3 % 3, k % 3
                m.pm[i, pl.ds(u * TB, TB), col(k)] = block(
                    2 * ux + kx - 1, 2 * uy + ky - 1, 2 * uz + kz - 1
                )

    for copy in seed_halo:
        copy.wait()
    patches(1)
    m.back[...] = dot_nt(m.pm[1], m.wup[...])
    for copy in brick_halo:
        copy.wait()
    patches(0)
    m.before[...] = dot(m.pm[0], m.wdp[...])

    def gate(u, carry):
        rows = pl.ds(pl.multiple_of(u * TB, TB), TB)
        v = m.before[rows, :]
        g = jax.nn.sigmoid(v)
        m.cc[0, u] = (v * g * occ).astype(BF)
        m.cc[1, u] = (m.back[rows, :] * (g * (1.0 + v * (1.0 - g))) * occ).astype(BF)
        return carry

    lax.fori_loop(0, 8, gate, 0)

    for i in range(2):
        for u in range(4):
            m.chy_send[i, u] = dot(pick_low, m.cc[i, (u // 2) * 4 + u % 2]).astype(BF)
    coarse_halo = [
        send(
            m.cc.at[:, pl.ds(0, 4), pl.ds(0, 16)],
            m.chx,
            m.halo_send.at[6],
            m.halo_recv.at[6],
            near(-1, 0),
        ),
        send(m.chy_send, m.chy, m.halo_send.at[7], m.halo_recv.at[7], near(0, -1)),
        send(
            m.cc.at[:, pl.ds(0, 2), pl.ds(0, 16)],
            m.chc,
            m.halo_send.at[8],
            m.halo_recv.at[8],
            near(-1, -1),
        ),
    ]

    ident = one_hot(jnp.equal(*iotas(C2, C2)))

    def tile_grad(i, out):
        turned = dot_nt(ident, m.cc[i].reshape(8 * TB, C2)).astype(BF)

        def grad(n, carry):
            cols = pl.ds(pl.multiple_of(n * 512, 512), 512)
            out[:, cols] = dot(turned, m.pm[1 - i, :, cols]).astype(out.dtype)
            return carry

        lax.fori_loop(0, 7, grad, 0, unroll=True)

    tile_grad(1 - core, m.sb)
    core_copies = []
    for t in range(3):
        rows = pl.ds(t * 64, 64)
        core_copies.append(
            send(m.sb.at[rows], m.r0.at[rows], m.core_send.at[t, 0], m.core_recv.at[t, 0], sibling)
        )
    tile_grad(core, m.part)

    axis_copies = []

    def to_axis(stage, t, axis, src, dst):
        copies = []
        for d in range(1, 4):
            i = lax.rem(pos[axis] + d, 4)
            copies.append(
                send(
                    src(i),
                    dst(d),
                    m.ax_send.at[stage, t, d - 1],
                    m.ax_recv.at[stage, t, d - 1],
                    along(axis, i),
                )
            )
        axis_copies.extend(copies)
        return copies

    def rows_of(t, i):
        return pl.ds(pl.multiple_of(t * 64 + i * 16, 16), 16)

    def cols_of(j):
        return pl.ds(pl.multiple_of(j * PART, L), PART)

    stage_a, stage_b, stage_c, stage_d, stage_e = [], [], [], [], []

    def run_a():
        for t in range(3):
            rows = pl.ds(t * 64, 64)
            core_copies[t].wait_recv()
            m.part[rows, :] = m.part[rows, :] + m.r0[rows, :].astype(F32)
            m.ab[rows, :] = m.part[rows, :].astype(BF)
            stage_a.append(
                to_axis(
                    0,
                    t,
                    ORDERS[t][0],
                    lambda i: m.ab.at[rows_of(t, i)],
                    lambda d: m.ar.at[t, d - 1],
                )
            )

    def run_b():
        for t in range(3):
            for copy in stage_a[t]:
                copy.wait_recv()
            mine = m.part[rows_of(t, pos[ORDERS[t][0]]), :]
            for d in range(3):
                mine = mine + m.ar[t, d].astype(F32)
            m.part[rows_of(t, pos[ORDERS[t][0]]), :] = mine
            m.bb[t] = mine.astype(BF)
            stage_b.append(
                to_axis(
                    1,
                    t,
                    ORDERS[t][1],
                    lambda j: m.bb.at[t, :, cols_of(j)],
                    lambda d: m.br.at[t, d - 1],
                )
            )

    def run_c():
        for t in range(3):
            first, second, third = ORDERS[t]
            for copy in stage_b[t]:
                copy.wait_recv()
            mine = m.part[rows_of(t, pos[first]), cols_of(pos[second])]
            for d in range(3):
                mine = mine + m.br[t, d].astype(F32)
            m.cr[t, pos[third]] = mine.astype(BF)
            stage_c.append(
                to_axis(
                    2,
                    t,
                    third,
                    lambda i: m.cr.at[t, pos[third]],
                    lambda d: m.cr.at[t, pos[third]],
                )
            )

    def run_d():
        for t in range(3):
            first, second, third = ORDERS[t]
            for d in range(1, 4):
                await_bytes(
                    m.cr.at[t, lax.rem(pos[third] + 4 - d, 4)], m.ax_recv.at[2, t, d - 1]
                )
            whole = m.cr[t, 0].astype(F32)
            for d in range(1, 4):
                whole = whole + m.cr[t, d].astype(F32)
            here = m.total.at[core, rows_of(t, pos[first]), cols_of(pos[second])]
            here[...] = whole.astype(BF)
            stage_d.append(to_axis(3, t, second, lambda j: here, lambda d: here))

    def hand_over(t, n, i):
        here = m.total.at[core, rows_of(t, i)]
        core_copies.append(
            send(here, here, m.core_send.at[t, 1 + n], m.core_recv.at[t, 1 + n], sibling)
        )

    def run_e():
        for t in range(3):
            first, second, third = ORDERS[t]
            for d in range(1, 4):
                j = lax.rem(pos[second] + 4 - d, 4)
                await_bytes(
                    m.total.at[core, rows_of(t, pos[first]), cols_of(j)],
                    m.ax_recv.at[3, t, d - 1],
                )
            here = m.total.at[core, rows_of(t, pos[first])]
            stage_e.append(to_axis(4, t, first, lambda j: here, lambda d: here))
            hand_over(t, 0, pos[first])

    def run_f():
        for d in (1, 3, 2):
            for t in range(3):
                i = lax.rem(pos[ORDERS[t][0]] + 4 - d, 4)
                await_bytes(m.total.at[core, rows_of(t, i)], m.ax_recv.at[4, t, d - 1])
                hand_over(t, d, i)

    rw, cw = iotas(TB, 80)
    by = (rw >> 2) & 3
    lift_y = one_hot(
        ((cw < TB) & (by < 3) & (cw == rw + 4))
        | ((by == 3) & (s < NY_DEV - 1) & (cw == TB + (rw >> 4) * 4 + (rw & 3)))
    )
    rw, cw = iotas(TB, 96)
    by = (rw >> 2) & 3
    bx = rw >> 4
    lift_xy = one_hot(
        ((cw < TB) & (by < 3) & (cw == rw + 4))
        | ((by == 3) & (s < NY_DEV - 1) & (bx < 3) & (cw == TB + (bx + 1) * 4 + (rw & 3)))
        | (
            (by == 3)
            & (s < NY_DEV - 1)
            & (bx == 3)
            & (a < NX_DEV - 1)
            & (cw == 80 + (rw & 3))
        )
    )
    lift_z = one_hot(((rows_i & 3) < 3) & (cols_i == rows_i + 1))

    def at(ux, uy, uz):
        return ux * 9 + uy * 3 + uz

    def extend(i):
        for u in range(8):
            m.ce[i, at(u // 4, u // 2 % 2, u % 2)] = m.cc[i, u]
        for uy in range(2):
            for uz in range(2):
                h = m.chx[i, uy * 2 + uz]
                m.ce[i, at(2, uy, uz), pl.ds(0, 48), :] = m.cc[i, uy * 2 + uz, pl.ds(16, 48), :]
                m.ce[i, at(2, uy, uz), pl.ds(48, 16), :] = jnp.where(
                    a < NX_DEV - 1, h, jnp.zeros_like(h)
                )
        for uz in range(2):
            for ux in range(2):
                rows = jnp.concatenate([m.ce[i, at(ux, 0, uz)], m.chy[i, ux * 2 + uz]], axis=0)
                m.ce[i, at(ux, 2, uz)] = dot(lift_y, rows).astype(BF)
            rows = jnp.concatenate(
                [m.ce[i, at(2, 0, uz)], m.chy[i, uz], m.chc[i, uz]], axis=0
            )
            m.ce[i, at(2, 2, uz)] = dot(lift_xy, rows).astype(BF)
        for ux in range(3):
            for uy in range(3):
                m.ce[i, at(ux, uy, 2)] = dot(lift_z, m.ce[i, at(ux, uy, 0)]).astype(BF)

    terms = (((1, 0),), ((2, 0), (0, 1)))

    def transposed(i, emit, parities=range(8)):
        for p in parities:
            px, py, pz = p // 4, p // 2 % 2, p % 2
            total = None
            for kx, sx in terms[px]:
                for ky, sy in terms[py]:
                    for kz, sz in terms[pz]:
                        rows = jnp.concatenate(
                            [
                                m.ce[i, at(u // 4 + sx, u // 2 % 2 + sy, u % 2 + sz)]
                                for u in range(8)
                            ],
                            axis=0,
                        )
                        k = kx * 9 + ky * 3 + kz
                        if i == 0:
                            term = dot(rows, m.wup[:, col(k)])
                        else:
                            term = dot_nt(rows, m.wdp[col(k), :])
                        total = term if total is None else total + term
            for u in range(8):
                vx, vy, vz = 2 * (u // 4) + px, 2 * (u // 2 % 2) + py, 2 * (u % 2) + pz
                emit(vx, vy, vz, total[u * TB : (u + 1) * TB])

    def emit_result(vx, vy, vz, value):
        value = (m.eg[0, :, col(vx * 16 + vy * 4 + vz)].astype(F32) + value) * occ
        m.scr[pl.ds((vx * 4 + vy) * 256 + vz, TB, stride=4), :] = value

    def emit_grad(vx, vy, vz, value):
        cols = col(vx * 16 + vy * 4 + vz)
        m.fb[:, cols] = (m.eg[1, :, cols].astype(F32) + value).astype(BF)

    for copy in coarse_halo:
        copy.wait()
    extend(1)
    run_a()
    transposed(1, emit_grad)

    def gather(n, carry):
        cols = pl.ds(pl.multiple_of(n * 512, 512), 512)
        values = dot(from_slot, m.fb[:, cols])
        for b in range(4):
            for rank in range(2):
                rows = pl.ds(rank * VOX + n * 4 + b, NY_DEV, stride=2 * VOX)
                m.scr2[rows, :] = values[
                    rank * NY_DEV : (rank + 1) * NY_DEV, b * L : (b + 1) * L
                ]
        return carry

    def reply(d, carry):
        for rank in range(2):
            base = pl.multiple_of((2 * d + rank) * VOX, VOX)
            tail = m.scr2[pl.ds(base + ROWS, 16), :]
            for p in range(3):
                body = m.scr2[pl.ds(base + p * 16, 16), :]
                m.rep[d, pl.ds(rank * ROWS + p * 16, 16), :] = jnp.where(
                    lane < C, body, pltpu.roll(tail, C - 32 * p, 1)
                ).astype(BF)
        return carry

    def send_back(part):
        for e in FAR_FIRST[part * 8 : part * 8 + 8]:
            send(m.rep.at[e], m.ret.at[e], m.back_send.at[0], m.back_recv.at[0], offset(e, -1))

    lax.fori_loop(0, 16, gather, 0, unroll=8)
    run_b()
    lax.fori_loop(0, NY_DEV, reply, 0, unroll=8)
    send_back(0)
    m.ret[0] = m.rep[0]
    extend(0)
    run_c()
    send_back(1)
    transposed(0, emit_result, range(0, 6))
    run_d()
    send_back(2)
    transposed(0, emit_result, range(6, 8))
    run_e()
    send_back(3)

    def result_out(g, carry):
        vx, vy = g // 4, lax.rem(g, 4)
        for b in range(16):
            x, y = 4 * (b // 4) + vx, 4 * (b % 4) + vy
            rows = pl.ds(pl.multiple_of(g * 256 + b * 16, 16), 16)
            m.res_v[x * 16 + y] = m.scr[rows, :][:, :C].astype(BF)
        return carry

    lax.fori_loop(0, 16, result_out, 0)
    run_f()
    await_bytes(m.ret.at[pl.ds(1, NY_DEV - 1)], m.back_recv.at[0])
    for t in range(3):
        for d in range(4):
            i = lax.rem(pos[ORDERS[t][0]] + 4 - d, 4)
            await_bytes(m.total.at[1 - core, rows_of(t, i)], m.core_recv.at[t, 1 + d])
    await_bytes(m.tag_r.at[pl.ds(1, NY_DEV - 1)], m.tag_send.at[0])
    await_bytes(m.out_b.at[pl.ds(1, NY_DEV - 1)], m.a2a_send.at[0])
    await_bytes(m.rep.at[pl.ds(1, NY_DEV - 1)], m.back_send.at[0])
    for copy in core_copies + axis_copies:
        copy.wait_send()


def main_call(owner, slot, bricks, cot, wd, wu):
    vmem = pl.BlockSpec(memory_space=pltpu.VMEM)
    hbm = pl.BlockSpec(memory_space=pl.ANY)
    scratch = [pltpu.VMEM(shape, dtype) for shape, dtype in SCRATCH.values()]
    scratch += [pltpu.SemaphoreType.DMA(shape) for shape in SEMS.values()]
    scratch += [pltpu.SMEM((1, L), I32)]
    return pl.pallas_call(
        main_kernel,
        out_shape=(
            pltpu.VMEM((256, 16, C), BF),
            pltpu.VMEM((NY_DEV, PAIR, L), BF),
            pltpu.VMEM((2, C2, NL), BF),
            pltpu.VMEM((1, L), I32),
        ),
        in_specs=[vmem, vmem, hbm, hbm, hbm, hbm],
        out_specs=[vmem] * 4,
        scratch_shapes=scratch,
        compiler_params=pltpu.CompilerParams(
            collective_id=0, has_side_effects=True, vmem_limit_bytes=50 * 2**20
        ),
    )(owner, slot, bricks, cot, wd, wu)


def final_kernel(
    target, ret, grads, early, brick_grads, down, up, result, target_s, bg_v, down_v, up_v, sems
):
    pass_on = pltpu.make_async_copy(early, result, sems.at[0])
    pass_on.start()
    get_target = pltpu.make_async_copy(target, target_s, sems.at[8])
    get_target.start()
    lane = lax.broadcasted_iota(I32, (16, L), 1)
    ident = one_hot(jnp.equal(*iotas(C, L)))
    puts = []
    for k in range(27):
        up_v[k] = grads[0, :, pl.ds(k * L, L)][:, :C].astype(F32)
        down_v[k] = dot_nt(ident, grads[1, :, pl.ds(k * L, L)])
        if k % 9 == 8:
            part = pl.ds(k - 8, 9)
            puts.append(pltpu.make_async_copy(up_v.at[part], up.at[part], sems.at[2 + k // 9]))
            puts.append(pltpu.make_async_copy(down_v.at[part], down.at[part], sems.at[5 + k // 9]))
            puts[-2].start()
            puts[-1].start()

    get_target.wait()

    def take(j, carry):
        body = ret[target_s[0, j]]
        bg_v[j, pl.ds(0, ROWS), :] = body[:, :C]
        tail = [
            pltpu.roll(body[p * 16 : (p + 1) * 16].astype(F32), 32 * (p + 1), 1) for p in range(3)
        ]
        tail = jnp.where(lane < 32, tail[0], jnp.where(lane < 64, tail[1], tail[2]))
        bg_v[j, pl.ds(ROWS, 16), :] = tail[:, :C].astype(BF)
        return carry

    lax.fori_loop(0, ENTRIES, take, 0, unroll=8)
    puts.append(pltpu.make_async_copy(bg_v, brick_grads, sems.at[1]))
    puts[-1].start()
    pass_on.wait()
    for put in puts:
        put.wait()


def final_call(target, ret, grads, early):
    vmem = pl.BlockSpec(memory_space=pltpu.VMEM)
    hbm = pl.BlockSpec(memory_space=pl.ANY)
    return pl.pallas_call(
        final_kernel,
        out_shape=(
            jax.ShapeDtypeStruct((ENTRIES, VOX, C), BF),
            jax.ShapeDtypeStruct((27, C, C2), F32),
            jax.ShapeDtypeStruct((27, C2, C), F32),
            jax.ShapeDtypeStruct((256, 16, C), BF),
        ),
        in_specs=[vmem] * 4,
        out_specs=[hbm] * 4,
        scratch_shapes=[
            pltpu.SMEM((1, L), I32),
            pltpu.VMEM((ENTRIES, VOX, C), BF),
            pltpu.VMEM((27, C, C2), F32),
            pltpu.VMEM((27, C2, C), F32),
            pltpu.SemaphoreType.DMA((9,)),
        ],
        compiler_params=pltpu.CompilerParams(vmem_limit_bytes=20 * 2**20),
    )(target, ret, grads, early)


def on_device(bricks, brick_owner, brick_slot, down_weight, up_weight, cotangent):
    early, ret, grads, target = main_call(
        brick_owner.reshape(1, ENTRIES),
        brick_slot.reshape(1, ENTRIES),
        bricks.reshape(ENTRIES, VOX, C),
        cotangent.reshape(256, 16, C),
        down_weight,
        up_weight,
    )
    brick_grads, down, up, result = final_call(target, ret.reshape(TB, ROWS, L), grads, early)
    return (
        result.reshape(16, 16, 16, C),
        brick_grads.reshape(1, 1, ENTRIES, VOX, C),
        down,
        up,
    )


def solution(mesh):
    placed = (
        P("gx", "gy", None, None, None),
        P("gx", "gy", None),
        P("gx", "gy", None),
        P(),
        P(),
        P("gx", "gy", None, None),
    )
    return jax.shard_map(
        on_device,
        mesh=mesh,
        in_specs=placed,
        out_specs=(P("gx", "gy", None, None), P("gx", "gy", None, None, None), P(), P()),
        check_vma=False,
    )
```

```python
import jax
import jax.numpy as jnp
from jax import lax
from jax.experimental import pallas as pl
from jax.experimental.pallas import tpu as pltpu
from jax.sharding import PartitionSpec as P

C = 96
C2 = 192
L = 128
TB = 64
VOX = 64
ENTRIES = 56
NY_DEV = 32
NX_DEV = 4
NL = 28 * L
NC = 21 * L
NP = 24 * L
PART = NP // 4
ROWS = VOX * C // L
PAIR = 2 * ROWS

BF = jnp.bfloat16
F32 = jnp.float32
I32 = jnp.int32
MESH = pl.DeviceIdType.MESH
ORDERS = (("x", "y", "z"), ("y", "z", "x"), ("z", "x", "y"))
FAR_FIRST = sorted(
    range(1, NY_DEV), key=lambda e: -(min(e // 8, 4 - e // 8) + min(e // 2 % 4, 4 - e // 2 % 4))
)
NT = (((1,), (1,)), ((), ()))


def dot(a, b):
    return jnp.dot(a, b, preferred_element_type=F32)


def dot_nt(a, b):
    return lax.dot_general(a, b, NT, preferred_element_type=F32)


def iotas(rows, cols):
    return (
        lax.broadcasted_iota(I32, (rows, cols), 0),
        lax.broadcasted_iota(I32, (rows, cols), 1),
    )


def one_hot(hit):
    return jnp.where(hit, 1.0, 0.0).astype(BF)


def col(block, width=L, count=1):
    return pl.ds(block * width, count * width)


SCRATCH = dict(
    bricks_v=((ENTRIES, VOX, C), BF),
    cot_v=((256, 16, C), BF),
    wd_v=((27, C, C2), BF),
    wu_v=((27, C2, C), BF),
    out_b=((NY_DEV, PAIR, L), BF),
    recv_b=((NY_DEV, PAIR, L), BF),
    entry_v=((1, L), I32),
    tag_v=((1, L), I32),
    tag_r=((NY_DEV, 1, L), I32),
    scr=((TB * VOX, L), F32),
    scr2=((TB * VOX, L), F32),
    eg=((2, TB, VOX * L), BF),
    ex=((2, TB, 16 * L), BF),
    ey=((2, TB, 20 * L), BF),
    ez=((2, TB, 25 * L), BF),
    hx=((2, 16, 16 * L), BF),
    hy=((2, 16, 16 * L), BF),
    hc=((2, 16, 4 * L), BF),
    hy_send=((2, 16, 16 * L), BF),
    pm=((2, 8 * TB, NL), BF),
    wdp=((NL, C2), BF),
    wup=((C2, NL), BF),
    before=((8 * TB, C2), F32),
    back=((8 * TB, C2), F32),
    cc=((2, 8, TB, C2), BF),
    ce=((2, 27, TB, C2), BF),
    chx=((2, 4, 16, C2), BF),
    chy=((2, 4, 16, C2), BF),
    chc=((2, 2, 16, C2), BF),
    chy_send=((2, 4, 16, C2), BF),
    part=((C2, NC), F32),
    sb=((C2, NC), BF),
    r0=((C2, NC), BF),
    ab=((C2, NC), BF),
    ar=((3, 3, 16, NC), BF),
    mine=((3, 16, NP), F32),
    bb=((3, 16, NP), BF),
    br=((3, 3, 16, PART), BF),
    cr=((3, 4, 16, PART), BF),
    fb=((TB, VOX * L), BF),
    rep=((NY_DEV, PAIR, L), BF),
)
SEMS = dict(
    load=(4,),
    route=(1,),
    tag_send=(1,),
    tag_recv=(1,),
    a2a_send=(1,),
    a2a_recv=(NY_DEV,),
    halo_send=(9,),
    halo_recv=(9,),
    back_send=(1,),
    back_recv=(1,),
    core_send=(7,),
    core_recv=(7,),
    hand_send=(3, 4),
    hand_recv=(3, 4),
    ax_send=(5, 3, 3),
    ax_recv=(5, 3, 3),
)


def main_kernel(owner, slot, bricks, cot, wd, wu, result, ret_out, grads, target, *scratch):
    r = dict(zip(list(SCRATCH) + list(SEMS) + ["entry_s"], scratch))

    class R:
        pass

    m = R()
    m.__dict__.update(r)
    m.res_v, m.ret, m.total = result, ret_out, grads

    a = lax.axis_index("gx")
    s = lax.axis_index("gy")
    core = lax.rem(s, 2)
    zpos = lax.rem(s // 2, 4)
    ypos = s // 8
    pos = dict(x=a, y=ypos, z=zpos)

    def along(axis, i):
        if axis == "x":
            return (i, s)
        if axis == "y":
            return (a, (i * 4 + zpos) * 2 + core)
        return (a, (ypos * 4 + i) * 2 + core)

    def near(dx, dy):
        return (lax.rem(a + dx + NX_DEV, NX_DEV), lax.rem(s + dy + NY_DEV, NY_DEV))

    def offset(e, sign):
        y = lax.rem(ypos + sign * (e // 8) + 4, 4)
        z = lax.rem(zpos + sign * (e // 2 % 4) + 4, 4)
        return (a, (y * 4 + z) * 2 + lax.rem(core + e % 2, 2))

    sibling = (a, s + 1 - 2 * core)

    def send(src, dst, send_sem, recv_sem, device):
        copy = pltpu.make_async_remote_copy(
            src_ref=src,
            dst_ref=dst,
            send_sem=send_sem,
            recv_sem=recv_sem,
            device_id=device,
            device_id_type=MESH,
        )
        copy.start()
        return copy

    def await_bytes(ref, sem):
        pltpu.make_async_copy(ref, ref, sem).wait()

    loads = [
        pltpu.make_async_copy(src, dst, m.load.at[i])
        for i, (src, dst) in enumerate(
            ((bricks, m.bricks_v), (cot, m.cot_v), (wd, m.wd_v), (wu, m.wu_v))
        )
    ]
    for load in loads:
        load.start()

    barrier = pltpu.get_barrier_semaphore()

    def greet(d, carry):
        pl.semaphore_signal(barrier, inc=1, device_id=near(0, d), device_id_type=MESH)
        return carry

    lax.fori_loop(1, NY_DEV, greet, 0)
    for d in range(1, NX_DEV):
        pl.semaphore_signal(barrier, inc=1, device_id=near(d, 0), device_id_type=MESH)
    pl.semaphore_signal(barrier, inc=1, device_id=near(1, 1), device_id_type=MESH)
    pl.semaphore_signal(barrier, inc=1, device_id=near(-1, -1), device_id_type=MESH)

    rj, cj = iotas(ENTRIES, ENTRIES)
    own = owner[...]
    far = (
        (((own >> 3) - ypos) & 3) * 8 + ((((own >> 1) & 3) - zpos) & 3) * 2 + ((own - core) & 1)
    )
    far = jnp.broadcast_to(far, (ENTRIES, ENTRIES))

    def turn(rows):
        return jnp.sum(jnp.where(rj == cj, rows, 0), axis=1, keepdims=True)

    far_col = turn(far)
    rank = jnp.sum(jnp.where((far_col == far) & (rj < cj), 1, 0), axis=0, keepdims=True)
    goes = jnp.broadcast_to(2 * far[:1] + rank, (ENTRIES, ENTRIES))
    goes_col = turn(goes)
    slot_of = turn(jnp.broadcast_to(slot[...], (ENTRIES, ENTRIES)))
    rt, ct = iotas(ENTRIES, L)
    hit = goes_col == ct
    m.entry_v[...] = jnp.sum(jnp.where(hit, rt, 0), axis=0, keepdims=True)
    m.tag_v[...] = jnp.sum(jnp.where(hit, slot_of + 1, 0), axis=0, keepdims=True) - 1
    target[...] = jnp.zeros((1, L), I32)
    target[:, pl.ds(0, ENTRIES)] = goes[:1]
    route = pltpu.make_async_copy(m.entry_v, m.entry_s, m.route.at[0])
    route.start()
    route.wait()

    lane = lax.broadcasted_iota(I32, (16, L), 1)
    loads[0].wait()

    def pack(d, carry):
        for rank in range(2):
            brick = m.bricks_v[m.entry_s[0, 2 * d + rank]]
            m.out_b[d, pl.ds(rank * ROWS, ROWS), pl.ds(0, C)] = brick[:ROWS]
            for p in range(3):
                m.out_b[d, pl.ds(rank * ROWS + p * 16, 16), pl.ds(C, L - C)] = brick[
                    ROWS:, p * 32 : (p + 1) * 32
                ]
        return carry

    lax.fori_loop(0, NY_DEV, pack, 0, unroll=8)
    pl.semaphore_wait(barrier, NY_DEV - 1 + NX_DEV - 1 + 2)

    for e in FAR_FIRST:
        send(m.tag_v, m.tag_r.at[e], m.tag_send.at[0], m.tag_recv.at[0], offset(e, 1))
        send(m.out_b.at[e], m.recv_b.at[e], m.a2a_send.at[0], m.a2a_recv.at[e], offset(e, 1))
    m.tag_r[0] = m.tag_v[...]
    m.recv_b[0] = m.out_b[0]

    m.scr[...] = jnp.zeros((TB * VOX, L), F32)
    loads[1].wait()

    def cot_in(g, carry):
        vx, vy = g // 4, lax.rem(g, 4)
        for b in range(16):
            x, y = 4 * (b // 4) + vx, 4 * (b % 4) + vy
            rows = pl.ds(pl.multiple_of(g * 256 + b * 16, 16), 16)
            m.scr[rows, pl.ds(0, C)] = m.cot_v[x * 16 + y].astype(F32)
        return carry

    lax.fori_loop(0, 16, cot_in, 0)

    def cot_out(g, carry):
        for vz in range(4):
            rows = pl.ds(g * 256 + vz, TB, stride=4)
            cols = pl.ds(pl.multiple_of((g * 4 + vz) * L, L), L)
            m.eg[1, :, cols] = m.scr[rows, :].astype(BF)
        return carry

    lax.fori_loop(0, 16, cot_out, 0)

    rows_i, cols_i = iotas(TB, TB)
    await_bytes(m.tag_r.at[pl.ds(1, NY_DEV - 1)], m.tag_recv.at[0])
    rg, cg = iotas(NY_DEV, L)
    tags = m.tag_r[...].reshape(NY_DEV, L).astype(F32)
    slot_col = jnp.concatenate(
        [
            jnp.sum(jnp.where(cg == 2 * rg + rank, tags, 0.0), axis=1, keepdims=True)
            for rank in range(2)
        ],
        axis=0,
    )
    from_slot = one_hot(slot_col == cols_i.astype(F32))
    to_slot = dot_nt(one_hot(rows_i == cols_i), from_slot)
    occ = jnp.sum(to_slot, axis=1, keepdims=True)
    to_slot = to_slot.astype(BF)

    def mask_seed(n, carry):
        cols = pl.ds(pl.multiple_of(n * 1024, 1024), 1024)
        m.eg[1, :, cols] = (m.eg[1, :, cols].astype(F32) * occ).astype(BF)
        return carry

    lax.fori_loop(0, 8, mask_seed, 0)

    q, c = iotas(16, TB)
    pick_top = one_hot(c == (q >> 2) * 16 + 12 + (q & 3))
    pick_low = one_hot(c == (q >> 2) * 16 + (q & 3))

    def send_halo(i):
        for vx in range(4):
            m.hy_send[i, :, col(vx, 512)] = dot(
                pick_top, m.eg[i, :, pl.ds((vx * 16 + 12) * L, 512)]
            ).astype(BF)
        moves = (
            (m.eg.at[i, pl.ds(48, 16), pl.ds(48 * L, 16 * L)], m.hx.at[i], near(1, 0)),
            (m.hy_send.at[i], m.hy.at[i], near(0, 1)),
            (m.eg.at[i, pl.ds(48, 16), pl.ds(60 * L, 4 * L)], m.hc.at[i], near(1, 1)),
        )
        return [
            send(src, dst, m.halo_send.at[3 * i + n], m.halo_recv.at[3 * i + n], device)
            for n, (src, dst, device) in enumerate(moves)
        ]

    seed_halo = send_halo(1)

    loads[2].wait()
    loads[3].wait()
    m.wup[...] = jnp.zeros((C2, NL), BF)
    for k in range(27):
        m.wdp[pl.ds(k * L, C), :] = m.wd_v[k]
        m.wdp[pl.ds(k * L + C, L - C), :] = jnp.zeros((L - C, C2), BF)
        m.wup[:, pl.ds(k * L, C)] = m.wu_v[k]
    m.wdp[pl.ds(27 * L, L), :] = jnp.zeros((L, C2), BF)
    for i in range(2):
        m.pm[i, :, pl.ds(27 * L, L)] = jnp.zeros((8 * TB, L), BF)
    for t in range(3):
        m.mine[t, :, pl.ds(NC, NP - NC)] = jnp.zeros((16, NP - NC), F32)
        m.bb[t, :, pl.ds(NC, NP - NC)] = jnp.zeros((16, NP - NC), BF)

    def brick_in(d):
        for rank in range(2):
            body = m.recv_b[d, pl.ds(rank * ROWS, ROWS), :].astype(F32)
            base = (2 * d + rank) * VOX
            m.scr[pl.ds(base, ROWS), :] = body
            tail = [pltpu.roll(body[p * 16 : (p + 1) * 16], 32 * (p + 1), 1) for p in range(3)]
            m.scr[pl.ds(base + ROWS, 16), :] = jnp.where(
                lane < 32,
                tail[0],
                jnp.where(lane < 64, tail[1], jnp.where(lane < 96, tail[2], 0.0)),
            )

    brick_in(0)
    for e in FAR_FIRST:
        await_bytes(m.recv_b.at[e], m.a2a_recv.at[e])
        brick_in(e)

    def place_bricks(g):
        blocks = []
        for vz in range(4):
            v = g * 4 + vz
            ranks = [m.scr[pl.ds(rank * VOX + v, NY_DEV, stride=2 * VOX), :] for rank in range(2)]
            blocks.append(jnp.concatenate(ranks, axis=0).astype(BF))
        m.eg[0, :, col(g, 512)] = dot(to_slot, jnp.concatenate(blocks, axis=1)).astype(BF)

    rim = [g for g in range(16) if g // 4 == 3 or g % 4 == 3]
    for g in rim:
        place_bricks(g)
    brick_halo = send_halo(0)
    for g in range(16):
        if g not in rim:
            place_bricks(g)

    rw, cw = iotas(TB, 80)
    by = (rw >> 2) & 3
    shift_y = one_hot(
        ((cw < TB) & (by > 0) & (cw == rw - 4))
        | ((by == 0) & (s > 0) & (cw == TB + (rw >> 4) * 4 + (rw & 3)))
    )
    rw, cw = iotas(TB, 96)
    by = (rw >> 2) & 3
    bx = rw >> 4
    shift_xy = one_hot(
        ((cw < TB) & (by > 0) & (cw == rw - 4))
        | ((by == 0) & (s > 0) & (bx > 0) & (cw == TB + (bx - 1) * 4 + (rw & 3)))
        | ((by == 0) & (s > 0) & (bx == 0) & (a > 0) & (cw == 80 + 12 + (rw & 3)))
    )
    shift_z = one_hot(((rows_i & 3) > 0) & (cols_i == rows_i - 1))

    def rims(i):
        hx = m.hx[i]
        m.ex[i, pl.ds(0, 16), :] = jnp.where(a > 0, hx, jnp.zeros_like(hx))
        m.ex[i, pl.ds(16, 48), :] = m.eg[i, pl.ds(0, 48), pl.ds(48 * L, 16 * L)]
        rows = jnp.concatenate(
            [m.ex[i, :, pl.ds(12 * L, 512)], m.hy[i, :, pl.ds(3 * 512, 512)], m.hc[i]], axis=0
        )
        m.ey[i, :, pl.ds(0, 512)] = dot(shift_xy, rows).astype(BF)
        for vx in range(4):
            rows = jnp.concatenate(
                [m.eg[i, :, pl.ds((vx * 16 + 12) * L, 512)], m.hy[i, :, pl.ds(vx * 512, 512)]],
                axis=0,
            )
            m.ey[i, :, pl.ds((vx + 1) * 512, 512)] = dot(shift_y, rows).astype(BF)

    def patches(i, early):
        def block(vx, vy, vz):
            if vz < 0:
                return m.ez[i, :, col((vx + 1) * 5 + vy + 1)]
            if vy < 0:
                return m.ey[i, :, col((vx + 1) * 4 + vz)]
            if vx < 0:
                return m.ex[i, :, col(vy * 4 + vz)]
            return m.eg[i, :, col(vx * 16 + vy * 4 + vz)]

        def shifted(places):
            cols = jnp.concatenate([block(vx, vy, 3) for vx, vy in places], axis=1)
            values = dot(shift_z, cols).astype(BF)
            for n, (vx, vy) in enumerate(places):
                m.ez[i, :, col((vx + 1) * 5 + vy + 1)] = values[:, n * L : (n + 1) * L]

        if early:
            for vx in range(4):
                shifted([(vx, vy) for vy in range(4)])
        else:
            rims(i)
            shifted([(-1, vy) for vy in range(-1, 4)])
            shifted([(vx, -1) for vx in range(4)])
        for u in range(8):
            ux, uy, uz = u // 4, u // 2 % 2, u % 2
            for k in range(27):
                vx, vy, vz = 2 * ux + k // 9 - 1, 2 * uy + k // 3 % 3 - 1, 2 * uz + k % 3 - 1
                if (vx >= 0 and vy >= 0) == early:
                    m.pm[i, pl.ds(u * TB, TB), col(k)] = block(vx, vy, vz)

    def forward(first, count):
        return dot(m.pm[0, :, col(first, L, count)], m.wdp[col(first, L, count), :])

    patches(1, True)
    for copy in seed_halo:
        copy.wait()
    patches(1, False)
    m.back[...] = dot_nt(m.pm[1], m.wup[...])
    patches(0, True)
    m.before[...] = forward(12, 6) + forward(21, 7)
    for copy in brick_halo:
        copy.wait()
    patches(0, False)
    m.before[...] += forward(0, 12) + forward(18, 3)

    def gate(u, carry):
        rows = pl.ds(pl.multiple_of(u * TB, TB), TB)
        v = m.before[rows, :]
        g = jax.nn.sigmoid(v)
        m.cc[0, u] = (v * g * occ).astype(BF)
        m.cc[1, u] = (m.back[rows, :] * (g * (1.0 + v * (1.0 - g))) * occ).astype(BF)
        return carry

    lax.fori_loop(0, 8, gate, 0)

    for i in range(2):
        for u in range(4):
            m.chy_send[i, u] = dot(pick_low, m.cc[i, (u // 2) * 4 + u % 2]).astype(BF)
    coarse_halo = [
        send(
            m.cc.at[:, pl.ds(0, 4), pl.ds(0, 16)],
            m.chx,
            m.halo_send.at[6],
            m.halo_recv.at[6],
            near(-1, 0),
        ),
        send(m.chy_send, m.chy, m.halo_send.at[7], m.halo_recv.at[7], near(0, -1)),
        send(
            m.cc.at[:, pl.ds(0, 2), pl.ds(0, 16)],
            m.chc,
            m.halo_send.at[8],
            m.halo_recv.at[8],
            near(-1, -1),
        ),
    ]

    ident = one_hot(jnp.equal(*iotas(C2, C2)))

    wide = lax.broadcasted_iota(I32, (C2, L), 1)

    def tile_grad(i, out, after):
        turned = dot_nt(ident, m.cc[i].reshape(8 * TB, C2)).astype(BF)
        for g in range(7):
            values = dot(turned, m.pm[1 - i, :, pl.ds(g * 512, 512)])
            for p in range(3):
                block = values[:, p * L : (p + 1) * L]
                if g < 6:
                    spare = pltpu.roll(values[:, 3 * L :], C - 32 * p, 1)
                    block = jnp.where(wide < C, block, spare)
                out[:, col(g * 3 + p)] = block.astype(out.dtype)
            after(g)

    core_copies = []

    def to_sibling(g):
        cols = pl.ds(g * 3 * L, 3 * L)
        core_copies.append(
            send(
                m.sb.at[:, cols],
                m.r0.at[:, cols],
                m.core_send.at[g],
                m.core_recv.at[g],
                sibling,
            )
        )

    tile_grad(1 - core, m.sb, to_sibling)
    tile_grad(core, m.part, lambda g: None)

    axis_copies = []

    def to_axis(stage, t, axis, src, dst):
        copies = []
        for d in (2, 1, 3):
            i = lax.rem(pos[axis] + d, 4)
            copies.append(
                send(
                    src(i),
                    dst(d),
                    m.ax_send.at[stage, t, d - 1],
                    m.ax_recv.at[stage, t, d - 1],
                    along(axis, i),
                )
            )
        axis_copies.extend(copies)
        return copies

    def rows_of(t, i):
        return pl.ds(pl.multiple_of(t * 64 + i * 16, 16), 16)

    def cols_of(j):
        return pl.ds(pl.multiple_of(j * PART, L), PART)

    stage_a, stage_b, stage_c, stage_d, stage_e = [], [], [], [], []

    def run_a():
        for g in range(7):
            core_copies[g].wait_recv()
        for t in range(3):
            rows = pl.ds(t * 64, 64)
            m.part[rows, :] = m.part[rows, :] + m.r0[rows, :].astype(F32)
            m.ab[rows, :] = m.part[rows, :].astype(BF)
            stage_a.append(
                to_axis(
                    0,
                    t,
                    ORDERS[t][0],
                    lambda i: m.ab.at[rows_of(t, i)],
                    lambda d: m.ar.at[t, d - 1],
                )
            )

    def run_b():
        for t in range(3):
            for copy in stage_a[t]:
                copy.wait_recv()
            mine = m.part[rows_of(t, pos[ORDERS[t][0]]), :]
            for d in range(3):
                mine = mine + m.ar[t, d].astype(F32)
            m.mine[t, :, pl.ds(0, NC)] = mine
            m.bb[t, :, pl.ds(0, NC)] = mine.astype(BF)
            stage_b.append(
                to_axis(
                    1,
                    t,
                    ORDERS[t][1],
                    lambda j: m.bb.at[t, :, cols_of(j)],
                    lambda d: m.br.at[t, d - 1],
                )
            )

    def run_c():
        for t in range(3):
            first, second, third = ORDERS[t]
            for copy in stage_b[t]:
                copy.wait_recv()
            mine = m.mine[t, :, cols_of(pos[second])]
            for d in range(3):
                mine = mine + m.br[t, d].astype(F32)
            m.cr[t, pos[third]] = mine.astype(BF)
            stage_c.append(
                to_axis(
                    2,
                    t,
                    third,
                    lambda i: m.cr.at[t, pos[third]],
                    lambda d: m.cr.at[t, pos[third]],
                )
            )

    def run_d():
        for t in range(3):
            first, second, third = ORDERS[t]
            for d in range(1, 4):
                await_bytes(
                    m.cr.at[t, lax.rem(pos[third] + 4 - d, 4)], m.ax_recv.at[2, t, d - 1]
                )
            whole = m.cr[t, 0].astype(F32)
            for d in range(1, 4):
                whole = whole + m.cr[t, d].astype(F32)
            here = m.total.at[core, rows_of(t, pos[first]), cols_of(pos[second])]
            here[...] = whole.astype(BF)
            stage_d.append(to_axis(3, t, second, lambda j: here, lambda d: here))

    def strip(c, t, i):
        return m.total.at[c, rows_of(t, i), pl.ds(0, NC)]

    def hand_over(t, n, i):
        here = strip(core, t, i)
        core_copies.append(
            send(here, here, m.hand_send.at[t, n], m.hand_recv.at[t, n], sibling)
        )

    def run_e():
        for t in range(3):
            first, second, third = ORDERS[t]
            for d in range(1, 4):
                j = lax.rem(pos[second] + 4 - d, 4)
                await_bytes(
                    m.total.at[core, rows_of(t, pos[first]), cols_of(j)],
                    m.ax_recv.at[3, t, d - 1],
                )
            here = strip(core, t, pos[first])
            stage_e.append(to_axis(4, t, first, lambda j: here, lambda d: here))
            hand_over(t, 0, pos[first])

    def run_f():
        for d in (1, 3, 2):
            for t in range(3):
                i = lax.rem(pos[ORDERS[t][0]] + 4 - d, 4)
                await_bytes(strip(core, t, i), m.ax_recv.at[4, t, d - 1])
                hand_over(t, d, i)

    rw, cw = iotas(TB, 80)
    by = (rw >> 2) & 3
    lift_y = one_hot(
        ((cw < TB) & (by < 3) & (cw == rw + 4))
        | ((by == 3) & (s < NY_DEV - 1) & (cw == TB + (rw >> 4) * 4 + (rw & 3)))
    )
    rw, cw = iotas(TB, 96)
    by = (rw >> 2) & 3
    bx = rw >> 4
    lift_xy = one_hot(
        ((cw < TB) & (by < 3) & (cw == rw + 4))
        | ((by == 3) & (s < NY_DEV - 1) & (bx < 3) & (cw == TB + (bx + 1) * 4 + (rw & 3)))
        | (
            (by == 3)
            & (s < NY_DEV - 1)
            & (bx == 3)
            & (a < NX_DEV - 1)
            & (cw == 80 + (rw & 3))
        )
    )
    lift_z = one_hot(((rows_i & 3) < 3) & (cols_i == rows_i + 1))

    def at(ux, uy, uz):
        return ux * 9 + uy * 3 + uz

    def extend(i):
        for u in range(8):
            m.ce[i, at(u // 4, u // 2 % 2, u % 2)] = m.cc[i, u]
        for uy in range(2):
            for uz in range(2):
                h = m.chx[i, uy * 2 + uz]
                m.ce[i, at(2, uy, uz), pl.ds(0, 48), :] = m.cc[i, uy * 2 + uz, pl.ds(16, 48), :]
                m.ce[i, at(2, uy, uz), pl.ds(48, 16), :] = jnp.where(
                    a < NX_DEV - 1, h, jnp.zeros_like(h)
                )
        for uz in range(2):
            for ux in range(2):
                rows = jnp.concatenate([m.ce[i, at(ux, 0, uz)], m.chy[i, ux * 2 + uz]], axis=0)
                m.ce[i, at(ux, 2, uz)] = dot(lift_y, rows).astype(BF)
            rows = jnp.concatenate(
                [m.ce[i, at(2, 0, uz)], m.chy[i, uz], m.chc[i, uz]], axis=0
            )
            m.ce[i, at(2, 2, uz)] = dot(lift_xy, rows).astype(BF)
        for ux in range(3):
            for uy in range(3):
                m.ce[i, at(ux, uy, 2)] = dot(lift_z, m.ce[i, at(ux, uy, 0)]).astype(BF)

    terms = (((1, 0),), ((2, 0), (0, 1)))

    def transposed(i, emit, parities=range(8)):
        for p in parities:
            px, py, pz = p // 4, p // 2 % 2, p % 2
            total = None
            for kx, sx in terms[px]:
                for ky, sy in terms[py]:
                    for kz, sz in terms[pz]:
                        rows = jnp.concatenate(
                            [
                                m.ce[i, at(u // 4 + sx, u // 2 % 2 + sy, u % 2 + sz)]
                                for u in range(8)
                            ],
                            axis=0,
                        )
                        k = kx * 9 + ky * 3 + kz
                        if i == 0:
                            term = dot(rows, m.wup[:, col(k)])
                        else:
                            term = dot_nt(rows, m.wdp[col(k), :])
                        total = term if total is None else total + term
            for u in range(8):
                vx, vy, vz = 2 * (u // 4) + px, 2 * (u // 2 % 2) + py, 2 * (u % 2) + pz
                emit(vx, vy, vz, total[u * TB : (u + 1) * TB])

    def emit_result(vx, vy, vz, value):
        value = (m.eg[0, :, col(vx * 16 + vy * 4 + vz)].astype(F32) + value) * occ
        m.scr[pl.ds((vx * 4 + vy) * 256 + vz, TB, stride=4), :] = value

    def emit_grad(vx, vy, vz, value):
        cols = col(vx * 16 + vy * 4 + vz)
        m.fb[:, cols] = (m.eg[1, :, cols].astype(F32) + value).astype(BF)

    run_a()
    for copy in coarse_halo:
        copy.wait()
    extend(1)
    transposed(1, emit_grad)

    def gather(n, carry):
        cols = pl.ds(pl.multiple_of(n * 512, 512), 512)
        values = dot(from_slot, m.fb[:, cols])
        for b in range(4):
            for rank in range(2):
                rows = pl.ds(rank * VOX + n * 4 + b, NY_DEV, stride=2 * VOX)
                m.scr2[rows, :] = values[
                    rank * NY_DEV : (rank + 1) * NY_DEV, b * L : (b + 1) * L
                ]
        return carry

    def reply(d, carry):
        for rank in range(2):
            base = pl.multiple_of((2 * d + rank) * VOX, VOX)
            tail = m.scr2[pl.ds(base + ROWS, 16), :]
            for p in range(3):
                body = m.scr2[pl.ds(base + p * 16, 16), :]
                m.rep[d, pl.ds(rank * ROWS + p * 16, 16), :] = jnp.where(
                    lane < C, body, pltpu.roll(tail, C - 32 * p, 1)
                ).astype(BF)
        return carry

    def send_back(part):
        for e in FAR_FIRST[(0, 6, 14)[part] : (6, 14, NY_DEV - 1)[part]]:
            send(m.rep.at[e], m.ret.at[e], m.back_send.at[0], m.back_recv.at[0], offset(e, -1))

    lax.fori_loop(0, 16, gather, 0, unroll=8)
    run_b()
    lax.fori_loop(0, NY_DEV, reply, 0, unroll=8)
    send_back(0)
    m.ret[0] = m.rep[0]
    extend(0)
    run_c()
    send_back(1)
    transposed(0, emit_result, range(0, 6))
    run_d()
    send_back(2)
    transposed(0, emit_result, range(6, 8))
    run_e()

    def result_out(g, carry):
        vx, vy = g // 4, lax.rem(g, 4)
        for b in range(16):
            x, y = 4 * (b // 4) + vx, 4 * (b % 4) + vy
            rows = pl.ds(pl.multiple_of(g * 256 + b * 16, 16), 16)
            m.res_v[x * 16 + y] = m.scr[rows, :][:, :C].astype(BF)
        return carry

    lax.fori_loop(0, 16, result_out, 0)
    run_f()
    await_bytes(m.ret.at[pl.ds(1, NY_DEV - 1)], m.back_recv.at[0])
    for t in range(3):
        for d in range(4):
            i = lax.rem(pos[ORDERS[t][0]] + 4 - d, 4)
            await_bytes(strip(1 - core, t, i), m.hand_recv.at[t, d])
    await_bytes(m.tag_r.at[pl.ds(1, NY_DEV - 1)], m.tag_send.at[0])
    await_bytes(m.out_b.at[pl.ds(1, NY_DEV - 1)], m.a2a_send.at[0])
    await_bytes(m.rep.at[pl.ds(1, NY_DEV - 1)], m.back_send.at[0])
    for copy in core_copies + axis_copies:
        copy.wait_send()


def main_call(owner, slot, bricks, cot, wd, wu):
    vmem = pl.BlockSpec(memory_space=pltpu.VMEM)
    hbm = pl.BlockSpec(memory_space=pl.ANY)
    scratch = [pltpu.VMEM(shape, dtype) for shape, dtype in SCRATCH.values()]
    scratch += [pltpu.SemaphoreType.DMA(shape) for shape in SEMS.values()]
    scratch += [pltpu.SMEM((1, L), I32)]
    return pl.pallas_call(
        main_kernel,
        out_shape=(
            pltpu.VMEM((256, 16, C), BF),
            pltpu.VMEM((NY_DEV, PAIR, L), BF),
            pltpu.VMEM((2, C2, NP), BF),
            pltpu.VMEM((1, L), I32),
        ),
        in_specs=[vmem, vmem, hbm, hbm, hbm, hbm],
        out_specs=[vmem] * 4,
        scratch_shapes=scratch,
        compiler_params=pltpu.CompilerParams(
            collective_id=0, has_side_effects=True, vmem_limit_bytes=50 * 2**20
        ),
    )(owner, slot, bricks, cot, wd, wu)


def final_kernel(
    target, ret, grads, early, brick_grads, down, up, result, target_s, bg_v, down_v, up_v, sems
):
    pass_on = pltpu.make_async_copy(early, result, sems.at[0])
    pass_on.start()
    get_target = pltpu.make_async_copy(target, target_s, sems.at[8])
    get_target.start()
    lane = lax.broadcasted_iota(I32, (16, L), 1)
    ident = one_hot(jnp.equal(*iotas(C, L)))
    puts = []
    rs, cs = iotas(C, 3 * L)
    spread = one_hot(((cs & (L - 1)) >= C) & (rs == (cs >> 7) * 32 + (cs & (L - 1)) - C))
    rs, cs = iotas(3 * L, C)
    gather = one_hot(((rs & (L - 1)) >= C) & (cs == (rs >> 7) * 32 + (rs & (L - 1)) - C))
    for k in range(27):
        group, p = k // 4, k % 4
        if p < 3:
            cols = pl.ds((group * 3 + p) * L, L)
            up_v[k] = grads[0, :, cols][:, :C].astype(F32)
            down_v[k] = dot_nt(ident, grads[1, :, cols])
        else:
            cols = pl.ds(group * 3 * L, 3 * L)
            up_v[k] = dot(grads[0, :, cols], gather)
            down_v[k] = dot_nt(spread, grads[1, :, cols])
        if k % 9 == 8:
            part = pl.ds(k - 8, 9)
            puts.append(pltpu.make_async_copy(up_v.at[part], up.at[part], sems.at[2 + k // 9]))
            puts.append(pltpu.make_async_copy(down_v.at[part], down.at[part], sems.at[5 + k // 9]))
            puts[-2].start()
            puts[-1].start()

    get_target.wait()

    def take(j, carry):
        body = ret[target_s[0, j]]
        bg_v[j, pl.ds(0, ROWS), :] = body[:, :C]
        tail = [
            pltpu.roll(body[p * 16 : (p + 1) * 16].astype(F32), 32 * (p + 1), 1) for p in range(3)
        ]
        tail = jnp.where(lane < 32, tail[0], jnp.where(lane < 64, tail[1], tail[2]))
        bg_v[j, pl.ds(ROWS, 16), :] = tail[:, :C].astype(BF)
        return carry

    lax.fori_loop(0, ENTRIES, take, 0, unroll=8)
    puts.append(pltpu.make_async_copy(bg_v, brick_grads, sems.at[1]))
    puts[-1].start()
    pass_on.wait()
    for put in puts:
        put.wait()


def final_call(target, ret, grads, early):
    vmem = pl.BlockSpec(memory_space=pltpu.VMEM)
    hbm = pl.BlockSpec(memory_space=pl.ANY)
    return pl.pallas_call(
        final_kernel,
        out_shape=(
            jax.ShapeDtypeStruct((ENTRIES, VOX, C), BF),
            jax.ShapeDtypeStruct((27, C, C2), F32),
            jax.ShapeDtypeStruct((27, C2, C), F32),
            jax.ShapeDtypeStruct((256, 16, C), BF),
        ),
        in_specs=[vmem] * 4,
        out_specs=[hbm] * 4,
        scratch_shapes=[
            pltpu.SMEM((1, L), I32),
            pltpu.VMEM((ENTRIES, VOX, C), BF),
            pltpu.VMEM((27, C, C2), F32),
            pltpu.VMEM((27, C2, C), F32),
            pltpu.SemaphoreType.DMA((9,)),
        ],
        compiler_params=pltpu.CompilerParams(vmem_limit_bytes=20 * 2**20),
    )(target, ret, grads, early)


def on_device(bricks, brick_owner, brick_slot, down_weight, up_weight, cotangent):
    early, ret, grads, target = main_call(
        brick_owner.reshape(1, ENTRIES),
        brick_slot.reshape(1, ENTRIES),
        bricks.reshape(ENTRIES, VOX, C),
        cotangent.reshape(256, 16, C),
        down_weight,
        up_weight,
    )
    brick_grads, down, up, result = final_call(target, ret.reshape(TB, ROWS, L), grads, early)
    return (
        result.reshape(16, 16, 16, C),
        brick_grads.reshape(1, 1, ENTRIES, VOX, C),
        down,
        up,
    )


def solution(mesh):
    placed = (
        P("gx", "gy", None, None, None),
        P("gx", "gy", None),
        P("gx", "gy", None),
        P(),
        P(),
        P("gx", "gy", None, None),
    )
    return jax.shard_map(
        on_device,
        mesh=mesh,
        in_specs=placed,
        out_specs=(P("gx", "gy", None, None), P("gx", "gy", None, None, None), P(), P()),
        check_vma=False,
    )
```

```python
import jax
import jax.numpy as jnp
from jax import lax
from jax.experimental import pallas as pl
from jax.experimental.pallas import tpu as pltpu
from jax.sharding import PartitionSpec as P

C = 96
C2 = 192
L = 128
TB = 64
VOX = 64
ENTRIES = 56
NY_DEV = 32
NX_DEV = 4
NL = 28 * L
NC = 21 * L
NP = 24 * L
PART = NP // 4
ROWS = VOX * C // L
PAIR = 2 * ROWS

BF = jnp.bfloat16
F32 = jnp.float32
I32 = jnp.int32
MESH = pl.DeviceIdType.MESH
ORDERS = (("x", "y", "z"), ("y", "z", "x"), ("z", "x", "y"))
FAR_FIRST = sorted(
    range(1, NY_DEV), key=lambda e: -(min(e // 8, 4 - e // 8) + min(e // 2 % 4, 4 - e // 2 % 4))
)
NT = (((1,), (1,)), ((), ()))


def dot(a, b):
    return jnp.dot(a, b, preferred_element_type=F32)


def dot_nt(a, b):
    return lax.dot_general(a, b, NT, preferred_element_type=F32)


def iotas(rows, cols):
    return (
        lax.broadcasted_iota(I32, (rows, cols), 0),
        lax.broadcasted_iota(I32, (rows, cols), 1),
    )


def one_hot(hit):
    return jnp.where(hit, 1.0, 0.0).astype(BF)


def col(block, width=L, count=1):
    return pl.ds(block * width, count * width)


SCRATCH = dict(
    bricks_v=((ENTRIES, VOX, C), BF),
    cot_v=((256, 16, C), BF),
    wd_v=((27, C, C2), BF),
    wu_v=((27, C2, C), BF),
    out_b=((NY_DEV, PAIR, L), BF),
    recv_b=((NY_DEV, PAIR, L), BF),
    entry_v=((1, L), I32),
    tag_v=((1, L), I32),
    tag_r=((NY_DEV, 1, L), I32),
    scr=((TB * VOX, L), F32),
    scr2=((TB * VOX, L), F32),
    eg=((2, TB, VOX * L), BF),
    ex=((2, TB, 16 * L), BF),
    ey=((2, TB, 20 * L), BF),
    ez=((2, TB, 25 * L), BF),
    hx=((2, 16, 16 * L), BF),
    hy=((2, 16, 16 * L), BF),
    hc=((2, 16, 4 * L), BF),
    hy_send=((2, 16, 16 * L), BF),
    pm=((2, 8 * TB, NL), BF),
    wdp=((NL, C2), BF),
    wup=((C2, NL), BF),
    before=((8 * TB, C2), F32),
    back=((8 * TB, C2), F32),
    cc=((2, 8, TB, C2), BF),
    ce=((2, 27, TB, C2), BF),
    chx=((2, 4, 16, C2), BF),
    chy=((2, 4, 16, C2), BF),
    chc=((2, 2, 16, C2), BF),
    chy_send=((2, 4, 16, C2), BF),
    part=((C2, NC), F32),
    sb=((C2, NC), BF),
    r0=((C2, NC), BF),
    ab=((C2, NC), BF),
    ar=((3, 3, 16, NC), BF),
    mine=((3, 16, NP), F32),
    bb=((3, 16, NP), BF),
    br=((3, 3, 16, PART), BF),
    cr=((3, 4, 16, PART), BF),
    fb=((TB, VOX * L), BF),
    rep=((NY_DEV, PAIR, L), BF),
)
SEMS = dict(
    load=(4,),
    route=(1,),
    tag_send=(1,),
    tag_recv=(1,),
    a2a_send=(1,),
    a2a_recv=(NY_DEV,),
    halo_send=(9,),
    halo_recv=(9,),
    back_send=(1,),
    back_recv=(1,),
    core_send=(7,),
    core_recv=(7,),
    hand_send=(3, 4),
    hand_recv=(3, 4),
    ax_send=(5, 3, 3),
    ax_recv=(5, 3, 3),
)


def main_kernel(owner, slot, bricks, cot, wd, wu, result, ret_out, grads, target, *scratch):
    r = dict(zip(list(SCRATCH) + list(SEMS) + ["entry_s"], scratch))

    class R:
        pass

    m = R()
    m.__dict__.update(r)
    m.res_v, m.ret, m.total = result, ret_out, grads

    a = lax.axis_index("gx")
    s = lax.axis_index("gy")
    core = lax.rem(s, 2)
    zpos = lax.rem(s // 2, 4)
    ypos = s // 8
    pos = dict(x=a, y=ypos, z=zpos)

    def along(axis, i):
        if axis == "x":
            return (i, s)
        if axis == "y":
            return (a, (i * 4 + zpos) * 2 + core)
        return (a, (ypos * 4 + i) * 2 + core)

    def near(dx, dy):
        return (lax.rem(a + dx + NX_DEV, NX_DEV), lax.rem(s + dy + NY_DEV, NY_DEV))

    def offset(e, sign):
        y = lax.rem(ypos + sign * (e // 8) + 4, 4)
        z = lax.rem(zpos + sign * (e // 2 % 4) + 4, 4)
        return (a, (y * 4 + z) * 2 + lax.rem(core + e % 2, 2))

    sibling = (a, s + 1 - 2 * core)

    def send(src, dst, send_sem, recv_sem, device):
        copy = pltpu.make_async_remote_copy(
            src_ref=src,
            dst_ref=dst,
            send_sem=send_sem,
            recv_sem=recv_sem,
            device_id=device,
            device_id_type=MESH,
        )
        copy.start()
        return copy

    def await_bytes(ref, sem):
        pltpu.make_async_copy(ref, ref, sem).wait()

    loads = [
        pltpu.make_async_copy(src, dst, m.load.at[i])
        for i, (src, dst) in enumerate(
            ((bricks, m.bricks_v), (cot, m.cot_v), (wd, m.wd_v), (wu, m.wu_v))
        )
    ]
    for load in loads:
        load.start()

    barrier = pltpu.get_barrier_semaphore()

    def greet(d, carry):
        pl.semaphore_signal(barrier, inc=1, device_id=near(0, d), device_id_type=MESH)
        return carry

    lax.fori_loop(1, NY_DEV, greet, 0)
    for d in range(1, NX_DEV):
        pl.semaphore_signal(barrier, inc=1, device_id=near(d, 0), device_id_type=MESH)
    pl.semaphore_signal(barrier, inc=1, device_id=near(1, 1), device_id_type=MESH)
    pl.semaphore_signal(barrier, inc=1, device_id=near(-1, -1), device_id_type=MESH)

    rj, cj = iotas(ENTRIES, ENTRIES)
    own = owner[...]
    far = (
        (((own >> 3) - ypos) & 3) * 8 + ((((own >> 1) & 3) - zpos) & 3) * 2 + ((own - core) & 1)
    )
    far = jnp.broadcast_to(far, (ENTRIES, ENTRIES))

    def turn(rows):
        return jnp.sum(jnp.where(rj == cj, rows, 0), axis=1, keepdims=True)

    far_col = turn(far)
    rank = jnp.sum(jnp.where((far_col == far) & (rj < cj), 1, 0), axis=0, keepdims=True)
    goes = jnp.broadcast_to(2 * far[:1] + rank, (ENTRIES, ENTRIES))
    goes_col = turn(goes)
    slot_of = turn(jnp.broadcast_to(slot[...], (ENTRIES, ENTRIES)))
    rt, ct = iotas(ENTRIES, L)
    hit = goes_col == ct
    m.entry_v[...] = jnp.sum(jnp.where(hit, rt, 0), axis=0, keepdims=True)
    m.tag_v[...] = jnp.sum(jnp.where(hit, slot_of + 1, 0), axis=0, keepdims=True) - 1
    target[...] = jnp.zeros((1, L), I32)
    target[:, pl.ds(0, ENTRIES)] = goes[:1]
    route = pltpu.make_async_copy(m.entry_v, m.entry_s, m.route.at[0])
    route.start()
    route.wait()

    lane = lax.broadcasted_iota(I32, (16, L), 1)
    loads[0].wait()

    def pack(d, carry):
        for rank in range(2):
            brick = m.bricks_v[m.entry_s[0, 2 * d + rank]]
            m.out_b[d, pl.ds(rank * ROWS, ROWS), pl.ds(0, C)] = brick[:ROWS]
            for p in range(3):
                m.out_b[d, pl.ds(rank * ROWS + p * 16, 16), pl.ds(C, L - C)] = brick[
                    ROWS:, p * 32 : (p + 1) * 32
                ]
        return carry

    lax.fori_loop(0, NY_DEV, pack, 0, unroll=8)
    pl.semaphore_wait(barrier, NY_DEV - 1 + NX_DEV - 1 + 2)

    for e in FAR_FIRST:
        send(m.tag_v, m.tag_r.at[e], m.tag_send.at[0], m.tag_recv.at[0], offset(e, 1))
    for e in FAR_FIRST:
        send(m.out_b.at[e], m.recv_b.at[e], m.a2a_send.at[0], m.a2a_recv.at[e], offset(e, 1))
    m.tag_r[0] = m.tag_v[...]
    m.recv_b[0] = m.out_b[0]

    m.scr[...] = jnp.zeros((TB * VOX, L), F32)
    loads[1].wait()

    def cot_in(g, carry):
        vx, vy = g // 4, lax.rem(g, 4)
        for b in range(16):
            x, y = 4 * (b // 4) + vx, 4 * (b % 4) + vy
            rows = pl.ds(pl.multiple_of(g * 256 + b * 16, 16), 16)
            m.scr[rows, pl.ds(0, C)] = m.cot_v[x * 16 + y].astype(F32)
        return carry

    lax.fori_loop(0, 16, cot_in, 0)

    def cot_out(g, carry):
        for vz in range(4):
            rows = pl.ds(g * 256 + vz, TB, stride=4)
            cols = pl.ds(pl.multiple_of((g * 4 + vz) * L, L), L)
            m.eg[1, :, cols] = m.scr[rows, :].astype(BF)
        return carry

    lax.fori_loop(0, 16, cot_out, 0)

    loads[2].wait()
    loads[3].wait()
    m.wup[...] = jnp.zeros((C2, NL), BF)
    for k in range(27):
        m.wdp[pl.ds(k * L, C), :] = m.wd_v[k]
        m.wdp[pl.ds(k * L + C, L - C), :] = jnp.zeros((L - C, C2), BF)
        m.wup[:, pl.ds(k * L, C)] = m.wu_v[k]
    m.wdp[pl.ds(27 * L, L), :] = jnp.zeros((L, C2), BF)
    for i in range(2):
        m.pm[i, :, pl.ds(27 * L, L)] = jnp.zeros((8 * TB, L), BF)
    for t in range(3):
        m.mine[t, :, pl.ds(NC, NP - NC)] = jnp.zeros((16, NP - NC), F32)
        m.bb[t, :, pl.ds(NC, NP - NC)] = jnp.zeros((16, NP - NC), BF)

    rows_i, cols_i = iotas(TB, TB)
    await_bytes(m.tag_r.at[pl.ds(1, NY_DEV - 1)], m.tag_recv.at[0])
    rg, cg = iotas(NY_DEV, L)
    tags = m.tag_r[...].reshape(NY_DEV, L).astype(F32)
    slot_col = jnp.concatenate(
        [
            jnp.sum(jnp.where(cg == 2 * rg + rank, tags, 0.0), axis=1, keepdims=True)
            for rank in range(2)
        ],
        axis=0,
    )
    from_slot = one_hot(slot_col == cols_i.astype(F32))
    to_slot = dot_nt(one_hot(rows_i == cols_i), from_slot)
    occ = jnp.sum(to_slot, axis=1, keepdims=True)
    to_slot = to_slot.astype(BF)

    def mask_seed(n, carry):
        cols = pl.ds(pl.multiple_of(n * 1024, 1024), 1024)
        m.eg[1, :, cols] = (m.eg[1, :, cols].astype(F32) * occ).astype(BF)
        return carry

    lax.fori_loop(0, 8, mask_seed, 0)

    q, c = iotas(16, TB)
    pick_top = one_hot(c == (q >> 2) * 16 + 12 + (q & 3))
    pick_low = one_hot(c == (q >> 2) * 16 + (q & 3))

    def send_halo(i):
        for vx in range(4):
            m.hy_send[i, :, col(vx, 512)] = dot(
                pick_top, m.eg[i, :, pl.ds((vx * 16 + 12) * L, 512)]
            ).astype(BF)
        moves = (
            (m.eg.at[i, pl.ds(48, 16), pl.ds(48 * L, 16 * L)], m.hx.at[i], near(1, 0)),
            (m.hy_send.at[i], m.hy.at[i], near(0, 1)),
            (m.eg.at[i, pl.ds(48, 16), pl.ds(60 * L, 4 * L)], m.hc.at[i], near(1, 1)),
        )
        return [
            send(src, dst, m.halo_send.at[3 * i + n], m.halo_recv.at[3 * i + n], device)
            for n, (src, dst, device) in enumerate(moves)
        ]

    seed_halo = send_halo(1)

    def brick_in(d):
        for rank in range(2):
            body = m.recv_b[d, pl.ds(rank * ROWS, ROWS), :].astype(F32)
            base = (2 * d + rank) * VOX
            m.scr[pl.ds(base, ROWS), :] = body
            tail = [pltpu.roll(body[p * 16 : (p + 1) * 16], 32 * (p + 1), 1) for p in range(3)]
            m.scr[pl.ds(base + ROWS, 16), :] = jnp.where(
                lane < 32,
                tail[0],
                jnp.where(lane < 64, tail[1], jnp.where(lane < 96, tail[2], 0.0)),
            )

    brick_in(0)
    for e in FAR_FIRST:
        await_bytes(m.recv_b.at[e], m.a2a_recv.at[e])
        brick_in(e)

    def place_bricks(g):
        blocks = []
        for vz in range(4):
            v = g * 4 + vz
            ranks = [m.scr[pl.ds(rank * VOX + v, NY_DEV, stride=2 * VOX), :] for rank in range(2)]
            blocks.append(jnp.concatenate(ranks, axis=0).astype(BF))
        m.eg[0, :, col(g, 512)] = dot(to_slot, jnp.concatenate(blocks, axis=1)).astype(BF)

    rim = [g for g in range(16) if g // 4 == 3 or g % 4 == 3]
    for g in rim:
        place_bricks(g)
    brick_halo = send_halo(0)
    for g in range(16):
        if g not in rim:
            place_bricks(g)

    rw, cw = iotas(TB, 80)
    by = (rw >> 2) & 3
    shift_y = one_hot(
        ((cw < TB) & (by > 0) & (cw == rw - 4))
        | ((by == 0) & (s > 0) & (cw == TB + (rw >> 4) * 4 + (rw & 3)))
    )
    rw, cw = iotas(TB, 96)
    by = (rw >> 2) & 3
    bx = rw >> 4
    shift_xy = one_hot(
        ((cw < TB) & (by > 0) & (cw == rw - 4))
        | ((by == 0) & (s > 0) & (bx > 0) & (cw == TB + (bx - 1) * 4 + (rw & 3)))
        | ((by == 0) & (s > 0) & (bx == 0) & (a > 0) & (cw == 80 + 12 + (rw & 3)))
    )
    shift_z = one_hot(((rows_i & 3) > 0) & (cols_i == rows_i - 1))

    def rims(i):
        hx = m.hx[i]
        m.ex[i, pl.ds(0, 16), :] = jnp.where(a > 0, hx, jnp.zeros_like(hx))
        m.ex[i, pl.ds(16, 48), :] = m.eg[i, pl.ds(0, 48), pl.ds(48 * L, 16 * L)]
        rows = jnp.concatenate(
            [m.ex[i, :, pl.ds(12 * L, 512)], m.hy[i, :, pl.ds(3 * 512, 512)], m.hc[i]], axis=0
        )
        m.ey[i, :, pl.ds(0, 512)] = dot(shift_xy, rows).astype(BF)
        for vx in range(4):
            rows = jnp.concatenate(
                [m.eg[i, :, pl.ds((vx * 16 + 12) * L, 512)], m.hy[i, :, pl.ds(vx * 512, 512)]],
                axis=0,
            )
            m.ey[i, :, pl.ds((vx + 1) * 512, 512)] = dot(shift_y, rows).astype(BF)

    def patches(i, early):
        def block(vx, vy, vz):
            if vz < 0:
                return m.ez[i, :, col((vx + 1) * 5 + vy + 1)]
            if vy < 0:
                return m.ey[i, :, col((vx + 1) * 4 + vz)]
            if vx < 0:
                return m.ex[i, :, col(vy * 4 + vz)]
            return m.eg[i, :, col(vx * 16 + vy * 4 + vz)]

        def shifted(places):
            cols = jnp.concatenate([block(vx, vy, 3) for vx, vy in places], axis=1)
            values = dot(shift_z, cols).astype(BF)
            for n, (vx, vy) in enumerate(places):
                m.ez[i, :, col((vx + 1) * 5 + vy + 1)] = values[:, n * L : (n + 1) * L]

        if early:
            for vx in range(4):
                shifted([(vx, vy) for vy in range(4)])
        else:
            rims(i)
            shifted([(-1, vy) for vy in range(-1, 4)])
            shifted([(vx, -1) for vx in range(4)])
        for u in range(8):
            ux, uy, uz = u // 4, u // 2 % 2, u % 2
            for k in range(27):
                vx, vy, vz = 2 * ux + k // 9 - 1, 2 * uy + k // 3 % 3 - 1, 2 * uz + k % 3 - 1
                if (vx >= 0 and vy >= 0) == early:
                    m.pm[i, pl.ds(u * TB, TB), col(k)] = block(vx, vy, vz)

    def forward(first, count):
        return dot(m.pm[0, :, col(first, L, count)], m.wdp[col(first, L, count), :])

    patches(1, True)
    for copy in seed_halo:
        copy.wait()
    patches(1, False)
    m.back[...] = dot_nt(m.pm[1], m.wup[...])
    patches(0, True)
    m.before[...] = forward(12, 6) + forward(21, 7)
    for copy in brick_halo:
        copy.wait()
    patches(0, False)
    m.before[...] += forward(0, 12) + forward(18, 3)

    def gate(u, carry):
        rows = pl.ds(pl.multiple_of(u * TB, TB), TB)
        v = m.before[rows, :]
        g = jax.nn.sigmoid(v)
        m.cc[0, u] = (v * g * occ).astype(BF)
        m.cc[1, u] = (m.back[rows, :] * (g * (1.0 + v * (1.0 - g))) * occ).astype(BF)
        return carry

    lax.fori_loop(0, 8, gate, 0)

    for i in range(2):
        for u in range(4):
            m.chy_send[i, u] = dot(pick_low, m.cc[i, (u // 2) * 4 + u % 2]).astype(BF)
    coarse_halo = [
        send(
            m.cc.at[:, pl.ds(0, 4), pl.ds(0, 16)],
            m.chx,
            m.halo_send.at[6],
            m.halo_recv.at[6],
            near(-1, 0),
        ),
        send(m.chy_send, m.chy, m.halo_send.at[7], m.halo_recv.at[7], near(0, -1)),
        send(
            m.cc.at[:, pl.ds(0, 2), pl.ds(0, 16)],
            m.chc,
            m.halo_send.at[8],
            m.halo_recv.at[8],
            near(-1, -1),
        ),
    ]

    ident = one_hot(jnp.equal(*iotas(C2, C2)))

    wide = lax.broadcasted_iota(I32, (C2, L), 1)

    def tile_grad(i, out, after):
        turned = dot_nt(ident, m.cc[i].reshape(8 * TB, C2)).astype(BF)
        for g in range(7):
            values = dot(turned, m.pm[1 - i, :, pl.ds(g * 512, 512)])
            for p in range(3):
                block = values[:, p * L : (p + 1) * L]
                if g < 6:
                    spare = pltpu.roll(values[:, 3 * L :], C - 32 * p, 1)
                    block = jnp.where(wide < C, block, spare)
                out[:, col(g * 3 + p)] = block.astype(out.dtype)
            after(g)

    core_copies = []

    def to_sibling(g):
        cols = pl.ds(g * 3 * L, 3 * L)
        core_copies.append(
            send(
                m.sb.at[:, cols],
                m.r0.at[:, cols],
                m.core_send.at[g],
                m.core_recv.at[g],
                sibling,
            )
        )

    tile_grad(1 - core, m.sb, to_sibling)
    tile_grad(core, m.part, lambda g: None)

    axis_copies = []

    def to_axis(stage, t, axis, src, dst):
        copies = []
        for d in (2, 1, 3):
            i = lax.rem(pos[axis] + d, 4)
            copies.append(
                send(
                    src(i),
                    dst(d),
                    m.ax_send.at[stage, t, d - 1],
                    m.ax_recv.at[stage, t, d - 1],
                    along(axis, i),
                )
            )
        axis_copies.extend(copies)
        return copies

    def rows_of(t, i):
        return pl.ds(pl.multiple_of(t * 64 + i * 16, 16), 16)

    def cols_of(j):
        return pl.ds(pl.multiple_of(j * PART, L), PART)

    stage_a, stage_b, stage_c, stage_d, stage_e = [], [], [], [], []

    def run_a():
        for g in range(7):
            core_copies[g].wait_recv()
        for t in range(3):
            rows = pl.ds(t * 64, 64)
            m.part[rows, :] = m.part[rows, :] + m.r0[rows, :].astype(F32)
            m.ab[rows, :] = m.part[rows, :].astype(BF)
            stage_a.append(
                to_axis(
                    0,
                    t,
                    ORDERS[t][0],
                    lambda i: m.ab.at[rows_of(t, i)],
                    lambda d: m.ar.at[t, d - 1],
                )
            )

    def run_b():
        for t in range(3):
            for copy in stage_a[t]:
                copy.wait_recv()
            mine = m.part[rows_of(t, pos[ORDERS[t][0]]), :]
            for d in range(3):
                mine = mine + m.ar[t, d].astype(F32)
            m.mine[t, :, pl.ds(0, NC)] = mine
            m.bb[t, :, pl.ds(0, NC)] = mine.astype(BF)
            stage_b.append(
                to_axis(
                    1,
                    t,
                    ORDERS[t][1],
                    lambda j: m.bb.at[t, :, cols_of(j)],
                    lambda d: m.br.at[t, d - 1],
                )
            )

    def run_c():
        for t in range(3):
            first, second, third = ORDERS[t]
            for copy in stage_b[t]:
                copy.wait_recv()
            mine = m.mine[t, :, cols_of(pos[second])]
            for d in range(3):
                mine = mine + m.br[t, d].astype(F32)
            m.cr[t, pos[third]] = mine.astype(BF)
            stage_c.append(
                to_axis(
                    2,
                    t,
                    third,
                    lambda i: m.cr.at[t, pos[third]],
                    lambda d: m.cr.at[t, pos[third]],
                )
            )

    def run_d():
        for t in range(3):
            first, second, third = ORDERS[t]
            for d in range(1, 4):
                await_bytes(
                    m.cr.at[t, lax.rem(pos[third] + 4 - d, 4)], m.ax_recv.at[2, t, d - 1]
                )
            whole = m.cr[t, 0].astype(F32)
            for d in range(1, 4):
                whole = whole + m.cr[t, d].astype(F32)
            here = m.total.at[core, rows_of(t, pos[first]), cols_of(pos[second])]
            here[...] = whole.astype(BF)
            stage_d.append(to_axis(3, t, second, lambda j: here, lambda d: here))

    def strip(c, t, i):
        return m.total.at[c, rows_of(t, i), pl.ds(0, NC)]

    def hand_over(t, n, i):
        here = strip(core, t, i)
        core_copies.append(
            send(here, here, m.hand_send.at[t, n], m.hand_recv.at[t, n], sibling)
        )

    def run_e():
        for t in range(3):
            first, second, third = ORDERS[t]
            for d in range(1, 4):
                j = lax.rem(pos[second] + 4 - d, 4)
                await_bytes(
                    m.total.at[core, rows_of(t, pos[first]), cols_of(j)],
                    m.ax_recv.at[3, t, d - 1],
                )
            here = strip(core, t, pos[first])
            stage_e.append(to_axis(4, t, first, lambda j: here, lambda d: here))
            hand_over(t, 0, pos[first])

    def run_f():
        for d in (1, 3, 2):
            for t in range(3):
                i = lax.rem(pos[ORDERS[t][0]] + 4 - d, 4)
                await_bytes(strip(core, t, i), m.ax_recv.at[4, t, d - 1])
                hand_over(t, d, i)

    rw, cw = iotas(TB, 80)
    by = (rw >> 2) & 3
    lift_y = one_hot(
        ((cw < TB) & (by < 3) & (cw == rw + 4))
        | ((by == 3) & (s < NY_DEV - 1) & (cw == TB + (rw >> 4) * 4 + (rw & 3)))
    )
    rw, cw = iotas(TB, 96)
    by = (rw >> 2) & 3
    bx = rw >> 4
    lift_xy = one_hot(
        ((cw < TB) & (by < 3) & (cw == rw + 4))
        | ((by == 3) & (s < NY_DEV - 1) & (bx < 3) & (cw == TB + (bx + 1) * 4 + (rw & 3)))
        | (
            (by == 3)
            & (s < NY_DEV - 1)
            & (bx == 3)
            & (a < NX_DEV - 1)
            & (cw == 80 + (rw & 3))
        )
    )
    lift_z = one_hot(((rows_i & 3) < 3) & (cols_i == rows_i + 1))

    def at(ux, uy, uz):
        return ux * 9 + uy * 3 + uz

    def extend(i):
        for u in range(8):
            m.ce[i, at(u // 4, u // 2 % 2, u % 2)] = m.cc[i, u]
        for uy in range(2):
            for uz in range(2):
                h = m.chx[i, uy * 2 + uz]
                m.ce[i, at(2, uy, uz), pl.ds(0, 48), :] = m.cc[i, uy * 2 + uz, pl.ds(16, 48), :]
                m.ce[i, at(2, uy, uz), pl.ds(48, 16), :] = jnp.where(
                    a < NX_DEV - 1, h, jnp.zeros_like(h)
                )
        for uz in range(2):
            for ux in range(2):
                rows = jnp.concatenate([m.ce[i, at(ux, 0, uz)], m.chy[i, ux * 2 + uz]], axis=0)
                m.ce[i, at(ux, 2, uz)] = dot(lift_y, rows).astype(BF)
            rows = jnp.concatenate(
                [m.ce[i, at(2, 0, uz)], m.chy[i, uz], m.chc[i, uz]], axis=0
            )
            m.ce[i, at(2, 2, uz)] = dot(lift_xy, rows).astype(BF)
        for ux in range(3):
            for uy in range(3):
                m.ce[i, at(ux, uy, 2)] = dot(lift_z, m.ce[i, at(ux, uy, 0)]).astype(BF)

    terms = (((1, 0),), ((2, 0), (0, 1)))

    def transposed(i, emit, parities=range(8)):
        for p in parities:
            px, py, pz = p // 4, p // 2 % 2, p % 2
            total = None
            for kx, sx in terms[px]:
                for ky, sy in terms[py]:
                    for kz, sz in terms[pz]:
                        rows = jnp.concatenate(
                            [
                                m.ce[i, at(u // 4 + sx, u // 2 % 2 + sy, u % 2 + sz)]
                                for u in range(8)
                            ],
                            axis=0,
                        )
                        k = kx * 9 + ky * 3 + kz
                        if i == 0:
                            term = dot(rows, m.wup[:, col(k)])
                        else:
                            term = dot_nt(rows, m.wdp[col(k), :])
                        total = term if total is None else total + term
            for u in range(8):
                vx, vy, vz = 2 * (u // 4) + px, 2 * (u // 2 % 2) + py, 2 * (u % 2) + pz
                emit(vx, vy, vz, total[u * TB : (u + 1) * TB])

    def emit_result(vx, vy, vz, value):
        value = (m.eg[0, :, col(vx * 16 + vy * 4 + vz)].astype(F32) + value) * occ
        m.scr[pl.ds((vx * 4 + vy) * 256 + vz, TB, stride=4), :] = value

    def emit_grad(vx, vy, vz, value):
        cols = col(vx * 16 + vy * 4 + vz)
        m.fb[:, cols] = (m.eg[1, :, cols].astype(F32) + value).astype(BF)

    run_a()
    for copy in coarse_halo:
        copy.wait()
    extend(1)
    transposed(1, emit_grad)

    def gather(n, carry):
        cols = pl.ds(pl.multiple_of(n * 512, 512), 512)
        values = dot(from_slot, m.fb[:, cols])
        for b in range(4):
            for rank in range(2):
                rows = pl.ds(rank * VOX + n * 4 + b, NY_DEV, stride=2 * VOX)
                m.scr2[rows, :] = values[
                    rank * NY_DEV : (rank + 1) * NY_DEV, b * L : (b + 1) * L
                ]
        return carry

    def reply(d, carry):
        for rank in range(2):
            base = pl.multiple_of((2 * d + rank) * VOX, VOX)
            tail = m.scr2[pl.ds(base + ROWS, 16), :]
            for p in range(3):
                body = m.scr2[pl.ds(base + p * 16, 16), :]
                m.rep[d, pl.ds(rank * ROWS + p * 16, 16), :] = jnp.where(
                    lane < C, body, pltpu.roll(tail, C - 32 * p, 1)
                ).astype(BF)
        return carry

    def send_back(part):
        for e in FAR_FIRST[(0, 6, 14)[part] : (6, 14, NY_DEV - 1)[part]]:
            send(m.rep.at[e], m.ret.at[e], m.back_send.at[0], m.back_recv.at[0], offset(e, -1))

    lax.fori_loop(0, 16, gather, 0, unroll=8)
    run_b()
    lax.fori_loop(0, NY_DEV, reply, 0, unroll=8)
    send_back(0)
    m.ret[0] = m.rep[0]
    extend(0)
    run_c()
    send_back(1)
    transposed(0, emit_result, range(0, 6))
    run_d()
    send_back(2)
    transposed(0, emit_result, range(6, 8))
    run_e()

    def result_out(g, carry):
        vx, vy = g // 4, lax.rem(g, 4)
        for b in range(16):
            x, y = 4 * (b // 4) + vx, 4 * (b % 4) + vy
            rows = pl.ds(pl.multiple_of(g * 256 + b * 16, 16), 16)
            m.res_v[x * 16 + y] = m.scr[rows, :][:, :C].astype(BF)
        return carry

    lax.fori_loop(0, 16, result_out, 0)
    run_f()
    await_bytes(m.ret.at[pl.ds(1, NY_DEV - 1)], m.back_recv.at[0])
    for t in range(3):
        for d in range(4):
            i = lax.rem(pos[ORDERS[t][0]] + 4 - d, 4)
            await_bytes(strip(1 - core, t, i), m.hand_recv.at[t, d])
    await_bytes(m.tag_r.at[pl.ds(1, NY_DEV - 1)], m.tag_send.at[0])
    await_bytes(m.out_b.at[pl.ds(1, NY_DEV - 1)], m.a2a_send.at[0])
    await_bytes(m.rep.at[pl.ds(1, NY_DEV - 1)], m.back_send.at[0])
    for copy in core_copies + axis_copies:
        copy.wait_send()


def main_call(owner, slot, bricks, cot, wd, wu):
    vmem = pl.BlockSpec(memory_space=pltpu.VMEM)
    hbm = pl.BlockSpec(memory_space=pl.ANY)
    scratch = [pltpu.VMEM(shape, dtype) for shape, dtype in SCRATCH.values()]
    scratch += [pltpu.SemaphoreType.DMA(shape) for shape in SEMS.values()]
    scratch += [pltpu.SMEM((1, L), I32)]
    return pl.pallas_call(
        main_kernel,
        out_shape=(
            pltpu.VMEM((256, 16, C), BF),
            pltpu.VMEM((NY_DEV, PAIR, L), BF),
            pltpu.VMEM((2, C2, NP), BF),
            pltpu.VMEM((1, L), I32),
        ),
        in_specs=[vmem, vmem, hbm, hbm, hbm, hbm],
        out_specs=[vmem] * 4,
        scratch_shapes=scratch,
        compiler_params=pltpu.CompilerParams(
            collective_id=0, has_side_effects=True, vmem_limit_bytes=50 * 2**20
        ),
    )(owner, slot, bricks, cot, wd, wu)


def final_kernel(
    target, ret, grads, early, brick_grads, down, up, result, target_s, bg_v, down_v, up_v, sems
):
    pass_on = pltpu.make_async_copy(early, result, sems.at[0])
    pass_on.start()
    get_target = pltpu.make_async_copy(target, target_s, sems.at[8])
    get_target.start()
    lane = lax.broadcasted_iota(I32, (16, L), 1)
    ident = one_hot(jnp.equal(*iotas(C, L)))
    puts = []
    rs, cs = iotas(C, 3 * L)
    spread = one_hot(((cs & (L - 1)) >= C) & (rs == (cs >> 7) * 32 + (cs & (L - 1)) - C))
    rs, cs = iotas(3 * L, C)
    gather = one_hot(((rs & (L - 1)) >= C) & (cs == (rs >> 7) * 32 + (rs & (L - 1)) - C))
    for k in range(27):
        group, p = k // 4, k % 4
        if p < 3:
            cols = pl.ds((group * 3 + p) * L, L)
            up_v[k] = grads[0, :, cols][:, :C].astype(F32)
            down_v[k] = dot_nt(ident, grads[1, :, cols])
        else:
            cols = pl.ds(group * 3 * L, 3 * L)
            up_v[k] = dot(grads[0, :, cols], gather)
            down_v[k] = dot_nt(spread, grads[1, :, cols])
        if k % 9 == 8:
            part = pl.ds(k - 8, 9)
            puts.append(pltpu.make_async_copy(up_v.at[part], up.at[part], sems.at[2 + k // 9]))
            puts.append(pltpu.make_async_copy(down_v.at[part], down.at[part], sems.at[5 + k // 9]))
            puts[-2].start()
            puts[-1].start()

    get_target.wait()

    def take(j, carry):
        body = ret[target_s[0, j]]
        bg_v[j, pl.ds(0, ROWS), :] = body[:, :C]
        tail = [
            pltpu.roll(body[p * 16 : (p + 1) * 16].astype(F32), 32 * (p + 1), 1) for p in range(3)
        ]
        tail = jnp.where(lane < 32, tail[0], jnp.where(lane < 64, tail[1], tail[2]))
        bg_v[j, pl.ds(ROWS, 16), :] = tail[:, :C].astype(BF)
        return carry

    lax.fori_loop(0, ENTRIES, take, 0, unroll=8)
    puts.append(pltpu.make_async_copy(bg_v, brick_grads, sems.at[1]))
    puts[-1].start()
    pass_on.wait()
    for put in puts:
        put.wait()


def final_call(target, ret, grads, early):
    vmem = pl.BlockSpec(memory_space=pltpu.VMEM)
    hbm = pl.BlockSpec(memory_space=pl.ANY)
    return pl.pallas_call(
        final_kernel,
        out_shape=(
            jax.ShapeDtypeStruct((ENTRIES, VOX, C), BF),
            jax.ShapeDtypeStruct((27, C, C2), F32),
            jax.ShapeDtypeStruct((27, C2, C), F32),
            jax.ShapeDtypeStruct((256, 16, C), BF),
        ),
        in_specs=[vmem] * 4,
        out_specs=[hbm] * 4,
        scratch_shapes=[
            pltpu.SMEM((1, L), I32),
            pltpu.VMEM((ENTRIES, VOX, C), BF),
            pltpu.VMEM((27, C, C2), F32),
            pltpu.VMEM((27, C2, C), F32),
            pltpu.SemaphoreType.DMA((9,)),
        ],
        compiler_params=pltpu.CompilerParams(vmem_limit_bytes=20 * 2**20),
    )(target, ret, grads, early)


def on_device(bricks, brick_owner, brick_slot, down_weight, up_weight, cotangent):
    early, ret, grads, target = main_call(
        brick_owner.reshape(1, ENTRIES),
        brick_slot.reshape(1, ENTRIES),
        bricks.reshape(ENTRIES, VOX, C),
        cotangent.reshape(256, 16, C),
        down_weight,
        up_weight,
    )
    brick_grads, down, up, result = final_call(target, ret.reshape(TB, ROWS, L), grads, early)
    return (
        result.reshape(16, 16, 16, C),
        brick_grads.reshape(1, 1, ENTRIES, VOX, C),
        down,
        up,
    )


def solution(mesh):
    placed = (
        P("gx", "gy", None, None, None),
        P("gx", "gy", None),
        P("gx", "gy", None),
        P(),
        P(),
        P("gx", "gy", None, None),
    )
    return jax.shard_map(
        on_device,
        mesh=mesh,
        in_specs=placed,
        out_specs=(P("gx", "gy", None, None), P("gx", "gy", None, None, None), P(), P()),
        check_vma=False,
    )
```

```python
import jax
import jax.numpy as jnp
from jax import lax
from jax.experimental import pallas as pl
from jax.experimental.pallas import tpu as pltpu
from jax.sharding import PartitionSpec as P

C = 96
C2 = 192
L = 128
TB = 64
VOX = 64
ENTRIES = 56
NY_DEV = 32
NX_DEV = 4
NL = 28 * L
NC = 21 * L
NP = 24 * L
PART = NP // 4
ROWS = VOX * C // L
PAIR = 2 * ROWS

BF = jnp.bfloat16
F32 = jnp.float32
I32 = jnp.int32
MESH = pl.DeviceIdType.MESH
ORDERS = (("x", "y", "z"), ("y", "z", "x"), ("z", "x", "y"))
FAR_FIRST = sorted(
    range(1, NY_DEV), key=lambda e: -(min(e // 8, 4 - e // 8) + min(e // 2 % 4, 4 - e // 2 % 4))
)
NT = (((1,), (1,)), ((), ()))


def dot(a, b):
    return jnp.dot(a, b, preferred_element_type=F32)


def dot_nt(a, b):
    return lax.dot_general(a, b, NT, preferred_element_type=F32)


def iotas(rows, cols):
    return (
        lax.broadcasted_iota(I32, (rows, cols), 0),
        lax.broadcasted_iota(I32, (rows, cols), 1),
    )


def one_hot(hit):
    return jnp.where(hit, 1.0, 0.0).astype(BF)


def col(block, width=L, count=1):
    return pl.ds(block * width, count * width)


SCRATCH = dict(
    bricks_v=((ENTRIES, VOX, C), BF),
    cot_v=((256, 16, C), BF),
    wd_v=((27, C, C2), BF),
    wu_v=((27, C2, C), BF),
    out_b=((NY_DEV, PAIR, L), BF),
    recv_b=((NY_DEV, PAIR, L), BF),
    entry_v=((1, L), I32),
    tag_v=((1, L), I32),
    tag_r=((NY_DEV, 1, L), I32),
    scr=((TB * VOX, L), F32),
    scr2=((TB * VOX, L), F32),
    eg=((2, TB, VOX * L), BF),
    ex=((2, TB, 16 * L), BF),
    ey=((2, TB, 20 * L), BF),
    ez=((2, TB, 25 * L), BF),
    hx=((2, 16, 16 * L), BF),
    hy=((2, 16, 16 * L), BF),
    hc=((2, 16, 4 * L), BF),
    hy_send=((2, 16, 16 * L), BF),
    pm=((2, 8 * TB, NL), BF),
    wdp=((NL, C2), BF),
    wup=((C2, NL), BF),
    before=((8 * TB, C2), F32),
    back=((8 * TB, C2), F32),
    cc=((2, 8, TB, C2), BF),
    ce=((2, 27, TB, C2), BF),
    chx=((2, 4, 16, C2), BF),
    chy=((2, 4, 16, C2), BF),
    chc=((2, 2, 16, C2), BF),
    chy_send=((2, 4, 16, C2), BF),
    part=((C2, NC), F32),
    sb=((C2, NC), BF),
    r0=((C2, NC), BF),
    ab=((C2, NC), BF),
    ar=((3, 3, 16, NC), BF),
    mine=((3, 16, NP), F32),
    bb=((3, 16, NP), BF),
    br=((3, 3, 16, PART), BF),
    cr=((3, 4, 16, PART), BF),
    fb=((TB, VOX * L), BF),
    rep=((NY_DEV, PAIR, L), BF),
)
SEMS = dict(
    load=(4,),
    route=(1,),
    tag_send=(1,),
    tag_recv=(1,),
    a2a_send=(1,),
    a2a_recv=(NY_DEV,),
    halo_send=(9,),
    halo_recv=(9,),
    back_send=(1,),
    back_recv=(1,),
    core_send=(7,),
    core_recv=(7,),
    hand_send=(3, 4),
    hand_recv=(3, 4),
    ax_send=(5, 3, 3),
    ax_recv=(5, 3, 3),
)


def main_kernel(owner, slot, bricks, cot, wd, wu, result, ret_out, grads, target, *scratch):
    r = dict(zip(list(SCRATCH) + list(SEMS) + ["entry_s"], scratch))

    class R:
        pass

    m = R()
    m.__dict__.update(r)
    m.res_v, m.ret, m.total = result, ret_out, grads

    a = lax.axis_index("gx")
    s = lax.axis_index("gy")
    core = lax.rem(s, 2)
    zpos = lax.rem(s // 2, 4)
    ypos = s // 8
    pos = dict(x=a, y=ypos, z=zpos)

    def along(axis, i):
        if axis == "x":
            return (i, s)
        if axis == "y":
            return (a, (i * 4 + zpos) * 2 + core)
        return (a, (ypos * 4 + i) * 2 + core)

    def near(dx, dy):
        return (lax.rem(a + dx + NX_DEV, NX_DEV), lax.rem(s + dy + NY_DEV, NY_DEV))

    def offset(e, sign):
        y = lax.rem(ypos + sign * (e // 8) + 4, 4)
        z = lax.rem(zpos + sign * (e // 2 % 4) + 4, 4)
        return (a, (y * 4 + z) * 2 + lax.rem(core + e % 2, 2))

    sibling = (a, s + 1 - 2 * core)

    def send(src, dst, send_sem, recv_sem, device):
        copy = pltpu.make_async_remote_copy(
            src_ref=src,
            dst_ref=dst,
            send_sem=send_sem,
            recv_sem=recv_sem,
            device_id=device,
            device_id_type=MESH,
        )
        copy.start()
        return copy

    def await_bytes(ref, sem):
        pltpu.make_async_copy(ref, ref, sem).wait()

    loads = [
        pltpu.make_async_copy(src, dst, m.load.at[i])
        for i, (src, dst) in enumerate(
            ((bricks, m.bricks_v), (cot, m.cot_v), (wd, m.wd_v), (wu, m.wu_v))
        )
    ]
    for load in loads:
        load.start()

    barrier = pltpu.get_barrier_semaphore()

    def greet(d, carry):
        pl.semaphore_signal(barrier, inc=1, device_id=near(0, d), device_id_type=MESH)
        return carry

    lax.fori_loop(1, NY_DEV, greet, 0)
    for d in range(1, NX_DEV):
        pl.semaphore_signal(barrier, inc=1, device_id=near(d, 0), device_id_type=MESH)
    pl.semaphore_signal(barrier, inc=1, device_id=near(1, 1), device_id_type=MESH)
    pl.semaphore_signal(barrier, inc=1, device_id=near(-1, -1), device_id_type=MESH)

    rj, cj = iotas(ENTRIES, ENTRIES)
    own = owner[...]
    far = (
        (((own >> 3) - ypos) & 3) * 8 + ((((own >> 1) & 3) - zpos) & 3) * 2 + ((own - core) & 1)
    )
    far = jnp.broadcast_to(far, (ENTRIES, ENTRIES))

    def turn(rows):
        return jnp.sum(jnp.where(rj == cj, rows, 0), axis=1, keepdims=True)

    far_col = turn(far)
    rank = jnp.sum(jnp.where((far_col == far) & (rj < cj), 1, 0), axis=0, keepdims=True)
    goes = jnp.broadcast_to(2 * far[:1] + rank, (ENTRIES, ENTRIES))
    goes_col = turn(goes)
    slot_of = turn(jnp.broadcast_to(slot[...], (ENTRIES, ENTRIES)))
    rt, ct = iotas(ENTRIES, L)
    hit = goes_col == ct
    m.entry_v[...] = jnp.sum(jnp.where(hit, rt, 0), axis=0, keepdims=True)
    m.tag_v[...] = jnp.sum(jnp.where(hit, slot_of + 1, 0), axis=0, keepdims=True) - 1
    target[...] = jnp.zeros((1, L), I32)
    target[:, pl.ds(0, ENTRIES)] = goes[:1]
    route = pltpu.make_async_copy(m.entry_v, m.entry_s, m.route.at[0])
    route.start()
    route.wait()

    lane = lax.broadcasted_iota(I32, (16, L), 1)
    loads[0].wait()

    def pack(d, carry):
        for rank in range(2):
            brick = m.bricks_v[m.entry_s[0, 2 * d + rank]]
            m.out_b[d, pl.ds(rank * ROWS, ROWS), pl.ds(0, C)] = brick[:ROWS]
            for p in range(3):
                m.out_b[d, pl.ds(rank * ROWS + p * 16, 16), pl.ds(C, L - C)] = brick[
                    ROWS:, p * 32 : (p + 1) * 32
                ]
        return carry

    lax.fori_loop(0, NY_DEV, pack, 0, unroll=8)
    pl.semaphore_wait(barrier, NY_DEV - 1 + NX_DEV - 1 + 2)

    for e in FAR_FIRST:
        send(m.tag_v, m.tag_r.at[e], m.tag_send.at[0], m.tag_recv.at[0], offset(e, 1))
    for e in FAR_FIRST:
        send(m.out_b.at[e], m.recv_b.at[e], m.a2a_send.at[0], m.a2a_recv.at[e], offset(e, 1))
    m.tag_r[0] = m.tag_v[...]
    m.recv_b[0] = m.out_b[0]

    m.scr[...] = jnp.zeros((TB * VOX, L), F32)
    loads[1].wait()

    def cot_in(g, carry):
        vx, vy = g // 4, lax.rem(g, 4)
        for b in range(16):
            x, y = 4 * (b // 4) + vx, 4 * (b % 4) + vy
            rows = pl.ds(pl.multiple_of(g * 256 + b * 16, 16), 16)
            m.scr[rows, pl.ds(0, C)] = m.cot_v[x * 16 + y].astype(F32)
        return carry

    lax.fori_loop(0, 16, cot_in, 0)

    def cot_out(g, carry):
        for vz in range(4):
            rows = pl.ds(g * 256 + vz, TB, stride=4)
            cols = pl.ds(pl.multiple_of((g * 4 + vz) * L, L), L)
            m.eg[1, :, cols] = m.scr[rows, :].astype(BF)
        return carry

    lax.fori_loop(0, 16, cot_out, 0)

    loads[2].wait()
    loads[3].wait()
    m.wup[...] = jnp.zeros((C2, NL), BF)
    for k in range(27):
        m.wdp[pl.ds(k * L, C), :] = m.wd_v[k]
        m.wdp[pl.ds(k * L + C, L - C), :] = jnp.zeros((L - C, C2), BF)
        m.wup[:, pl.ds(k * L, C)] = m.wu_v[k]
    m.wdp[pl.ds(27 * L, L), :] = jnp.zeros((L, C2), BF)
    for i in range(2):
        m.pm[i, :, pl.ds(27 * L, L)] = jnp.zeros((8 * TB, L), BF)
    for t in range(3):
        m.mine[t, :, pl.ds(NC, NP - NC)] = jnp.zeros((16, NP - NC), F32)
        m.bb[t, :, pl.ds(NC, NP - NC)] = jnp.zeros((16, NP - NC), BF)

    rows_i, cols_i = iotas(TB, TB)
    await_bytes(m.tag_r.at[pl.ds(1, NY_DEV - 1)], m.tag_recv.at[0])
    rg, cg = iotas(NY_DEV, L)
    tags = m.tag_r[...].reshape(NY_DEV, L).astype(F32)
    slot_col = jnp.concatenate(
        [
            jnp.sum(jnp.where(cg == 2 * rg + rank, tags, 0.0), axis=1, keepdims=True)
            for rank in range(2)
        ],
        axis=0,
    )
    from_slot = one_hot(slot_col == cols_i.astype(F32))
    to_slot = dot_nt(one_hot(rows_i == cols_i), from_slot)
    occ = jnp.sum(to_slot, axis=1, keepdims=True)
    to_slot = to_slot.astype(BF)

    def mask_seed(n, carry):
        cols = pl.ds(pl.multiple_of(n * 1024, 1024), 1024)
        m.eg[1, :, cols] = (m.eg[1, :, cols].astype(F32) * occ).astype(BF)
        return carry

    lax.fori_loop(0, 8, mask_seed, 0)

    q, c = iotas(16, TB)
    pick_top = one_hot(c == (q >> 2) * 16 + 12 + (q & 3))
    pick_low = one_hot(c == (q >> 2) * 16 + (q & 3))

    def send_halo(i):
        for vx in range(4):
            m.hy_send[i, :, col(vx, 512)] = dot(
                pick_top, m.eg[i, :, pl.ds((vx * 16 + 12) * L, 512)]
            ).astype(BF)
        moves = (
            (m.eg.at[i, pl.ds(48, 16), pl.ds(48 * L, 16 * L)], m.hx.at[i], near(1, 0)),
            (m.hy_send.at[i], m.hy.at[i], near(0, 1)),
            (m.eg.at[i, pl.ds(48, 16), pl.ds(60 * L, 4 * L)], m.hc.at[i], near(1, 1)),
        )
        return [
            send(src, dst, m.halo_send.at[3 * i + n], m.halo_recv.at[3 * i + n], device)
            for n, (src, dst, device) in enumerate(moves)
        ]

    seed_halo = send_halo(1)

    def brick_in(d):
        for rank in range(2):
            body = m.recv_b[d, pl.ds(rank * ROWS, ROWS), :].astype(F32)
            base = (2 * d + rank) * VOX
            m.scr[pl.ds(base, ROWS), :] = body
            tail = [pltpu.roll(body[p * 16 : (p + 1) * 16], 32 * (p + 1), 1) for p in range(3)]
            m.scr[pl.ds(base + ROWS, 16), :] = jnp.where(
                lane < 32,
                tail[0],
                jnp.where(lane < 64, tail[1], jnp.where(lane < 96, tail[2], 0.0)),
            )

    brick_in(0)
    for e in FAR_FIRST:
        await_bytes(m.recv_b.at[e], m.a2a_recv.at[e])
        brick_in(e)

    def place_bricks(g):
        blocks = []
        for vz in range(4):
            v = g * 4 + vz
            ranks = [m.scr[pl.ds(rank * VOX + v, NY_DEV, stride=2 * VOX), :] for rank in range(2)]
            blocks.append(jnp.concatenate(ranks, axis=0).astype(BF))
        m.eg[0, :, col(g, 512)] = dot(to_slot, jnp.concatenate(blocks, axis=1)).astype(BF)

    rim = [g for g in range(16) if g // 4 == 3 or g % 4 == 3]
    for g in rim:
        place_bricks(g)
    brick_halo = send_halo(0)
    for g in range(16):
        if g not in rim:
            place_bricks(g)

    rw, cw = iotas(TB, 80)
    by = (rw >> 2) & 3
    shift_y = one_hot(
        ((cw < TB) & (by > 0) & (cw == rw - 4))
        | ((by == 0) & (s > 0) & (cw == TB + (rw >> 4) * 4 + (rw & 3)))
    )
    rw, cw = iotas(TB, 96)
    by = (rw >> 2) & 3
    bx = rw >> 4
    shift_xy = one_hot(
        ((cw < TB) & (by > 0) & (cw == rw - 4))
        | ((by == 0) & (s > 0) & (bx > 0) & (cw == TB + (bx - 1) * 4 + (rw & 3)))
        | ((by == 0) & (s > 0) & (bx == 0) & (a > 0) & (cw == 80 + 12 + (rw & 3)))
    )
    shift_z = one_hot(((rows_i & 3) > 0) & (cols_i == rows_i - 1))

    def rims(i):
        hx = m.hx[i]
        m.ex[i, pl.ds(0, 16), :] = jnp.where(a > 0, hx, jnp.zeros_like(hx))
        m.ex[i, pl.ds(16, 48), :] = m.eg[i, pl.ds(0, 48), pl.ds(48 * L, 16 * L)]
        rows = jnp.concatenate(
            [m.ex[i, :, pl.ds(12 * L, 512)], m.hy[i, :, pl.ds(3 * 512, 512)], m.hc[i]], axis=0
        )
        m.ey[i, :, pl.ds(0, 512)] = dot(shift_xy, rows).astype(BF)
        for vx in range(4):
            rows = jnp.concatenate(
                [m.eg[i, :, pl.ds((vx * 16 + 12) * L, 512)], m.hy[i, :, pl.ds(vx * 512, 512)]],
                axis=0,
            )
            m.ey[i, :, pl.ds((vx + 1) * 512, 512)] = dot(shift_y, rows).astype(BF)

    def patches(i, early):
        def block(vx, vy, vz):
            if vz < 0:
                return m.ez[i, :, col((vx + 1) * 5 + vy + 1)]
            if vy < 0:
                return m.ey[i, :, col((vx + 1) * 4 + vz)]
            if vx < 0:
                return m.ex[i, :, col(vy * 4 + vz)]
            return m.eg[i, :, col(vx * 16 + vy * 4 + vz)]

        def shifted(places):
            cols = jnp.concatenate([block(vx, vy, 3) for vx, vy in places], axis=1)
            values = dot(shift_z, cols).astype(BF)
            for n, (vx, vy) in enumerate(places):
                m.ez[i, :, col((vx + 1) * 5 + vy + 1)] = values[:, n * L : (n + 1) * L]

        if early:
            for vx in range(4):
                shifted([(vx, vy) for vy in range(4)])
        else:
            rims(i)
            shifted([(-1, vy) for vy in range(-1, 4)])
            shifted([(vx, -1) for vx in range(4)])
        for u in range(8):
            ux, uy, uz = u // 4, u // 2 % 2, u % 2
            for k in range(27):
                vx, vy, vz = 2 * ux + k // 9 - 1, 2 * uy + k // 3 % 3 - 1, 2 * uz + k % 3 - 1
                if (vx >= 0 and vy >= 0) == early:
                    m.pm[i, pl.ds(u * TB, TB), col(k)] = block(vx, vy, vz)

    def forward(first, count):
        return dot(m.pm[0, :, col(first, L, count)], m.wdp[col(first, L, count), :])

    patches(1, True)
    for copy in seed_halo:
        copy.wait()
    patches(1, False)
    m.back[...] = dot_nt(m.pm[1], m.wup[...])
    patches(0, True)
    m.before[...] = forward(12, 6) + forward(21, 7)
    for copy in brick_halo:
        copy.wait()
    patches(0, False)
    m.before[...] += forward(0, 12) + forward(18, 3)

    def gate(u, carry):
        rows = pl.ds(pl.multiple_of(u * TB, TB), TB)
        v = m.before[rows, :]
        g = jax.nn.sigmoid(v)
        m.cc[0, u] = (v * g * occ).astype(BF)
        m.cc[1, u] = (m.back[rows, :] * (g * (1.0 + v * (1.0 - g))) * occ).astype(BF)
        return carry

    lax.fori_loop(0, 8, gate, 0)

    for i in range(2):
        for u in range(4):
            m.chy_send[i, u] = dot(pick_low, m.cc[i, (u // 2) * 4 + u % 2]).astype(BF)
    coarse_halo = [
        send(
            m.cc.at[:, pl.ds(0, 4), pl.ds(0, 16)],
            m.chx,
            m.halo_send.at[6],
            m.halo_recv.at[6],
            near(-1, 0),
        ),
        send(m.chy_send, m.chy, m.halo_send.at[7], m.halo_recv.at[7], near(0, -1)),
        send(
            m.cc.at[:, pl.ds(0, 2), pl.ds(0, 16)],
            m.chc,
            m.halo_send.at[8],
            m.halo_recv.at[8],
            near(-1, -1),
        ),
    ]

    ident = one_hot(jnp.equal(*iotas(C2, C2)))

    wide = lax.broadcasted_iota(I32, (C2, L), 1)

    def tile_grad(i, out, after):
        turned = dot_nt(ident, m.cc[i].reshape(8 * TB, C2)).astype(BF)
        for g in range(7):
            values = dot(turned, m.pm[1 - i, :, pl.ds(g * 512, 512)])
            for p in range(3):
                block = values[:, p * L : (p + 1) * L]
                if g < 6:
                    spare = pltpu.roll(values[:, 3 * L :], C - 32 * p, 1)
                    block = jnp.where(wide < C, block, spare)
                out[:, col(g * 3 + p)] = block.astype(out.dtype)
            after(g)

    core_copies = []

    def to_sibling(g):
        cols = pl.ds(g * 3 * L, 3 * L)
        core_copies.append(
            send(
                m.sb.at[:, cols],
                m.r0.at[:, cols],
                m.core_send.at[g],
                m.core_recv.at[g],
                sibling,
            )
        )

    tile_grad(1 - core, m.sb, to_sibling)
    tile_grad(core, m.part, lambda g: None)

    axis_copies = []

    def to_axis(stage, t, axis, src, dst):
        copies = []
        for d in (2, 1, 3):
            i = lax.rem(pos[axis] + d, 4)
            copies.append(
                send(
                    src(i),
                    dst(d),
                    m.ax_send.at[stage, t, d - 1],
                    m.ax_recv.at[stage, t, d - 1],
                    along(axis, i),
                )
            )
        axis_copies.extend(copies)
        return copies

    def rows_of(t, i):
        return pl.ds(pl.multiple_of(t * 64 + i * 16, 16), 16)

    def cols_of(j):
        return pl.ds(pl.multiple_of(j * PART, L), PART)

    stage_a, stage_b, stage_c, stage_d, stage_e = [], [], [], [], []

    def run_a():
        for g in range(7):
            core_copies[g].wait_recv()
        for t in range(3):
            rows = pl.ds(t * 64, 64)
            m.part[rows, :] = m.part[rows, :] + m.r0[rows, :].astype(F32)
            m.ab[rows, :] = m.part[rows, :].astype(BF)
            stage_a.append(
                to_axis(
                    0,
                    t,
                    ORDERS[t][0],
                    lambda i: m.ab.at[rows_of(t, i)],
                    lambda d: m.ar.at[t, d - 1],
                )
            )

    def run_b():
        for t in range(3):
            for copy in stage_a[t]:
                copy.wait_recv()
            mine = m.part[rows_of(t, pos[ORDERS[t][0]]), :]
            for d in range(3):
                mine = mine + m.ar[t, d].astype(F32)
            m.mine[t, :, pl.ds(0, NC)] = mine
            m.bb[t, :, pl.ds(0, NC)] = mine.astype(BF)
            stage_b.append(
                to_axis(
                    1,
                    t,
                    ORDERS[t][1],
                    lambda j: m.bb.at[t, :, cols_of(j)],
                    lambda d: m.br.at[t, d - 1],
                )
            )

    def run_c():
        for t in range(3):
            first, second, third = ORDERS[t]
            for copy in stage_b[t]:
                copy.wait_recv()
            mine = m.mine[t, :, cols_of(pos[second])]
            for d in range(3):
                mine = mine + m.br[t, d].astype(F32)
            m.cr[t, pos[third]] = mine.astype(BF)
            stage_c.append(
                to_axis(
                    2,
                    t,
                    third,
                    lambda i: m.cr.at[t, pos[third]],
                    lambda d: m.cr.at[t, pos[third]],
                )
            )

    def run_d():
        for t in range(3):
            first, second, third = ORDERS[t]
            for d in range(1, 4):
                await_bytes(
                    m.cr.at[t, lax.rem(pos[third] + 4 - d, 4)], m.ax_recv.at[2, t, d - 1]
                )
            whole = m.cr[t, 0].astype(F32)
            for d in range(1, 4):
                whole = whole + m.cr[t, d].astype(F32)
            here = m.total.at[core, rows_of(t, pos[first]), cols_of(pos[second])]
            here[...] = whole.astype(BF)
            stage_d.append(to_axis(3, t, second, lambda j: here, lambda d: here))

    def strip(c, t, i):
        return m.total.at[c, rows_of(t, i), pl.ds(0, NC)]

    def hand_over(t, n, i):
        here = strip(core, t, i)
        core_copies.append(
            send(here, here, m.hand_send.at[t, n], m.hand_recv.at[t, n], sibling)
        )

    def run_e():
        for t in range(3):
            first, second, third = ORDERS[t]
            for d in range(1, 4):
                j = lax.rem(pos[second] + 4 - d, 4)
                await_bytes(
                    m.total.at[core, rows_of(t, pos[first]), cols_of(j)],
                    m.ax_recv.at[3, t, d - 1],
                )
            here = strip(core, t, pos[first])
            stage_e.append(to_axis(4, t, first, lambda j: here, lambda d: here))
            hand_over(t, 0, pos[first])

    def run_f():
        for d in (1, 3, 2):
            for t in range(3):
                i = lax.rem(pos[ORDERS[t][0]] + 4 - d, 4)
                await_bytes(strip(core, t, i), m.ax_recv.at[4, t, d - 1])
                hand_over(t, d, i)

    rw, cw = iotas(TB, 80)
    by = (rw >> 2) & 3
    lift_y = one_hot(
        ((cw < TB) & (by < 3) & (cw == rw + 4))
        | ((by == 3) & (s < NY_DEV - 1) & (cw == TB + (rw >> 4) * 4 + (rw & 3)))
    )
    rw, cw = iotas(TB, 96)
    by = (rw >> 2) & 3
    bx = rw >> 4
    lift_xy = one_hot(
        ((cw < TB) & (by < 3) & (cw == rw + 4))
        | ((by == 3) & (s < NY_DEV - 1) & (bx < 3) & (cw == TB + (bx + 1) * 4 + (rw & 3)))
        | (
            (by == 3)
            & (s < NY_DEV - 1)
            & (bx == 3)
            & (a < NX_DEV - 1)
            & (cw == 80 + (rw & 3))
        )
    )
    lift_z = one_hot(((rows_i & 3) < 3) & (cols_i == rows_i + 1))

    def at(ux, uy, uz):
        return ux * 9 + uy * 3 + uz

    def extend(i):
        for u in range(8):
            m.ce[i, at(u // 4, u // 2 % 2, u % 2)] = m.cc[i, u]
        for uy in range(2):
            for uz in range(2):
                h = m.chx[i, uy * 2 + uz]
                m.ce[i, at(2, uy, uz), pl.ds(0, 48), :] = m.cc[i, uy * 2 + uz, pl.ds(16, 48), :]
                m.ce[i, at(2, uy, uz), pl.ds(48, 16), :] = jnp.where(
                    a < NX_DEV - 1, h, jnp.zeros_like(h)
                )
        for uz in range(2):
            for ux in range(2):
                rows = jnp.concatenate([m.ce[i, at(ux, 0, uz)], m.chy[i, ux * 2 + uz]], axis=0)
                m.ce[i, at(ux, 2, uz)] = dot(lift_y, rows).astype(BF)
            rows = jnp.concatenate(
                [m.ce[i, at(2, 0, uz)], m.chy[i, uz], m.chc[i, uz]], axis=0
            )
            m.ce[i, at(2, 2, uz)] = dot(lift_xy, rows).astype(BF)
        for ux in range(3):
            for uy in range(3):
                m.ce[i, at(ux, uy, 2)] = dot(lift_z, m.ce[i, at(ux, uy, 0)]).astype(BF)

    terms = (((1, 0),), ((2, 0), (0, 1)))

    def transposed(i, emit, parities=range(8)):
        for p in parities:
            px, py, pz = p // 4, p // 2 % 2, p % 2
            total = None
            for kx, sx in terms[px]:
                for ky, sy in terms[py]:
                    for kz, sz in terms[pz]:
                        rows = jnp.concatenate(
                            [
                                m.ce[i, at(u // 4 + sx, u // 2 % 2 + sy, u % 2 + sz)]
                                for u in range(8)
                            ],
                            axis=0,
                        )
                        k = kx * 9 + ky * 3 + kz
                        if i == 0:
                            term = dot(rows, m.wup[:, col(k)])
                        else:
                            term = dot_nt(rows, m.wdp[col(k), :])
                        total = term if total is None else total + term
            for u in range(8):
                vx, vy, vz = 2 * (u // 4) + px, 2 * (u // 2 % 2) + py, 2 * (u % 2) + pz
                emit(vx, vy, vz, total[u * TB : (u + 1) * TB])

    def emit_result(vx, vy, vz, value):
        value = (m.eg[0, :, col(vx * 16 + vy * 4 + vz)].astype(F32) + value) * occ
        m.scr[pl.ds((vx * 4 + vy) * 256 + vz, TB, stride=4), :] = value

    def emit_grad(vx, vy, vz, value):
        cols = col(vx * 16 + vy * 4 + vz)
        m.fb[:, cols] = (m.eg[1, :, cols].astype(F32) + value).astype(BF)

    run_a()
    for copy in coarse_halo:
        copy.wait()
    extend(1)
    transposed(1, emit_grad)

    def gather(n, carry):
        cols = pl.ds(pl.multiple_of(n * 512, 512), 512)
        values = dot(from_slot, m.fb[:, cols])
        for b in range(4):
            for rank in range(2):
                rows = pl.ds(rank * VOX + n * 4 + b, NY_DEV, stride=2 * VOX)
                m.scr2[rows, :] = values[
                    rank * NY_DEV : (rank + 1) * NY_DEV, b * L : (b + 1) * L
                ]
        return carry

    def reply(d, carry):
        for rank in range(2):
            base = pl.multiple_of((2 * d + rank) * VOX, VOX)
            tail = m.scr2[pl.ds(base + ROWS, 16), :]
            for p in range(3):
                body = m.scr2[pl.ds(base + p * 16, 16), :]
                m.rep[d, pl.ds(rank * ROWS + p * 16, 16), :] = jnp.where(
                    lane < C, body, pltpu.roll(tail, C - 32 * p, 1)
                ).astype(BF)
        return carry

    def send_back(part):
        for e in FAR_FIRST[(0, 6, 12, 20)[part] : (6, 12, 20, 31)[part]]:
            send(m.rep.at[e], m.ret.at[e], m.back_send.at[0], m.back_recv.at[0], offset(e, -1))

    lax.fori_loop(0, 16, gather, 0, unroll=8)
    run_b()
    lax.fori_loop(0, NY_DEV, reply, 0, unroll=8)
    send_back(0)
    m.ret[0] = m.rep[0]
    extend(0)
    run_c()
    send_back(1)
    transposed(0, emit_result, range(0, 6))
    run_d()
    send_back(2)
    transposed(0, emit_result, range(6, 8))
    run_e()
    send_back(3)

    def result_out(g, carry):
        vx, vy = g // 4, lax.rem(g, 4)
        for b in range(16):
            x, y = 4 * (b // 4) + vx, 4 * (b % 4) + vy
            rows = pl.ds(pl.multiple_of(g * 256 + b * 16, 16), 16)
            m.res_v[x * 16 + y] = m.scr[rows, :][:, :C].astype(BF)
        return carry

    lax.fori_loop(0, 16, result_out, 0)
    run_f()
    await_bytes(m.ret.at[pl.ds(1, NY_DEV - 1)], m.back_recv.at[0])
    for t in range(3):
        for d in range(4):
            i = lax.rem(pos[ORDERS[t][0]] + 4 - d, 4)
            await_bytes(strip(1 - core, t, i), m.hand_recv.at[t, d])
    await_bytes(m.tag_r.at[pl.ds(1, NY_DEV - 1)], m.tag_send.at[0])
    await_bytes(m.out_b.at[pl.ds(1, NY_DEV - 1)], m.a2a_send.at[0])
    await_bytes(m.rep.at[pl.ds(1, NY_DEV - 1)], m.back_send.at[0])
    for copy in core_copies + axis_copies:
        copy.wait_send()


def main_call(owner, slot, bricks, cot, wd, wu):
    vmem = pl.BlockSpec(memory_space=pltpu.VMEM)
    hbm = pl.BlockSpec(memory_space=pl.ANY)
    scratch = [pltpu.VMEM(shape, dtype) for shape, dtype in SCRATCH.values()]
    scratch += [pltpu.SemaphoreType.DMA(shape) for shape in SEMS.values()]
    scratch += [pltpu.SMEM((1, L), I32)]
    return pl.pallas_call(
        main_kernel,
        out_shape=(
            pltpu.VMEM((256, 16, C), BF),
            pltpu.VMEM((NY_DEV, PAIR, L), BF),
            pltpu.VMEM((2, C2, NP), BF),
            pltpu.VMEM((1, L), I32),
        ),
        in_specs=[vmem, vmem, hbm, hbm, hbm, hbm],
        out_specs=[vmem] * 4,
        scratch_shapes=scratch,
        compiler_params=pltpu.CompilerParams(
            collective_id=0, has_side_effects=True, vmem_limit_bytes=50 * 2**20
        ),
    )(owner, slot, bricks, cot, wd, wu)


def final_kernel(
    target, ret, grads, early, brick_grads, down, up, result, target_s, bg_v, down_v, up_v, sems
):
    pass_on = pltpu.make_async_copy(early, result, sems.at[0])
    pass_on.start()
    get_target = pltpu.make_async_copy(target, target_s, sems.at[8])
    get_target.start()
    lane = lax.broadcasted_iota(I32, (16, L), 1)
    ident = one_hot(jnp.equal(*iotas(C, L)))
    puts = []
    rs, cs = iotas(C, 3 * L)
    spread = one_hot(((cs & (L - 1)) >= C) & (rs == (cs >> 7) * 32 + (cs & (L - 1)) - C))
    rs, cs = iotas(3 * L, C)
    gather = one_hot(((rs & (L - 1)) >= C) & (cs == (rs >> 7) * 32 + (rs & (L - 1)) - C))
    for k in range(27):
        group, p = k // 4, k % 4
        if p < 3:
            cols = pl.ds((group * 3 + p) * L, L)
            up_v[k] = grads[0, :, cols][:, :C].astype(F32)
            down_v[k] = dot_nt(ident, grads[1, :, cols])
        else:
            cols = pl.ds(group * 3 * L, 3 * L)
            up_v[k] = dot(grads[0, :, cols], gather)
            down_v[k] = dot_nt(spread, grads[1, :, cols])
        if k % 9 == 8:
            part = pl.ds(k - 8, 9)
            puts.append(pltpu.make_async_copy(up_v.at[part], up.at[part], sems.at[2 + k // 9]))
            puts.append(pltpu.make_async_copy(down_v.at[part], down.at[part], sems.at[5 + k // 9]))
            puts[-2].start()
            puts[-1].start()

    get_target.wait()

    def take(j, carry):
        body = ret[target_s[0, j]]
        bg_v[j, pl.ds(0, ROWS), :] = body[:, :C]
        tail = [
            pltpu.roll(body[p * 16 : (p + 1) * 16].astype(F32), 32 * (p + 1), 1) for p in range(3)
        ]
        tail = jnp.where(lane < 32, tail[0], jnp.where(lane < 64, tail[1], tail[2]))
        bg_v[j, pl.ds(ROWS, 16), :] = tail[:, :C].astype(BF)
        return carry

    lax.fori_loop(0, ENTRIES, take, 0, unroll=8)
    puts.append(pltpu.make_async_copy(bg_v, brick_grads, sems.at[1]))
    puts[-1].start()
    pass_on.wait()
    for put in puts:
        put.wait()


def final_call(target, ret, grads, early):
    vmem = pl.BlockSpec(memory_space=pltpu.VMEM)
    hbm = pl.BlockSpec(memory_space=pl.ANY)
    return pl.pallas_call(
        final_kernel,
        out_shape=(
            jax.ShapeDtypeStruct((ENTRIES, VOX, C), BF),
            jax.ShapeDtypeStruct((27, C, C2), F32),
            jax.ShapeDtypeStruct((27, C2, C), F32),
            jax.ShapeDtypeStruct((256, 16, C), BF),
        ),
        in_specs=[vmem] * 4,
        out_specs=[hbm] * 4,
        scratch_shapes=[
            pltpu.SMEM((1, L), I32),
            pltpu.VMEM((ENTRIES, VOX, C), BF),
            pltpu.VMEM((27, C, C2), F32),
            pltpu.VMEM((27, C2, C), F32),
            pltpu.SemaphoreType.DMA((9,)),
        ],
        compiler_params=pltpu.CompilerParams(vmem_limit_bytes=20 * 2**20),
    )(target, ret, grads, early)


def on_device(bricks, brick_owner, brick_slot, down_weight, up_weight, cotangent):
    early, ret, grads, target = main_call(
        brick_owner.reshape(1, ENTRIES),
        brick_slot.reshape(1, ENTRIES),
        bricks.reshape(ENTRIES, VOX, C),
        cotangent.reshape(256, 16, C),
        down_weight,
        up_weight,
    )
    brick_grads, down, up, result = final_call(target, ret.reshape(TB, ROWS, L), grads, early)
    return (
        result.reshape(16, 16, 16, C),
        brick_grads.reshape(1, 1, ENTRIES, VOX, C),
        down,
        up,
    )


def solution(mesh):
    placed = (
        P("gx", "gy", None, None, None),
        P("gx", "gy", None),
        P("gx", "gy", None),
        P(),
        P(),
        P("gx", "gy", None, None),
    )
    return jax.shard_map(
        on_device,
        mesh=mesh,
        in_specs=placed,
        out_specs=(P("gx", "gy", None, None), P("gx", "gy", None, None, None), P(), P()),
        check_vma=False,
    )
```
